32 devices in a mesh: dp: 8 (over z, y), fsdp: 2 (over core), seq: 2 (over x).
Axes of the slice: x: 2, y: 2, z: 4, core: 2. Of those that a mesh axis runs over, the one named last changes fastest.
Arguments:
- states: bfloat16 [16, 1024, 768], P(('dp', 'fsdp'), 'seq'), may hold values from -6 to 6
- deleted: int32 [16, 1024], P(('dp', 'fsdp'), 'seq'), may hold values 0 or 1
- crop_lengths: int32 [16, 8], P(('dp', 'fsdp')), may hold values from 0 to 768, as said below
- query_weight: float32 [768, 768], P(('dp', 'fsdp', 'seq')), may hold values from -0.21875 to 0.21875
- query_bias: float32 [768], P(('dp', 'fsdp', 'seq')), may hold values from -3 to 3
- key_weight: float32 [768, 768], P(('dp', 'fsdp', 'seq')), may hold values from -0.21875 to 0.21875
- value_weight: float32 [768, 768], P(('dp', 'fsdp', 'seq')), may hold values from -0.21875 to 0.21875
- value_bias: float32 [768], P(('dp', 'fsdp', 'seq')), may hold values from -0.3125 to 0.3125
- output_weight: float32 [768, 768], P(('dp', 'fsdp', 'seq')), may hold values from -1.75 to 1.75
- output_bias: float32 [768], P(('dp', 'fsdp', 'seq')), may hold values from -1.75 to 1.75
- attn_gain: float32 [768], P(('dp', 'fsdp', 'seq')), may hold values from 0.5 to 1.5
- attn_shift: float32 [768], P(('dp', 'fsdp', 'seq')), may hold values from -1.75 to 1.75
- inner_weight: float32 [768, 3072], P(('dp', 'fsdp', 'seq')), may hold values from -0.21875 to 0.21875
- inner_bias: float32 [3072], P(('dp', 'fsdp', 'seq')), may hold values from -1.75 to 1.75
- outer_weight: float32 [3072, 768], P(('dp', 'fsdp', 'seq')), may hold values from -0.15625 to 0.15625
- outer_bias: float32 [768], P(('dp', 'fsdp', 'seq')), may hold values from -1.75 to 1.75
- final_gain: float32 [768], P(('dp', 'fsdp', 'seq')), may hold values from 0.5 to 1.5
- final_shift: float32 [768], P(('dp', 'fsdp', 'seq')), may hold values from -1.75 to 1.75
- cotangent: bfloat16 [16, 1024, 768], P(('dp', 'fsdp'), 'seq'), may hold values from -6 to 6
- pool_cotangent: float32 [16, 8, 768], P(('dp', 'fsdp')), may hold values from -768 to 768
Outputs:
- output: bfloat16 [16, 1024, 768], P(('dp', 'fsdp'), 'seq')
- pooled: float32 [16, 8, 768], P(('dp', 'fsdp'))
- states_grad: float32 [16, 1024, 768], P(('dp', 'fsdp'), 'seq')
- grad_query_weight: float32 [768, 768], P(('dp', 'fsdp', 'seq'))
- grad_query_bias: float32 [768], P(('dp', 'fsdp', 'seq'))
- grad_key_weight: float32 [768, 768], P(('dp', 'fsdp', 'seq'))
- grad_value_weight: float32 [768, 768], P(('dp', 'fsdp', 'seq'))
- grad_value_bias: float32 [768], P(('dp', 'fsdp', 'seq'))
- grad_output_weight: float32 [768, 768], P(('dp', 'fsdp', 'seq'))
- grad_output_bias: float32 [768], P(('dp', 'fsdp', 'seq'))
- grad_attn_gain: float32 [768], P(('dp', 'fsdp', 'seq'))
- grad_attn_shift: float32 [768], P(('dp', 'fsdp', 'seq'))
- grad_inner_weight: float32 [768, 3072], P(('dp', 'fsdp', 'seq'))
- grad_inner_bias: float32 [3072], P(('dp', 'fsdp', 'seq'))
- grad_outer_weight: float32 [3072, 768], P(('dp', 'fsdp', 'seq'))
- grad_outer_bias: float32 [768], P(('dp', 'fsdp', 'seq'))
- grad_final_gain: float32 [768], P(('dp', 'fsdp', 'seq'))
- grad_final_shift: float32 [768], P(('dp', 'fsdp', 'seq'))
The draws below stay inside these ranges and needn't reach their ends.
Inputs may be any that keep to these rules, and one draw needn't show every extreme that they name: `crop_lengths`: in every row the crops lie back to back from the row's first token and leave one or more padding tokens at its end. The rows fall into groups of 8 consecutive rows (rows 8k to 8k + 7); in each group exactly one row holds a single crop that ends half of 512 tokens before the row's end, its other slots empty. In every other row each crop has at most 256 tokens, and each nonempty crop but the row's last has half of 256 tokens or more.
All inputs are finite; a program needn't handle non-finite values. No bound on the sum of `deleted` on one device may be relied on, other than what follows from the above.
Results may differ from the reference program's by a relative error of at most 0.014.
The reference program's roundings to bfloat16 on the way count: a program that leaves them out, or rounds other values in their place, can miss the bound.
Values may be sent and summed in bfloat16 or wider, within the bound.
No kernel may reach another device: no remote copies, remote signals or barrier semaphores. Data moves between devices by JAX's collectives and lax.ppermute only.
A program may use at most 128 MiB of HBM per device.

```python
import jax
import jax.numpy as jnp
from jax import lax

D = 768
HEADS = 12
HEAD = 64
FF = 3072
ROW = 1024
CROP = 256
SHARD = 512
ROWS = 16
CROPS = 8


def draw_crop_lengths(key, part):
    key = jax.random.fold_in(key, 17)
    first, second, third = jax.random.split(key, 3)
    raw = jax.random.randint(first, (ROWS, CROPS), CROP // 2, CROP + 1, dtype=jnp.int32)
    padding = jax.random.randint(second, (ROWS, 1), 1, SHARD // 2 + 1, dtype=jnp.int32)
    chosen = jax.random.randint(third, (ROWS // 8, 1), 0, 8, dtype=jnp.int32)
    single = (jnp.arange(8, dtype=jnp.int32)[None, :] == chosen).reshape(ROWS, 1)
    slots = jnp.arange(CROPS, dtype=jnp.int32)[None, :]
    raw = jnp.where(single, jnp.where(slots == 0, ROW, 0), raw).astype(jnp.int32)
    limit = jnp.where(single, ROW - SHARD // 2, ROW - padding).astype(jnp.int32)
    crop_ends = jnp.minimum(jnp.cumsum(raw, axis=1, dtype=jnp.int32), limit)
    begins = jnp.concatenate([jnp.zeros((ROWS, 1), jnp.int32), crop_ends[:, :-1]], axis=1)
    return (crop_ends - begins).astype(jnp.int32)


def touch_ends(values, stream_key, smallest, high):
    place = [jax.random.randint(jax.random.fold_in(stream_key, axis), (), 0, length) for axis, length in enumerate(values.shape)]
    main_axis = values.shape.index(max(values.shape))
    neighbour = place[:main_axis] + [(place[main_axis] + 1) % values.shape[main_axis]] + place[main_axis + 1:]
    return values.at[tuple(place)].set(smallest).at[tuple(neighbour)].set(high)


def shard_levels(own_key, extent, shards, least, largest):
    def one(axis_at, parts):
        draws = jax.random.uniform(jax.random.fold_in(jax.random.fold_in(own_key, 6), axis_at), (parts,), jnp.float32, least / len(shards), largest / len(shards))
        return jnp.repeat(jnp.exp(draws), extent[axis_at] // parts).reshape((-1,) + (1,) * (len(extent) - axis_at - 1))

    loudness = one(*shards[0])
    for cut in shards[1:]:
        loudness = loudness * one(*cut)
    return loudness


def bell_draw(own_key, shape, width, most, shards=(), kind=jnp.bfloat16):
    entries = width * jax.random.normal(own_key, shape, jnp.float32)
    if shards:
        entries = entries * shard_levels(own_key, shape, shards, -0.22, 0.18)
    return jnp.clip(entries, -most, most).astype(kind)


def setup_inputs(seed: int = 0) -> dict:
    streams_of = jax.random.split(jax.random.key(seed), 21)
    return {
        "states": bell_draw(streams_of[0], (ROWS, ROW, D), 1.0, 6.0, ((0, 16), (1, 2))),
        "deleted": touch_ends((jax.random.randint(streams_of[1], (ROWS, ROW), 0, 10) < 1).astype(jnp.int32), jax.random.fold_in(streams_of[1], 1), 0, 1),
        "crop_lengths": draw_crop_lengths(jax.random.fold_in(streams_of[20], 71), 0),
        "query_weight": bell_draw(streams_of[3], (D, D), D ** -0.5, 0.21875, ((0, 32),), jnp.float32),
        "query_bias": bell_draw(streams_of[4], (D,), 0.5, 3.0, ((0, 32),), jnp.float32),
        "key_weight": bell_draw(streams_of[5], (D, D), D ** -0.5, 0.21875, ((0, 32),), jnp.float32),
        "value_weight": bell_draw(streams_of[6], (D, D), D ** -0.5, 0.21875, ((0, 32),), jnp.float32),
        "value_bias": bell_draw(streams_of[7], (D,), 0.05, 0.3125, ((0, 32),), jnp.float32),
        "output_weight": bell_draw(streams_of[8], (D, D), (D // 64) ** -0.5, 1.75, ((0, 32),), jnp.float32),
        "output_bias": bell_draw(streams_of[9], (D,), 0.3, 1.75, ((0, 32),), jnp.float32),
        "attn_gain": jnp.clip(1.0 + 0.1 * jax.random.normal(streams_of[10], (D,), jnp.float32), 0.5, 1.5),
        "attn_shift": bell_draw(streams_of[11], (D,), 0.3, 1.75, ((0, 32),), jnp.float32),
        "inner_weight": bell_draw(streams_of[12], (D, FF), D ** -0.5, 0.21875, ((0, 32),), jnp.float32),
        "inner_bias": bell_draw(streams_of[13], (FF,), 0.3, 1.75, ((0, 32),), jnp.float32),
        "outer_weight": bell_draw(streams_of[14], (FF, D), (FF // 2) ** -0.5, 0.15625, ((0, 32),), jnp.float32),
        "outer_bias": bell_draw(streams_of[15], (D,), 0.3, 1.75, ((0, 32),), jnp.float32),
        "final_gain": jnp.clip(1.0 + 0.1 * jax.random.normal(streams_of[16], (D,), jnp.float32), 0.5, 1.5),
        "final_shift": bell_draw(streams_of[17], (D,), 0.3, 1.75, ((0, 32),), jnp.float32),
        "cotangent": bell_draw(streams_of[18], (ROWS, ROW, D), 1.0, 6.0, ((0, 16), (1, 2))),
        "pool_cotangent": bell_draw(streams_of[19], (ROWS, CROPS, D), (CROP // 2), 768.0, ((0, 16),), jnp.float32),
    }


highest = lax.Precision.HIGHEST

@jax.custom_vjp
def low(v):
    return lax.optimization_barrier(v.astype(jnp.bfloat16)).astype(jnp.float32)

@jax.custom_vjp
def low_back(v):
    return v

def low_keep(v):
    return (low(v), None)

def low_pass(kept, grad):
    return (grad,)

def back_keep(v):
    return (v, None)

def back_low(kept, grad):
    return (low(grad),)
low.defvjp(low_keep, low_pass)
low_back.defvjp(back_keep, back_low)

def matmul(left, right):
    return jnp.dot(left, right, precision=highest, preferred_element_type=jnp.float32)

def layer_norm(values, gain, shift):
    centered = values - lax.optimization_barrier(jnp.mean(values, axis=-1, keepdims=True))
    spread = lax.optimization_barrier(jnp.mean(centered * centered, axis=-1, keepdims=True))
    return centered * lax.rsqrt(spread + 1e-06) * gain + shift

def crop_layout(lengths, deleted, places):
    crop_ends = jnp.cumsum(lengths, axis=-1, dtype=jnp.int32)
    segment = lax.optimization_barrier(jnp.sum((places[..., :, None] >= crop_ends[..., None, :]).astype(jnp.int32), axis=-1, dtype=jnp.int32)).astype(jnp.int32)
    retained = (deleted == 0) & (segment < lengths.shape[-1])
    key_tag = jnp.where(retained, segment, -1).astype(jnp.int32)
    return (segment, retained, key_tag)

def one_row(params, row_states, lengths, deleted):
    w_query, b_query, w_key, w_value, b_value, w_out, b_out, g_attn, s_attn, w_inner, b_inner, w_outer, b_outer, g_final, s_final = [low(param) for param in params]
    places = jnp.arange(ROW, dtype=jnp.int32)
    segment, retained, key_tag = crop_layout(lengths, deleted, places)
    queries = low_back(low(matmul(row_states, w_query) + b_query)).reshape(ROW, HEADS, HEAD)
    keys = low_back(low(matmul(row_states, w_key))).reshape(ROW, HEADS, HEAD)
    values = low_back(low(matmul(row_states, w_value) + b_value)).reshape(ROW, HEADS, HEAD)
    block = min(512, ROW)

    def attend(inputs):
        query_block, query_tag, query_place = inputs
        scores = low_back(jnp.einsum('qhd,khd->hqk', query_block, keys, precision=highest)) * 0.125
        allowed = (key_tag[None, :] == query_tag[:, None]) | (places[None, :] == query_place[:, None])
        masked = jnp.where(allowed[None], scores, -1e+30)
        top = lax.optimization_barrier(jnp.max(masked, axis=-1, keepdims=True))
        raised = jnp.exp(masked - top)
        probs = low(raised / lax.optimization_barrier(jnp.sum(raised, axis=-1, keepdims=True)))
        return jnp.einsum('hqk,khd->qhd', probs, values, precision=highest)
    mixed = lax.map(jax.checkpoint(attend), (queries.reshape(ROW // block, block, HEADS, HEAD), segment.reshape(ROW // block, block), places.reshape(ROW // block, block)))
    attended = low_back(low(mixed.reshape(ROW, D)))
    branch = low_back(matmul(attended, w_out) + b_out)
    normed = layer_norm(row_states + branch, g_attn, s_attn)
    inner = low_back(matmul(low(normed), w_inner) + b_inner)
    active = low(jax.nn.gelu(inner, approximate=False))
    outer = low_back(matmul(active, w_outer) + b_outer)
    result = layer_norm(normed + outer, g_final, s_final)
    member = ((segment[:, None] == jnp.arange(CROPS, dtype=jnp.int32)[None, :]) & retained[:, None]).astype(jnp.float32)
    counts = lax.optimization_barrier(jnp.sum(member, axis=0))
    pooled = matmul(member.T, result) / jnp.maximum(counts, 1.0)[:, None]
    return (result, pooled)

def forward(params, states, crop_lengths, deleted):

    def advance(totals, inputs):
        return (totals, jax.checkpoint(one_row)(params, inputs[0], inputs[1], inputs[2]))
    return lax.scan(advance, jnp.float32(0.0), (states, crop_lengths, deleted))[1]

def reference(states, deleted, crop_lengths, query_weight, query_bias, key_weight, value_weight, value_bias, output_weight, output_bias, attn_gain, attn_shift, inner_weight, inner_bias, outer_weight, outer_bias, final_gain, final_shift, cotangent, pool_cotangent):
    params = (query_weight, query_bias, key_weight, value_weight, value_bias, output_weight, output_bias, attn_gain, attn_shift, inner_weight, inner_bias, outer_weight, outer_bias, final_gain, final_shift)
    outputs, pullback = jax.vjp(lambda weights, inputs: forward(weights, inputs, crop_lengths, deleted), params, states.astype(jnp.float32))
    param_grads, states_grad = pullback((cotangent.astype(jnp.float32), pool_cotangent))
    grad_query_weight, grad_query_bias, grad_key_weight, grad_value_weight, grad_value_bias, grad_output_weight, grad_output_bias, grad_attn_gain, grad_attn_shift, grad_inner_weight, grad_inner_bias, grad_outer_weight, grad_outer_bias, grad_final_gain, grad_final_shift = param_grads
    return (outputs[0].astype(jnp.bfloat16), outputs[1], states_grad, grad_query_weight, grad_query_bias, grad_key_weight, grad_value_weight, grad_value_bias, grad_output_weight, grad_output_bias, grad_attn_gain, grad_attn_shift, grad_inner_weight, grad_inner_bias, grad_outer_weight, grad_outer_bias, grad_final_gain, grad_final_shift)
```

```python
from functools import partial

import jax
import jax.numpy as jnp
from jax import lax
from jax.experimental import pallas as pl
from jax.experimental.pallas import tpu as pltpu
from jax.sharding import PartitionSpec as P

HEADS = 12
HEAD = 64


highest = lax.Precision.HIGHEST
DP, FSDP, SEQ = "dp", "fsdp", "seq"
EVERY = (DP, FSDP, SEQ)
BY_ROW, FLAT = P(EVERY, None), P(EVERY)
ROWS = (DP, FSDP)


def layer_norm(values, gain, shift):
    centered = values - jnp.mean(values, axis=-1, keepdims=True)
    spread = jnp.mean(centered * centered, axis=-1, keepdims=True)
    return centered * lax.rsqrt(spread + 1e-06) * gain + shift


def crop_layout(lengths, deleted, places):
    crop_ends = jnp.cumsum(lengths, axis=-1, dtype=jnp.int32)
    segment = jnp.sum(
        (places[..., :, None] >= crop_ends[..., None, :]).astype(jnp.int32),
        axis=-1,
        dtype=jnp.int32,
    )
    retained = (deleted == 0) & (segment < lengths.shape[-1])
    key_tag = jnp.where(retained, segment, -1)
    return (segment, retained, key_tag)


def product(left, right):
    return jnp.dot(left, right, preferred_element_type=jnp.float32)


def column_sum(values):
    return jnp.sum(values.astype(jnp.float32), axis=0)


def sweep(carry, pieces, inner):
    count = pieces[0].shape[1]
    width = 256

    def turn(index, totals):
        offset = index * width
        parts = tuple((lax.dynamic_slice_in_dim(piece, offset, width, 1) for piece in pieces))
        return inner(totals, parts, offset)

    return lax.fori_loop(0, count // width, turn, carry)


def scores_at(query_part, key_part):
    return (
        jnp.einsum("rqhd,rkhd->rhqk", query_part, key_part, preferred_element_type=jnp.float32)
        * 0.125
    )


def allowed_at(query_tag, query_place, tags, begin):
    key_place = begin + jnp.arange(tags.shape[1], dtype=jnp.int32)
    same = tags[:, None, :] == query_tag[:, :, None]
    itself = key_place[None, None, :] == query_place[None, :, None]
    return (same | itself)[:, None]


def probs_at(raw, allowed, log_part):
    return jnp.where(allowed, jnp.exp(raw - log_part[..., None]), 0.0)


def body(
    states,
    deleted,
    crop_lengths,
    query_weight,
    query_bias,
    key_weight,
    value_weight,
    value_bias,
    output_weight,
    output_bias,
    attn_gain,
    attn_shift,
    inner_weight,
    inner_bias,
    outer_weight,
    outer_bias,
    final_gain,
    final_shift,
    cotangent,
    pool_cotangent,
):
    rows, shard, width = states.shape
    lowered = [
        master.astype(jnp.bfloat16)
        for master in (
            query_weight,
            query_bias,
            key_weight,
            value_weight,
            value_bias,
            output_weight,
            output_bias,
            attn_gain,
            attn_shift,
            inner_weight,
            inner_bias,
            outer_weight,
            outer_bias,
            final_gain,
            final_shift,
        )
    ]
    (
        w_query,
        b_query,
        w_key,
        w_value,
        b_value,
        w_out,
        b_out,
        g_attn,
        s_attn,
        w_inner,
        b_inner,
        w_outer,
        b_outer,
        g_final,
        s_final,
    ) = (
        lax.all_gather(lowered[0], EVERY, axis=0, tiled=True),
        lax.all_gather(lowered[1], EVERY, axis=0, tiled=True),
        lax.all_gather(lowered[2], EVERY, axis=0, tiled=True),
        lax.all_gather(lowered[3], EVERY, axis=0, tiled=True),
        lax.all_gather(lowered[4], EVERY, axis=0, tiled=True),
        lax.all_gather(lowered[5], EVERY, axis=0, tiled=True),
        lax.all_gather(lowered[6], EVERY, axis=0, tiled=True),
        lax.all_gather(lowered[7], EVERY, axis=0, tiled=True),
        lax.all_gather(lowered[8], EVERY, axis=0, tiled=True),
        lax.all_gather(lowered[9], EVERY, axis=0, tiled=True),
        lax.all_gather(lowered[10], EVERY, axis=0, tiled=True),
        lax.all_gather(lowered[11], EVERY, axis=0, tiled=True),
        lax.all_gather(lowered[12], EVERY, axis=0, tiled=True),
        lax.all_gather(lowered[13], EVERY, axis=0, tiled=True),
        lax.all_gather(lowered[14], EVERY, axis=0, tiled=True),
    )
    own_start = lax.axis_index(SEQ) * shard
    places = own_start + jnp.arange(shard, dtype=jnp.int32)
    segment, retained, key_tag = crop_layout(crop_lengths, deleted, places)
    flat = states.reshape(rows * shard, width)
    split = (rows, shard, HEADS, HEAD)
    queries = (product(flat, w_query) + b_query).astype(jnp.bfloat16).reshape(split)
    keys = product(flat, w_key).astype(jnp.bfloat16).reshape(split)
    values = (product(flat, w_value) + b_value).astype(jnp.bfloat16).reshape(split)

    def scale_step(totals, parts, begin):
        top, total = totals
        key_part, tags = parts
        allowed = allowed_at(segment, places, tags, begin)
        masked = jnp.where(allowed, scores_at(queries, key_part), -1e30)
        new_top = jnp.maximum(top, jnp.max(masked, axis=-1))
        raised = jnp.where(allowed, jnp.exp(masked - new_top[..., None]), 0.0)
        return (new_top, total * jnp.exp(top - new_top) + jnp.sum(raised, axis=-1))

    stat_shape = (rows, HEADS, shard)
    scale_init = (jnp.full(stat_shape, -1e30, jnp.float32), jnp.zeros(stat_shape, jnp.float32))
    top, total = sweep(
        scale_init,
        (
            lax.all_gather(keys, SEQ, axis=1, tiled=True),
            lax.all_gather(key_tag, SEQ, axis=1, tiled=True),
        ),
        inner=scale_step,
    )
    log_total = top + jnp.log(total)

    def mix_step(totals, parts, begin):
        coarse, fine = totals
        key_part, value_part, tags = parts
        probs = probs_at(
            scores_at(queries, key_part), allowed_at(segment, places, tags, begin), log_total
        )
        probs_low = probs.astype(jnp.bfloat16)
        rest = (probs - probs_low.astype(jnp.float32)).astype(jnp.bfloat16)
        coarse = coarse + jnp.einsum(
            "rhqk,rkhd->rqhd", probs_low, value_part, preferred_element_type=jnp.float32
        )
        fine = fine + jnp.einsum(
            "rhqk,rkhd->rqhd", rest, value_part, preferred_element_type=jnp.float32
        )
        return (coarse, fine)

    empty = jnp.zeros(split, jnp.float32)
    coarse, fine = sweep(
        (empty, empty),
        (
            lax.all_gather(keys, SEQ, axis=1, tiled=True),
            lax.all_gather(values, SEQ, axis=1, tiled=True),
            lax.all_gather(key_tag, SEQ, axis=1, tiled=True),
        ),
        inner=mix_step,
    )
    attended = coarse.astype(jnp.bfloat16).reshape(rows * shard, width)
    branch = product(attended, w_out) + b_out
    residual = states.astype(jnp.float32).reshape(rows * shard, width) + branch
    normed, attn_back = jax.vjp(
        layer_norm, residual, g_attn.astype(jnp.float32), s_attn.astype(jnp.float32)
    )
    normed_low = normed.astype(jnp.bfloat16)
    inner = product(normed_low, w_inner) + b_inner
    active_full, gelu_back = jax.vjp(partial(jax.nn.gelu, approximate=False), inner)
    active = active_full.astype(jnp.bfloat16)
    outer = product(active, w_outer) + b_outer
    result, final_back = jax.vjp(
        layer_norm, normed + outer, g_final.astype(jnp.float32), s_final.astype(jnp.float32)
    )
    output = result.astype(jnp.bfloat16).reshape(rows, shard, width)
    crops = crop_lengths.shape[1]
    member = (
        (segment[..., None] == jnp.arange(crops, dtype=jnp.int32)) & retained[..., None]
    ).astype(jnp.float32)
    partial_sums = jnp.einsum(
        "rnc,rnd->rcd",
        member,
        result.reshape(rows, shard, width),
        precision=highest,
        preferred_element_type=jnp.float32,
    )
    sums, counts = lax.psum((partial_sums, jnp.sum(member, axis=1)), SEQ)
    divisor = jnp.maximum(counts, 1.0)[..., None]
    pooled = sums / divisor
    w_query, w_key, w_value, w_out, w_inner, w_outer = (
        lax.all_gather(lowered[0], EVERY, axis=0, tiled=True),
        lax.all_gather(lowered[2], EVERY, axis=0, tiled=True),
        lax.all_gather(lowered[3], EVERY, axis=0, tiled=True),
        lax.all_gather(lowered[5], EVERY, axis=0, tiled=True),
        lax.all_gather(lowered[9], EVERY, axis=0, tiled=True),
        lax.all_gather(lowered[11], EVERY, axis=0, tiled=True),
    )
    result_grad = cotangent.astype(jnp.float32) + jnp.einsum(
        "rnc,rcd->rnd",
        member,
        pool_cotangent / divisor,
        precision=highest,
        preferred_element_type=jnp.float32,
    )
    sum_grad, grad_final_gain, grad_final_shift = final_back(
        result_grad.reshape(rows * shard, width)
    )
    outer_grad = sum_grad.astype(jnp.bfloat16)
    grad_outer_bias = column_sum(outer_grad)
    grad_outer_weight = product(active.T, outer_grad)
    inner_grad = gelu_back(product(outer_grad, w_outer.T))[0].astype(jnp.bfloat16)
    grad_inner_bias = column_sum(inner_grad)
    grad_inner_weight = product(normed_low.T, inner_grad)
    normed_grad = sum_grad + product(inner_grad, w_inner.T)
    residual_grad, grad_attn_gain, grad_attn_shift = attn_back(normed_grad)
    branch_grad = residual_grad.astype(jnp.bfloat16)
    grad_output_bias = column_sum(branch_grad)
    grad_output_weight = product(attended.T, branch_grad)
    mixed_grad = product(branch_grad, w_out.T).astype(jnp.bfloat16).reshape(split)
    delta = jnp.sum(mixed_grad.astype(jnp.float32) * (coarse + fine), axis=-1)
    delta_local = jnp.transpose(delta, (0, 2, 1))
    all_log, all_delta = (
        lax.all_gather(jnp.transpose(log_total, (0, 2, 1)), SEQ, axis=1, tiled=True),
        lax.all_gather(delta, SEQ, axis=1, tiled=True),
    )

    def key_side(totals, parts, begin):
        key_grad, value_grad = totals
        query_part, grad_part, tags_part = parts
        count = tags_part.shape[1]
        log_part = jnp.transpose(lax.dynamic_slice_in_dim(all_log, begin, count, 1), (0, 2, 1))
        delta_part = jnp.transpose(lax.dynamic_slice_in_dim(all_delta, begin, count, 1), (0, 2, 1))
        query_place = begin + jnp.arange(count, dtype=jnp.int32)
        allowed = allowed_at(tags_part, query_place, key_tag, own_start)
        probs = probs_at(scores_at(query_part, keys), allowed, log_part)
        value_grad = value_grad + jnp.einsum(
            "rhqk,rqhd->rkhd",
            probs.astype(jnp.bfloat16),
            grad_part,
            preferred_element_type=jnp.float32,
        )
        prob_grad = jnp.einsum(
            "rqhd,rkhd->rhqk", grad_part, values, preferred_element_type=jnp.float32
        )
        score_grad = (probs * (prob_grad - delta_part[..., None]) * 0.125).astype(jnp.bfloat16)
        key_grad = key_grad + jnp.einsum(
            "rhqk,rqhd->rkhd", score_grad, query_part, preferred_element_type=jnp.float32
        )
        return (key_grad, value_grad)

    key_grad, value_grad = sweep(
        (empty, empty),
        (
            lax.all_gather(queries, SEQ, axis=1, tiled=True),
            lax.all_gather(mixed_grad, SEQ, axis=1, tiled=True),
            lax.all_gather(segment, SEQ, axis=1, tiled=True),
        ),
        inner=key_side,
    )

    def query_side(query_grad, parts, begin):
        key_part, value_part, tags = parts
        probs = probs_at(
            scores_at(queries, key_part), allowed_at(segment, places, tags, begin), log_total
        )
        prob_grad = jnp.einsum(
            "rqhd,rkhd->rhqk", mixed_grad, value_part, preferred_element_type=jnp.float32
        )
        score_grad = (probs * (prob_grad - delta_local[..., None]) * 0.125).astype(jnp.bfloat16)
        return query_grad + jnp.einsum(
            "rhqk,rkhd->rqhd", score_grad, key_part, preferred_element_type=jnp.float32
        )

    query_grad = sweep(
        empty,
        (
            lax.all_gather(keys, SEQ, axis=1, tiled=True),
            lax.all_gather(values, SEQ, axis=1, tiled=True),
            lax.all_gather(key_tag, SEQ, axis=1, tiled=True),
        ),
        inner=query_side,
    )
    query_low = query_grad.astype(jnp.bfloat16).reshape(rows * shard, width)
    key_low = key_grad.astype(jnp.bfloat16).reshape(rows * shard, width)
    value_low = value_grad.astype(jnp.bfloat16).reshape(rows * shard, width)
    grad_query_weight = product(flat.T, query_low)
    grad_query_bias = column_sum(query_low)
    grad_key_weight = product(flat.T, key_low)
    grad_value_weight = product(flat.T, value_low)
    grad_value_bias = column_sum(value_low)
    states_grad = (
        residual_grad
        + product(query_low, w_query.T)
        + product(key_low, w_key.T)
        + product(value_low, w_value.T)
    ).reshape(rows, shard, width)
    summed = (
        lax.psum_scatter(grad_query_weight, EVERY, scatter_dimension=0, tiled=True),
        lax.psum_scatter(grad_query_bias, EVERY, scatter_dimension=0, tiled=True),
        lax.psum_scatter(grad_key_weight, EVERY, scatter_dimension=0, tiled=True),
        lax.psum_scatter(grad_value_weight, EVERY, scatter_dimension=0, tiled=True),
        lax.psum_scatter(grad_value_bias, EVERY, scatter_dimension=0, tiled=True),
        lax.psum_scatter(
            grad_output_weight, EVERY, scatter_dimension=0, tiled=True
        ),
        lax.psum_scatter(grad_output_bias, EVERY, scatter_dimension=0, tiled=True),
        lax.psum_scatter(grad_attn_gain, EVERY, scatter_dimension=0, tiled=True),
        lax.psum_scatter(grad_attn_shift, EVERY, scatter_dimension=0, tiled=True),
        lax.psum_scatter(grad_inner_weight, EVERY, scatter_dimension=0, tiled=True),
        lax.psum_scatter(grad_inner_bias, EVERY, scatter_dimension=0, tiled=True),
        lax.psum_scatter(grad_outer_weight, EVERY, scatter_dimension=0, tiled=True),
        lax.psum_scatter(grad_outer_bias, EVERY, scatter_dimension=0, tiled=True),
        lax.psum_scatter(grad_final_gain, EVERY, scatter_dimension=0, tiled=True),
        lax.psum_scatter(grad_final_shift, EVERY, scatter_dimension=0, tiled=True),
    )
    return (output, pooled, states_grad) + tuple(summed)


BF = jnp.bfloat16
F32 = jnp.float32
MIB = 1 << 20


def dot(left, right, left_dim=1, right_dim=0):
    return lax.dot_general(
        left,
        right,
        (((left_dim,), (right_dim,)), ((), ())),
        preferred_element_type=F32,
    )


def exact_dot(left, right, left_dim=1, right_dim=0):
    return lax.dot_general(
        left,
        right,
        (((left_dim,), (right_dim,)), ((), ())),
        precision=highest,
        preferred_element_type=F32,
    )


def crop_ends_of(lens_ref):
    ends, total = [], jnp.int32(0)
    for slot in range(lens_ref.shape[0]):
        total = total + lens_ref[slot]
        ends.append(total)
    return ends


def segment_of(ends, places):
    segment = jnp.zeros(places.shape, jnp.int32)
    for end in ends:
        segment = segment + (places >= end).astype(jnp.int32)
    return segment


def window_start(ends, block):
    middle = ends[0] * 0
    for end in ends:
        middle = jnp.maximum(middle, jnp.where(end <= 2 * block, end, 0))
    return jnp.where(middle < block, 0, block)


def pack_kernel(place, wq, wk, wv, wo, w1, w2, v24, v96, send, keep, small, p1a, p1b, p2):
    x = place[3]
    device = place[4]
    half = wq.shape[1] // 2
    for pair in range(half // 128):
        for index, ref in enumerate((wq, wk, wv)):
            left = ref[:, pair * 128 : pair * 128 + 128].astype(BF)
            right = ref[:, half + pair * 128 : half + pair * 128 + 128].astype(BF)
            begin = (pair * 3 + index) * 128
            keep[:, begin : begin + 128] = jnp.where(x == 0, left, right)
            send[:, begin : begin + 128] = jnp.where(x == 0, right, left)
    width = wo.shape[1]
    split = p1a.shape[1] - width
    p1a[:, :width] = wo[...].astype(BF)
    p1a[:, width:] = w1[:, :split].astype(BF)
    p1b[...] = w1[:, split:].astype(BF)
    p2[...] = w2[...].astype(BF)
    part = v24.shape[1]
    row = lax.broadcasted_iota(jnp.int32, (part, width), 0)
    lane = lax.broadcasted_iota(jnp.int32, (part, width), 1)
    spread = (row + device * part == lane).astype(BF)
    first = dot(v24[...].astype(BF), spread)
    part = v96.shape[1]
    row = lax.broadcasted_iota(jnp.int32, (part, width), 0)
    lane = lax.broadcasted_iota(jnp.int32, (part, width), 1)
    rows = []
    for index in range(8):
        if index < v96.shape[1] * 32 // width:
            spread = (row + device * part == lane + index * width).astype(BF)
            rows.append(dot(v96[...].astype(BF), spread))
    tall = lax.broadcasted_iota(jnp.int32, (8, width), 0)
    second = jnp.zeros((8, width), F32)
    for index, value in enumerate(rows):
        second = jnp.where(tall == index, value[:1], second)
    small[...] = jnp.concatenate([first, second], axis=0).astype(BF)


def blocks_in(place, parts, store, sems, flips, first=0):
    copies = []
    for part, (ref, offset) in enumerate(zip(parts, flips, strict=True)):
        for slot in range(ref.shape[0]):
            spot = slot_place(place, offset, slot)
            copies.append(
                pltpu.make_async_copy(
                    ref.at[slot], store.at[spot], sems.at[first + part * ref.shape[0] + slot]
                )
            )
    return copies


def xor(value, bits):
    if bits & 1:
        value = value + 1 - 2 * lax.rem(value, 2)
    if bits & 2:
        value = lax.rem(value + 2, 4)
    return value


def slot_place(place, flip, slot):
    flip_y, flip_c, flip_x = flip
    z = xor(place[0], slot % 4)
    y = xor(place[1], flip_y ^ (slot // 4))
    c = xor(place[2], flip_c)
    spot = (z * 2 + y) * 2 + c
    if flip_x is None:
        return spot
    return spot * 2 + xor(place[3], flip_x)


PAIR_FLIPS = ((0, 0, None), (1, 0, None), (0, 1, None), (1, 1, None))
FULL_FLIPS = ((0, 0, 0), (0, 0, 1), (0, 1, 0), (0, 1, 1))


def tag_row(ends, x, own, other):
    half = own.shape[1]
    parts = []
    for index in range(2):
        deleted = jnp.where(x == index, own[...], other[...])
        places = index * half + lax.broadcasted_iota(jnp.int32, (1, half), 1)
        segment = segment_of(ends, places)
        parts.append(jnp.where((deleted == 0) & (segment < len(ends)), segment, -1))
    return parts


def attend_block(ends, tags, q_ref, k_ref, v_ref, index, block, special):
    wide = 3 * block
    lane_low = lax.broadcasted_iota(jnp.int32, (block, 128), 1) < 64
    key_low = lax.broadcasted_iota(jnp.int32, (wide, 128), 1) < 64
    start = jnp.where(index <= 1, 0, jnp.where(index == 2, special, block))
    start = pl.multiple_of(start, block)
    begin = pl.multiple_of(index * block, block)
    places = begin + lax.broadcasted_iota(jnp.int32, (block, 1), 0)
    key_places = start + lax.broadcasted_iota(jnp.int32, (1, wide), 1)
    allowed = (tags[0:1, pl.ds(start, wide)] == segment_of(ends, places)) | (key_places == places)
    bias = jnp.where(allowed, 0.0, -1e30)
    outs = []
    for pair in range(q_ref.shape[1] // 128):
        columns = slice(pair * 128, pair * 128 + 128)
        queries = q_ref[pl.ds(begin, block), columns] * jnp.asarray(0.125, BF)
        keys = k_ref[pl.ds(start, wide), columns]
        values = v_ref[pl.ds(start, wide), columns]
        total = jnp.zeros((block, 128), F32)
        for side in range(2):
            mine = lane_low if side == 0 else ~lane_low
            key_mine = key_low if side == 0 else ~key_low
            scores = dot(jnp.where(mine, queries, 0), keys, 1, 1) + bias
            top = jnp.max(scores, axis=1, keepdims=True)
            raised = jnp.exp(scores - top)
            scale = 1.0 / jnp.sum(raised, axis=1, keepdims=True)
            probs = (raised * scale).astype(BF)
            total = total + dot(probs, jnp.where(key_mine, values, 0))
        outs.append(total.astype(BF))
    return jnp.concatenate(outs, axis=1)


def attend_half(ends, tags, q_ref, k_ref, v_ref, side, out):
    block = out.shape[0] // 2
    special = window_start(ends, block)

    def turn(step, carry):
        spot = pl.multiple_of(step * block, block)
        out[pl.ds(spot, block), :] = attend_block(
            ends, tags, q_ref, k_ref, v_ref, side * 2 + step, block, special
        )
        return carry

    lax.fori_loop(0, 2, turn, 0)


def fill_tags(ends, x, del_own, del_other, tags):
    half = del_own.shape[1]
    for index, part in enumerate(tag_row(ends, x, del_own, del_other)):
        tags[0:1, index * half : (index + 1) * half] = part


def attend_kernel(
    place, lens, del_own, del_other, st_own, st_other, a0, a1, a2, a3,
    q_out, k_out, v_out, mixed, small_out,
    store, rows, tags, sems, row_sems,
):
    x = place[3]
    copies = blocks_in(place, (a0, a1, a2, a3), store, sems, PAIR_FLIPS)
    for copy in copies:
        copy.start()
    own_copy = pltpu.make_async_copy(st_own, rows.at[x], row_sems.at[0])
    other_copy = pltpu.make_async_copy(st_other, rows.at[1 - x], row_sems.at[1])
    own_copy.start()
    other_copy.start()
    ends = crop_ends_of(lens)
    half = del_own.shape[1]
    fill_tags(ends, x, del_own, del_other, tags)
    for copy in copies:
        copy.wait()
    own_copy.wait()
    other_copy.wait()

    depth = store.shape[2] // 3
    small_out[...] = jnp.sum(store[:, 48:, :768].astype(F32), axis=0)
    split = pl.multiple_of(x * depth, depth)
    bias_q = small_out[0:1, pl.ds(split, depth)]
    bias_v = small_out[1:2, pl.ds(split, depth)]
    weight = store[:, :48, :].reshape(768, 3 * depth)

    def project(index, carry):
        begin = pl.multiple_of(index * half, half)
        product_ = dot(rows[index], weight)
        for pair in range(depth // 128):
            columns = slice(pair * 128, pair * 128 + 128)
            at = pair * 384
            q_out[pl.ds(begin, half), columns] = (
                product_[:, at : at + 128] + bias_q[:, columns]
            ).astype(BF)
            k_out[pl.ds(begin, half), columns] = product_[:, at + 128 : at + 256].astype(BF)
            v_out[pl.ds(begin, half), columns] = (
                product_[:, at + 256 : at + 384] + bias_v[:, columns]
            ).astype(BF)
        return carry

    lax.fori_loop(0, 2, project, 0)
    attend_half(ends, tags, q_out, k_out, v_out, 1 - x, mixed)


def attend_own_kernel(place, lens, del_own, del_other, q_in, k_in, v_in, mixed, tags):
    x = place[3]
    ends = crop_ends_of(lens)
    fill_tags(ends, x, del_own, del_other, tags)
    attend_half(ends, tags, q_in, k_in, v_in, x, mixed)


def norm_parts(values):
    centered = values - jnp.mean(values, axis=-1, keepdims=True)
    spread = jnp.mean(centered * centered, axis=-1, keepdims=True)
    scale = lax.rsqrt(spread + 1e-06)
    return centered * scale, scale


def norm_back(grad, gain, unit, scale):
    lifted = grad * gain
    return scale * (
        lifted
        - jnp.mean(lifted, axis=-1, keepdims=True)
        - unit * jnp.mean(lifted * unit, axis=-1, keepdims=True)
    )


def gelu_parts(inner):
    phi = 0.5 * (1.0 + lax.erf(inner * 0.7071067811865476))
    density = jnp.exp(inner * inner * -0.5) * 0.3989422804014327
    return inner * phi, phi + inner * density


def feed_kernel(
    place, lens, del_own, del_other, states, mix_own, mix_other, small, cot, pool_cot,
    p0, p1, p2, p3, r0, r1, r2, r3, f0, f1, f2, f3,
    output, pooled, residual_out, mg_own, mg_other, small_out, active, inner_low, low, outer_low, branch_low,
    w1, w2, slope, unit_a, scale_a, outer, grad, sems1, sems2,
):
    x = place[3]
    width = states.shape[1]
    count = states.shape[0]
    hidden = 4 * width
    part = width
    flat = p0.shape[2]
    in1 = blocks_in(place, (p0, p1, p2, p3), w1.at[:, :, :flat], sems1, PAIR_FLIPS)
    in1 += blocks_in(place, (r0, r1, r2, r3), w1.at[:, :, flat:], sems1, PAIR_FLIPS, 16)
    in2 = blocks_in(place, (f0, f1, f2, f3), w2, sems2, FULL_FLIPS)
    for copy in in1 + in2:
        copy.start()
    ends = crop_ends_of(lens)
    tags = tag_row(ends, x, del_own, del_other)
    slots = lax.broadcasted_iota(jnp.int32, (len(ends), count), 0)
    members = [(tag == slots).astype(F32) for tag in tags]
    counts = sum(jnp.sum(member, axis=1, keepdims=True) for member in members)
    divisor = jnp.maximum(counts, 1.0)
    member = jnp.where(x == 0, members[0], members[1])
    for copy in in1:
        copy.wait()

    def out_weight(side):
        return w1[pl.ds(side * 8, 8), :, :width].reshape(width // 2, width)

    branch = dot(mix_own[...], out_weight(x)) + dot(mix_other[...], out_weight(1 - x))
    branch = branch + small[2:3, :]
    unit, scale = norm_parts(states[...].astype(F32) + branch)
    unit_a[...] = unit
    scale_a[...] = scale
    value = unit * small[3:4, :] + small[4:5, :]
    low[...] = value.astype(BF)
    outer[...] = value + small[5:6, :]
    for copy in in2:
        copy.wait()

    def ahead(index, carry):
        begin = pl.multiple_of(index * part, part)
        weight = w1[:, :, pl.ds(width + begin, part)].reshape(width, part)
        inner = dot(low[...], weight) + small[pl.ds(8 + index, 1), :]
        act, bend = gelu_parts(inner)
        act = act.astype(BF)
        active[index] = act
        slope[index] = bend
        outer[...] += dot(act, w2[pl.ds(index * 8, 8)].reshape(part, width))
        return carry

    lax.fori_loop(0, hidden // part, ahead, 0)

    unit, scale = norm_parts(outer[...])
    result = unit * small[6:7, :] + small[7:8, :]
    output[...] = result.astype(BF)
    pooled[...] = exact_dot(member, result) / divisor
    grad_in = cot[...].astype(F32) + exact_dot(member, pool_cot[...] / divisor, 0, 0)
    small_out[0:2, :] = jnp.zeros((2, width), F32)
    small_out[12:16, :] = jnp.zeros((4, width), F32)
    small_out[6:7, :] = jnp.sum(grad_in * unit, axis=0, keepdims=True)
    small_out[7:8, :] = jnp.sum(grad_in, axis=0, keepdims=True)
    total = norm_back(grad_in, small[6:7, :], unit, scale)
    grad[...] = total
    outer_low[...] = total.astype(BF)
    small_out[5:6, :] = jnp.sum(outer_low[...].astype(F32), axis=0, keepdims=True)

    def back(index, carry):
        begin = pl.multiple_of(index * part, part)
        weight = w2[pl.ds(index * 8, 8)].reshape(part, width)
        inner = (dot(outer_low[...], weight, 1, 1) * slope[index]).astype(BF)
        inner_low[index] = inner
        small_out[pl.ds(8 + index, 1), :] = jnp.sum(inner.astype(F32), axis=0, keepdims=True)
        weight = w1[:, :, pl.ds(width + begin, part)].reshape(width, part)
        grad[...] += dot(inner, weight, 1, 1)
        return carry

    lax.fori_loop(0, hidden // part, back, 0)

    total = grad[...]
    unit = unit_a[...]
    small_out[3:4, :] = jnp.sum(total * unit, axis=0, keepdims=True)
    small_out[4:5, :] = jnp.sum(total, axis=0, keepdims=True)
    residual = norm_back(total, small[3:4, :], unit, scale_a[...])
    residual_out[...] = residual
    branch_low[...] = residual.astype(BF)
    small_out[2:3, :] = jnp.sum(branch_low[...].astype(F32), axis=0, keepdims=True)
    mg_own[...] = dot(branch_low[...], out_weight(x), 1, 1).astype(BF)
    mg_other[...] = dot(branch_low[...], out_weight(1 - x), 1, 1).astype(BF)


def outer_sum_kernel(place, active, outer_low, ka, kb, sa, sb, store, sems):
    width = outer_low.shape[1]

    def turn(index, carry):
        product_ = dot(active[index], outer_low[...], 0, 0).astype(BF)
        store[pl.ds(index * 8, 8)] = product_.reshape(8, width // 8, width)
        return carry

    lax.fori_loop(0, active.shape[0], turn, 0)
    copies = blocks_out(place, (ka, kb, sa, sb), store, sems, FULL_FLIPS, 0)
    for copy in copies:
        copy.start()
    for copy in copies:
        copy.wait()


def inner_sum_kernel(
    place, low, inner_low, branch_low, mix_own, mix_other, ka, kb, sa, sb, store, sems
):
    x = place[3]
    width = low.shape[1]
    for side, mix in ((x, mix_own), (1 - x, mix_other)):
        product_ = dot(mix[...], branch_low[...], 0, 0).astype(BF)
        store[pl.ds(side * 8, 8), :, :width] = product_.reshape(8, width // 16, width)

    def turn(index, carry):
        begin = pl.multiple_of((1 + index) * width, width)
        product_ = dot(low[...], inner_low[index], 0, 0).astype(BF)
        store[:, :, pl.ds(begin, width)] = product_.reshape(16, width // 16, width)
        return carry

    lax.fori_loop(0, inner_low.shape[0], turn, 0)
    copies = blocks_out(place, (ka, kb, sa, sb), store, sems, PAIR_FLIPS, 0)
    for copy in copies:
        copy.start()
    for copy in copies:
        copy.wait()


def blocks_out(place, parts, store, sems, flips, first):
    copies = []
    for part, (ref, offset) in enumerate(zip(parts, flips, strict=True)):
        for slot in range(ref.shape[0]):
            spot = slot_place(place, offset, slot)
            copies.append(
                pltpu.make_async_copy(
                    store.at[spot], ref.at[slot], sems.at[first + part * ref.shape[0] + slot]
                )
            )
    return copies


def retreat_kernel(
    place, lens, del_own, del_other, q_in, k_in, v_in, mg_own, mg_other, low, tags, dk, dv
):
    x = place[3]
    ends = crop_ends_of(lens)
    half = del_own.shape[1]
    for index, part in enumerate(tag_row(ends, x, del_own, del_other)):
        tall = jnp.transpose(jnp.broadcast_to(part.astype(F32), (8, half)))
        tags[index * half : (index + 1) * half, :] = tall[:, :1]
    dk[...] = jnp.zeros_like(dk)
    dv[...] = jnp.zeros_like(dv)
    block = half // 2
    wide = 3 * block
    special = window_start(ends, block)
    lane_low = lax.broadcasted_iota(jnp.int32, (block, 128), 1) < 64
    key_low = lax.broadcasted_iota(jnp.int32, (wide, 128), 1) < 64

    def turn(index, carry):
        start = jnp.where(index <= 1, 0, jnp.where(index == 2, special, block))
        start = pl.multiple_of(start, block)
        begin = pl.multiple_of(index * block, block)
        spot = pl.multiple_of(lax.rem(index, 2) * block, block)
        places = begin + lax.broadcasted_iota(jnp.int32, (1, block), 1)
        key_places = start + lax.broadcasted_iota(jnp.int32, (wide, 1), 0)
        allowed = (tags[pl.ds(start, wide), :] == segment_of(ends, places).astype(F32)) | (
            key_places == places
        )
        bias = jnp.where(allowed, 0.0, -1e30)
        queries = q_in[pl.ds(begin, block), :]
        keys = k_in[pl.ds(start, wide), :]
        values = v_in[pl.ds(start, wide), :]
        near = lax.div(index, 2) == x
        grads = jnp.where(near, mg_own[pl.ds(spot, block), :], mg_other[pl.ds(spot, block), :])
        q_total = jnp.zeros((block, 128), F32)
        k_total = jnp.zeros((wide, 128), F32)
        v_total = jnp.zeros((wide, 128), F32)
        for side in range(2):
            mine = lane_low if side == 0 else ~lane_low
            key_mine = key_low if side == 0 else ~key_low
            q_mine = jnp.where(mine, queries, 0)
            g_mine = jnp.where(mine, grads, 0)
            scores = dot(keys, q_mine * jnp.asarray(0.125, BF), 1, 1) + bias
            top = jnp.max(scores, axis=0, keepdims=True)
            raised = jnp.exp(scores - top)
            probs = raised * (1.0 / jnp.sum(raised, axis=0, keepdims=True))
            prob_grad = dot(values, g_mine, 1, 1)
            delta = jnp.sum(probs * prob_grad, axis=0, keepdims=True)
            score_grad = (probs * (prob_grad - delta) * 0.125).astype(BF)
            v_total = v_total + dot(probs.astype(BF), g_mine)
            k_total = k_total + dot(score_grad, q_mine)
            q_total = q_total + dot(score_grad, jnp.where(key_mine, keys, 0), 0, 0)
        low[pl.ds(begin, block), :128] = q_total.astype(BF)
        dk[pl.ds(start, wide), :] += k_total
        dv[pl.ds(start, wide), :] += v_total
        return carry

    lax.fori_loop(0, 4, turn, 0)
    low[:, 128:256] = dk[...].astype(BF)
    low[:, 256:] = dv[...].astype(BF)


def project_sum_kernel(
    place, st_own, st_other, low0, low1, low2, ka, kb, sa, sb, rows, store, row_sems, sems
):
    x = place[3]
    row_copies = [
        pltpu.make_async_copy(st_own, rows.at[x], row_sems.at[0]),
        pltpu.make_async_copy(st_other, rows.at[1 - x], row_sems.at[1]),
    ]
    for copy in row_copies:
        copy.start()
    lows = (low0, low1, low2)
    wide = low0.shape[1]
    lane_rows = lax.broadcasted_iota(jnp.int32, (24, 128), 0)
    extra = jnp.zeros((24, 128), F32)
    for index, ref in enumerate(lows):
        sums = jnp.sum(ref[...].astype(F32), axis=0, keepdims=True)
        extra = jnp.where(lane_rows == index, sums[:, :128], extra)
        extra = jnp.where(lane_rows == 3 + index, sums[:, 256:], extra)
    extra = jnp.concatenate([extra, extra], axis=0).astype(BF)
    store[:, :, 3 * wide :] = jnp.broadcast_to(extra[None], (16, 48, 128))
    for copy in row_copies:
        copy.wait()
    tokens = rows[...].reshape(2 * st_own.shape[0], st_own.shape[1])
    for index, ref in enumerate(lows):
        columns = slice(index * wide, (index + 1) * wide)
        store[:, :, columns] = dot(tokens, ref[...], 0, 0).astype(BF).reshape(16, 48, wide)
    copies = blocks_out(place, (ka, kb, sa, sb), store, sems, PAIR_FLIPS, 0)
    for copy in copies:
        copy.start()
    for copy in copies:
        copy.wait()


def states_sum_kernel(
    place, low0, low1, low2, residual, a0, a1, a2, a3, states_out, states_send, store, sems
):
    x = place[3]
    copies = blocks_in(place, (a0, a1, a2, a3), store, sems, PAIR_FLIPS)
    for copy in copies:
        copy.start()
    for copy in copies:
        copy.wait()
    half = residual.shape[0]
    lows = (low0, low1, low2)
    wide = low0.shape[1]

    def share(side):
        begin = pl.multiple_of(side * half, half)
        total = jnp.zeros(residual.shape, F32)
        for index, ref in enumerate(lows):
            weight = store[:, :48, index * wide : (index + 1) * wide].reshape(768, wide)
            total = total + dot(ref[pl.ds(begin, half), :], weight, 1, 1)
        return total

    states_send[...] = share(1 - x).astype(BF)
    states_out[...] = residual[...] + share(x)


def swap(value, axis):
    return lax.ppermute(value, axis, [(0, 1), (1, 0)])


def hop(value, planes, bits):
    return lax.ppermute(value, DP, [(i, i ^ bits) for i in range(planes)])


def add(*terms):
    return sum((term.astype(F32) for term in terms[1:]), terms[0].astype(F32)).astype(BF)


def call(kernel, outs, inputs, specs, scratch, name, micros=0, grid=()):
    return pl.pallas_call(
        kernel,
        out_shape=[jax.ShapeDtypeStruct(shape, kind) for shape, kind, _ in outs],
        in_specs=[
            pl.BlockSpec(memory_space=SPACES[key]) if isinstance(key, str) else key
            for key in specs
        ],
        out_specs=[pl.BlockSpec(memory_space=SPACES[key]) for _, _, key in outs],
        scratch_shapes=scratch,
        grid=grid,
        compiler_params=pltpu.CompilerParams(vmem_limit_bytes=60 * MIB),
        cost_estimate=pl.CostEstimate(
            flops=int(micros * 1.1e9), bytes_accessed=int(micros * 3e6), transcendentals=0
        ),
        name=name,
    )(*inputs)


SPACES = {"s": pltpu.SMEM, "v": pltpu.VMEM, "a": pl.ANY}


def after(value, *others):
    return lax.optimization_barrier((value,) + others)[0]


def column(rows, index):
    return pl.BlockSpec((rows, 128), lambda step: (0, index))


def halves_body(
    states, deleted, crop_lengths,
    query_weight, query_bias, key_weight, value_weight, value_bias, output_weight, output_bias,
    attn_gain, attn_shift, inner_weight, inner_bias, outer_weight, outer_bias, final_gain,
    final_shift, cotangent, pool_cotangent,
):
    planes = 8
    count, width = states.shape[1:]
    half = width // 2
    hidden = inner_weight.shape[1]
    part = query_weight.shape[0]
    long = outer_weight.shape[0]
    crops = crop_lengths.shape[1]
    tall = 3 * half
    flat = (width + hidden) // 2
    dma = pltpu.SemaphoreType.DMA
    dp, c, x = lax.axis_index(DP), lax.axis_index(FSDP), lax.axis_index(SEQ)
    device = (dp * 2 + c) * 2 + x
    place = jnp.stack([dp // 2, dp % 2, c, x, device]).astype(jnp.int32)
    lens = crop_lengths[0]
    own = states[0]

    v24 = jnp.stack(
        [query_bias, value_bias, output_bias, attn_gain, attn_shift, outer_bias, final_gain, final_shift]
    )
    v96 = jnp.broadcast_to(inner_bias[None], (8, long))
    send, keep, small, p1a, p1b, p2 = call(
        pack_kernel,
        [
            ((part, tall), BF, "v"),
            ((part, tall), BF, "v"),
            ((16, width), BF, "v"),
            ((part, flat), BF, "v"),
            ((part, flat), BF, "v"),
            ((long, width), BF, "v"),
        ],
        (place, query_weight, key_weight, value_weight, output_weight, inner_weight, outer_weight, v24, v96),
        "svvvvvvvv",
        [],
        "pack",
        2,
    )

    def pair_up(mine, theirs):
        return jnp.where(
            x == 0,
            jnp.concatenate([mine, theirs], axis=0),
            jnp.concatenate([theirs, mine], axis=0),
        )

    def along_z(block):
        return jnp.stack(
            [block, hop(block, planes, 2), hop(block, planes, 4), hop(block, planes, 6)]
        )

    del_other = swap(deleted, SEQ)
    both = pair_up(keep, swap(send, SEQ))
    tail = jnp.pad(add(small, swap(small, SEQ)), ((0, 0), (0, tall - width)))
    both_a = jnp.concatenate([both, tail], axis=0)
    quad_2 = along_z(p2)
    quad_a = along_z(both_a)
    other = swap(after(own, both_a), SEQ)
    quad_ay = after(hop(quad_a, planes, 1), other)
    parts_a = (quad_a, quad_ay, swap(quad_a, FSDP), swap(quad_ay, FSDP))
    octet = jnp.concatenate([quad_2, hop(quad_2, planes, 1)], axis=0)
    from_x = after(swap(after(p1a, both_a), SEQ), quad_a, other, del_other)
    quad_1 = along_z(pair_up(p1a, from_x))
    from_x = after(swap(after(p1b, both_a), SEQ), quad_1)
    quad_b = along_z(pair_up(p1b, from_x))

    marks = (place, lens, deleted, del_other)
    queries, keys, values, mix_send, small = call(
        attend_kernel,
        [((2 * count, half), BF, "v")] * 3 + [((count, half), BF, "v"), ((16, width), F32, "v")],
        marks + (after(own, octet, quad_1), other) + parts_a,
        "ssvvaaaaaa",
        [
            pltpu.VMEM((16, 64, tall), BF),
            pltpu.VMEM((2, count, width), BF),
            pltpu.VMEM((1, 2 * count), jnp.int32),
            dma((16,)),
            dma((2,)),
        ],
        "attend",
        0,
    )
    mix_other = swap(mix_send, SEQ)
    quad_1y = after(hop(quad_1, planes, 1), mix_send)
    (mix_own,) = call(
        attend_own_kernel,
        [((count, half), BF, "v")],
        marks + (after(queries, quad_b), keys, values),
        "ssvvvvv",
        [pltpu.VMEM((1, 2 * count), jnp.int32)],
        "attend_own",
        0,
    )

    octet_x = after(swap(octet, SEQ), mix_own)
    quad_by = after(hop(quad_b, planes, 1), mix_own)
    parts_2 = (octet, octet_x, swap(octet, FSDP), swap(octet_x, FSDP))
    parts_1 = (quad_1, quad_1y, swap(quad_1, FSDP), swap(quad_1y, FSDP))
    parts_1 += (quad_b, quad_by, swap(quad_b, FSDP), swap(quad_by, FSDP))
    four = ((hidden // width, count, width), BF, "v")
    tokens = ((count, width), BF, "v")
    (
        output, pooled, residual, mg_own, mg_send, small_grad,
        active, inner_low, low, outer_low, branch_low,
    ) = call(
        feed_kernel,
        [
            tokens,
            ((crops, width), F32, "v"),
            ((count, width), F32, "v"),
            ((count, half), BF, "v"),
            ((count, half), BF, "v"),
            ((16, width), F32, "v"),
            four, four, tokens, tokens, tokens,
        ],
        marks
        + (own, mix_own, mix_other, small, cotangent[0], pool_cotangent[0])
        + parts_1
        + parts_2,
        "ssvvvvvvvv" + "a" * 12,
        [
            pltpu.VMEM((16, 2 * part, width + hidden), BF),
            pltpu.VMEM((32, long, width), BF),
            pltpu.VMEM((hidden // width, count, width), F32),
            pltpu.VMEM((count, width), F32),
            pltpu.VMEM((count, 1), F32),
            pltpu.VMEM((count, width), F32),
            pltpu.VMEM((count, width), F32),
            dma((32,)),
            dma((32,)),
        ],
        "feed",
        28,
    )
    mg_other = swap(mg_send, SEQ)

    blocks_2 = ((8, long, width), BF, "a")
    keep_2a, keep_2b, send_2a, send_2b = call(
        outer_sum_kernel,
        [blocks_2] * 4,
        (place, active, outer_low),
        "svv",
        [pltpu.VMEM((32, long, width), BF), dma((32,))],
        "outer_sum",
        0,
    )
    blocks_1 = ((4, 2 * part, width + hidden), BF, "a")
    keep_1a, keep_1b, send_1a, send_1b = call(
        inner_sum_kernel,
        [blocks_1] * 4,
        (place, after(low, keep_2a, mg_other), inner_low, branch_low, mix_own, mix_other),
        "svvvvv",
        [pltpu.VMEM((16, 2 * part, width + hidden), BF), dma((16,))],
        "inner_sum",
        0,
    )

    t1_2 = add(keep_2b, swap(send_2b, FSDP))
    t1_1 = add(keep_1b, swap(send_1b, FSDP))
    smalls = small_grad + swap(small_grad, FSDP)

    lows = []
    gates = [(t1_2, t1_1, smalls)]
    for pair in range(half // 128):
        queries = after(queries, *gates[pair])
        specs = [pl.BlockSpec(memory_space=pltpu.SMEM)] * 2
        specs += [pl.BlockSpec(memory_space=pltpu.VMEM)] * 2
        specs += [column(2 * count, pair)] * 3 + [column(count, pair)] * 2
        (result,) = call(
            retreat_kernel,
            [((2 * count, 3 * 128), BF, "v")],
            marks + (queries, keys, values, mg_own, mg_other),
            specs,
            [
                pltpu.VMEM((2 * count, 1), F32),
                pltpu.VMEM((2 * count, 128), F32),
                pltpu.VMEM((2 * count, 128), F32),
            ],
            "retreat",
            0,
            (1,),
        )
        lows.append(result)
        smalls = smalls + after(hop(smalls, planes, 1 << pair), result)
        gates.append((result, smalls))

    t0_2 = add(keep_2a, swap(send_2a, FSDP))
    t0_1 = add(keep_1a, swap(send_1a, FSDP))
    u_2 = add(t0_2, after(swap(t1_2, SEQ), lows[2]))
    u_1 = add(t0_1, after(hop(t1_1, planes, 1), lows[2]))
    lows = [after(value, u_2, u_1) for value in lows]
    wide = tall + 128
    keep_a, keep_b, send_a, send_b = call(
        project_sum_kernel,
        [((4, 2 * part, wide), BF, "a")] * 4,
        (place, own, other) + tuple(lows),
        "saavvv",
        [
            pltpu.VMEM((2, count, width), BF),
            pltpu.VMEM((16, 2 * part, wide), BF),
            dma((2,)),
            dma((16,)),
        ],
        "project_sum",
        0,
    )
    states_part, states_send = call(
        states_sum_kernel,
        [((count, width), F32, "v"), tokens],
        (place,) + tuple(after(value, keep_a) for value in lows) + (residual,) + parts_a,
        "svvvvaaaa",
        [pltpu.VMEM((16, 64, tall), BF), dma((16,))],
        "states_sum",
        0,
    )
    states_grad = states_part + swap(states_send, SEQ).astype(F32)

    def last_z(u):
        return add(u[0], hop(u[1], planes, 2), hop(u[2], planes, 4), hop(u[3], planes, 6))

    t1 = add(keep_b, swap(send_b, FSDP))
    t0 = add(keep_a, swap(send_a, FSDP))
    v = last_z(add(t0, hop(t1, planes, 1))).reshape(2, part, wide)
    mine = jnp.where(x == 0, v[0], v[1])
    theirs = swap(jnp.where(x == 0, v[1], v[0]), SEQ)
    left = jnp.where(x == 0, mine, theirs).astype(F32)
    right = jnp.where(x == 0, theirs, mine).astype(F32)

    def gathered(index):
        columns = [
            side[:, (pair * 3 + index) * 128 : (pair * 3 + index + 1) * 128]
            for side in (left, right)
            for pair in range(half // 128)
        ]
        return jnp.concatenate(columns, axis=1)

    grad_query_weight, grad_key_weight, grad_value_weight = (gathered(i) for i in range(3))
    bias_grads = jnp.stack([left[:6, tall:], right[:6, tall:]]).reshape(2, 2, half)
    bias_grads = jnp.transpose(bias_grads, (1, 0, 2)).reshape(2, width)

    u1_2, u0_2 = u_2[4:], u_2[:4]
    v = add(u0_2, hop(u1_2, planes, 1))
    grad_outer_weight = (
        v[0].astype(F32)
        + hop(v[1], planes, 2).astype(F32)
        + hop(v[2], planes, 4).astype(F32)
        + hop(v[3], planes, 6).astype(F32)
    )
    v = last_z(u_1).reshape(2, part, width + hidden)
    mine = jnp.where(x == 0, v[0], v[1])
    theirs = swap(jnp.where(x == 0, v[1], v[0]), SEQ)
    total = mine.astype(F32) + theirs.astype(F32)
    grad_output_weight, grad_inner_weight = total[:, :width], total[:, width:]

    smalls = smalls + swap(smalls, SEQ)
    vectors = lax.dynamic_slice(smalls[:8], (0, device * part), (8, part))
    bias_grads = lax.dynamic_slice(bias_grads, (0, device * part), (2, part))
    grad_inner_bias = lax.dynamic_slice(
        smalls[8:12].reshape(hidden), (device * long,), (long,)
    )
    pooled = pooled + swap(pooled, SEQ)
    return (
        output[None],
        pooled[None],
        states_grad[None],
        grad_query_weight,
        bias_grads[0],
        grad_key_weight,
        grad_value_weight,
        bias_grads[1],
        grad_output_weight,
        vectors[2],
        vectors[3],
        vectors[4],
        grad_inner_weight,
        grad_inner_bias,
        grad_outer_weight,
        vectors[5],
        vectors[6],
        vectors[7],
    )


def solution(mesh):
    in_specs = (
        P(ROWS, SEQ, None),
        P(ROWS, SEQ),
        P(ROWS, None),
        BY_ROW,
        FLAT,
        BY_ROW,
        BY_ROW,
        FLAT,
        BY_ROW,
        FLAT,
        FLAT,
        FLAT,
        BY_ROW,
        FLAT,
        BY_ROW,
        FLAT,
        FLAT,
        FLAT,
        P(ROWS, SEQ, None),
        P(ROWS, None, None),
    )
    out_specs = (
        P(ROWS, SEQ, None),
        P(ROWS, None, None),
        P(ROWS, SEQ, None),
        BY_ROW,
        FLAT,
        BY_ROW,
        BY_ROW,
        FLAT,
        BY_ROW,
        FLAT,
        FLAT,
        FLAT,
        BY_ROW,
        FLAT,
        BY_ROW,
        FLAT,
        FLAT,
        FLAT,
    )
    shape = mesh.shape
    halves = (shape[DP], shape[FSDP], shape[SEQ]) == (8, 2, 2)
    chosen = halves_body if halves else body
    return jax.shard_map(chosen, mesh=mesh, in_specs=in_specs, out_specs=out_specs, check_vma=False)
```

```python
from functools import partial

import jax
import jax.numpy as jnp
from jax import lax
from jax.experimental import pallas as pl
from jax.experimental.pallas import tpu as pltpu
from jax.sharding import PartitionSpec as P

HEADS = 12
HEAD = 64


highest = lax.Precision.HIGHEST
DP, FSDP, SEQ = "dp", "fsdp", "seq"
EVERY = (DP, FSDP, SEQ)
BY_ROW, FLAT = P(EVERY, None), P(EVERY)
ROWS = (DP, FSDP)


def layer_norm(values, gain, shift):
    centered = values - jnp.mean(values, axis=-1, keepdims=True)
    spread = jnp.mean(centered * centered, axis=-1, keepdims=True)
    return centered * lax.rsqrt(spread + 1e-06) * gain + shift


def crop_layout(lengths, deleted, places):
    crop_ends = jnp.cumsum(lengths, axis=-1, dtype=jnp.int32)
    segment = jnp.sum(
        (places[..., :, None] >= crop_ends[..., None, :]).astype(jnp.int32),
        axis=-1,
        dtype=jnp.int32,
    )
    retained = (deleted == 0) & (segment < lengths.shape[-1])
    key_tag = jnp.where(retained, segment, -1)
    return (segment, retained, key_tag)


def product(left, right):
    return jnp.dot(left, right, preferred_element_type=jnp.float32)


def column_sum(values):
    return jnp.sum(values.astype(jnp.float32), axis=0)


def sweep(carry, pieces, inner):
    count = pieces[0].shape[1]
    width = 256

    def turn(index, totals):
        offset = index * width
        parts = tuple((lax.dynamic_slice_in_dim(piece, offset, width, 1) for piece in pieces))
        return inner(totals, parts, offset)

    return lax.fori_loop(0, count // width, turn, carry)


def scores_at(query_part, key_part):
    return (
        jnp.einsum("rqhd,rkhd->rhqk", query_part, key_part, preferred_element_type=jnp.float32)
        * 0.125
    )


def allowed_at(query_tag, query_place, tags, begin):
    key_place = begin + jnp.arange(tags.shape[1], dtype=jnp.int32)
    same = tags[:, None, :] == query_tag[:, :, None]
    itself = key_place[None, None, :] == query_place[None, :, None]
    return (same | itself)[:, None]


def probs_at(raw, allowed, log_part):
    return jnp.where(allowed, jnp.exp(raw - log_part[..., None]), 0.0)


def body(
    states,
    deleted,
    crop_lengths,
    query_weight,
    query_bias,
    key_weight,
    value_weight,
    value_bias,
    output_weight,
    output_bias,
    attn_gain,
    attn_shift,
    inner_weight,
    inner_bias,
    outer_weight,
    outer_bias,
    final_gain,
    final_shift,
    cotangent,
    pool_cotangent,
):
    rows, shard, width = states.shape
    lowered = [
        master.astype(jnp.bfloat16)
        for master in (
            query_weight,
            query_bias,
            key_weight,
            value_weight,
            value_bias,
            output_weight,
            output_bias,
            attn_gain,
            attn_shift,
            inner_weight,
            inner_bias,
            outer_weight,
            outer_bias,
            final_gain,
            final_shift,
        )
    ]
    (
        w_query,
        b_query,
        w_key,
        w_value,
        b_value,
        w_out,
        b_out,
        g_attn,
        s_attn,
        w_inner,
        b_inner,
        w_outer,
        b_outer,
        g_final,
        s_final,
    ) = (
        lax.all_gather(lowered[0], EVERY, axis=0, tiled=True),
        lax.all_gather(lowered[1], EVERY, axis=0, tiled=True),
        lax.all_gather(lowered[2], EVERY, axis=0, tiled=True),
        lax.all_gather(lowered[3], EVERY, axis=0, tiled=True),
        lax.all_gather(lowered[4], EVERY, axis=0, tiled=True),
        lax.all_gather(lowered[5], EVERY, axis=0, tiled=True),
        lax.all_gather(lowered[6], EVERY, axis=0, tiled=True),
        lax.all_gather(lowered[7], EVERY, axis=0, tiled=True),
        lax.all_gather(lowered[8], EVERY, axis=0, tiled=True),
        lax.all_gather(lowered[9], EVERY, axis=0, tiled=True),
        lax.all_gather(lowered[10], EVERY, axis=0, tiled=True),
        lax.all_gather(lowered[11], EVERY, axis=0, tiled=True),
        lax.all_gather(lowered[12], EVERY, axis=0, tiled=True),
        lax.all_gather(lowered[13], EVERY, axis=0, tiled=True),
        lax.all_gather(lowered[14], EVERY, axis=0, tiled=True),
    )
    own_start = lax.axis_index(SEQ) * shard
    places = own_start + jnp.arange(shard, dtype=jnp.int32)
    segment, retained, key_tag = crop_layout(crop_lengths, deleted, places)
    flat = states.reshape(rows * shard, width)
    split = (rows, shard, HEADS, HEAD)
    queries = (product(flat, w_query) + b_query).astype(jnp.bfloat16).reshape(split)
    keys = product(flat, w_key).astype(jnp.bfloat16).reshape(split)
    values = (product(flat, w_value) + b_value).astype(jnp.bfloat16).reshape(split)

    def scale_step(totals, parts, begin):
        top, total = totals
        key_part, tags = parts
        allowed = allowed_at(segment, places, tags, begin)
        masked = jnp.where(allowed, scores_at(queries, key_part), -1e30)
        new_top = jnp.maximum(top, jnp.max(masked, axis=-1))
        raised = jnp.where(allowed, jnp.exp(masked - new_top[..., None]), 0.0)
        return (new_top, total * jnp.exp(top - new_top) + jnp.sum(raised, axis=-1))

    stat_shape = (rows, HEADS, shard)
    scale_init = (jnp.full(stat_shape, -1e30, jnp.float32), jnp.zeros(stat_shape, jnp.float32))
    top, total = sweep(
        scale_init,
        (
            lax.all_gather(keys, SEQ, axis=1, tiled=True),
            lax.all_gather(key_tag, SEQ, axis=1, tiled=True),
        ),
        inner=scale_step,
    )
    log_total = top + jnp.log(total)

    def mix_step(totals, parts, begin):
        coarse, fine = totals
        key_part, value_part, tags = parts
        probs = probs_at(
            scores_at(queries, key_part), allowed_at(segment, places, tags, begin), log_total
        )
        probs_low = probs.astype(jnp.bfloat16)
        rest = (probs - probs_low.astype(jnp.float32)).astype(jnp.bfloat16)
        coarse = coarse + jnp.einsum(
            "rhqk,rkhd->rqhd", probs_low, value_part, preferred_element_type=jnp.float32
        )
        fine = fine + jnp.einsum(
            "rhqk,rkhd->rqhd", rest, value_part, preferred_element_type=jnp.float32
        )
        return (coarse, fine)

    empty = jnp.zeros(split, jnp.float32)
    coarse, fine = sweep(
        (empty, empty),
        (
            lax.all_gather(keys, SEQ, axis=1, tiled=True),
            lax.all_gather(values, SEQ, axis=1, tiled=True),
            lax.all_gather(key_tag, SEQ, axis=1, tiled=True),
        ),
        inner=mix_step,
    )
    attended = coarse.astype(jnp.bfloat16).reshape(rows * shard, width)
    branch = product(attended, w_out) + b_out
    residual = states.astype(jnp.float32).reshape(rows * shard, width) + branch
    normed, attn_back = jax.vjp(
        layer_norm, residual, g_attn.astype(jnp.float32), s_attn.astype(jnp.float32)
    )
    normed_low = normed.astype(jnp.bfloat16)
    inner = product(normed_low, w_inner) + b_inner
    active_full, gelu_back = jax.vjp(partial(jax.nn.gelu, approximate=False), inner)
    active = active_full.astype(jnp.bfloat16)
    outer = product(active, w_outer) + b_outer
    result, final_back = jax.vjp(
        layer_norm, normed + outer, g_final.astype(jnp.float32), s_final.astype(jnp.float32)
    )
    output = result.astype(jnp.bfloat16).reshape(rows, shard, width)
    crops = crop_lengths.shape[1]
    member = (
        (segment[..., None] == jnp.arange(crops, dtype=jnp.int32)) & retained[..., None]
    ).astype(jnp.float32)
    partial_sums = jnp.einsum(
        "rnc,rnd->rcd",
        member,
        result.reshape(rows, shard, width),
        precision=highest,
        preferred_element_type=jnp.float32,
    )
    sums, counts = lax.psum((partial_sums, jnp.sum(member, axis=1)), SEQ)
    divisor = jnp.maximum(counts, 1.0)[..., None]
    pooled = sums / divisor
    w_query, w_key, w_value, w_out, w_inner, w_outer = (
        lax.all_gather(lowered[0], EVERY, axis=0, tiled=True),
        lax.all_gather(lowered[2], EVERY, axis=0, tiled=True),
        lax.all_gather(lowered[3], EVERY, axis=0, tiled=True),
        lax.all_gather(lowered[5], EVERY, axis=0, tiled=True),
        lax.all_gather(lowered[9], EVERY, axis=0, tiled=True),
        lax.all_gather(lowered[11], EVERY, axis=0, tiled=True),
    )
    result_grad = cotangent.astype(jnp.float32) + jnp.einsum(
        "rnc,rcd->rnd",
        member,
        pool_cotangent / divisor,
        precision=highest,
        preferred_element_type=jnp.float32,
    )
    sum_grad, grad_final_gain, grad_final_shift = final_back(
        result_grad.reshape(rows * shard, width)
    )
    outer_grad = sum_grad.astype(jnp.bfloat16)
    grad_outer_bias = column_sum(outer_grad)
    grad_outer_weight = product(active.T, outer_grad)
    inner_grad = gelu_back(product(outer_grad, w_outer.T))[0].astype(jnp.bfloat16)
    grad_inner_bias = column_sum(inner_grad)
    grad_inner_weight = product(normed_low.T, inner_grad)
    normed_grad = sum_grad + product(inner_grad, w_inner.T)
    residual_grad, grad_attn_gain, grad_attn_shift = attn_back(normed_grad)
    branch_grad = residual_grad.astype(jnp.bfloat16)
    grad_output_bias = column_sum(branch_grad)
    grad_output_weight = product(attended.T, branch_grad)
    mixed_grad = product(branch_grad, w_out.T).astype(jnp.bfloat16).reshape(split)
    delta = jnp.sum(mixed_grad.astype(jnp.float32) * (coarse + fine), axis=-1)
    delta_local = jnp.transpose(delta, (0, 2, 1))
    all_log, all_delta = (
        lax.all_gather(jnp.transpose(log_total, (0, 2, 1)), SEQ, axis=1, tiled=True),
        lax.all_gather(delta, SEQ, axis=1, tiled=True),
    )

    def key_side(totals, parts, begin):
        key_grad, value_grad = totals
        query_part, grad_part, tags_part = parts
        count = tags_part.shape[1]
        log_part = jnp.transpose(lax.dynamic_slice_in_dim(all_log, begin, count, 1), (0, 2, 1))
        delta_part = jnp.transpose(lax.dynamic_slice_in_dim(all_delta, begin, count, 1), (0, 2, 1))
        query_place = begin + jnp.arange(count, dtype=jnp.int32)
        allowed = allowed_at(tags_part, query_place, key_tag, own_start)
        probs = probs_at(scores_at(query_part, keys), allowed, log_part)
        value_grad = value_grad + jnp.einsum(
            "rhqk,rqhd->rkhd",
            probs.astype(jnp.bfloat16),
            grad_part,
            preferred_element_type=jnp.float32,
        )
        prob_grad = jnp.einsum(
            "rqhd,rkhd->rhqk", grad_part, values, preferred_element_type=jnp.float32
        )
        score_grad = (probs * (prob_grad - delta_part[..., None]) * 0.125).astype(jnp.bfloat16)
        key_grad = key_grad + jnp.einsum(
            "rhqk,rqhd->rkhd", score_grad, query_part, preferred_element_type=jnp.float32
        )
        return (key_grad, value_grad)

    key_grad, value_grad = sweep(
        (empty, empty),
        (
            lax.all_gather(queries, SEQ, axis=1, tiled=True),
            lax.all_gather(mixed_grad, SEQ, axis=1, tiled=True),
            lax.all_gather(segment, SEQ, axis=1, tiled=True),
        ),
        inner=key_side,
    )

    def query_side(query_grad, parts, begin):
        key_part, value_part, tags = parts
        probs = probs_at(
            scores_at(queries, key_part), allowed_at(segment, places, tags, begin), log_total
        )
        prob_grad = jnp.einsum(
            "rqhd,rkhd->rhqk", mixed_grad, value_part, preferred_element_type=jnp.float32
        )
        score_grad = (probs * (prob_grad - delta_local[..., None]) * 0.125).astype(jnp.bfloat16)
        return query_grad + jnp.einsum(
            "rhqk,rkhd->rqhd", score_grad, key_part, preferred_element_type=jnp.float32
        )

    query_grad = sweep(
        empty,
        (
            lax.all_gather(keys, SEQ, axis=1, tiled=True),
            lax.all_gather(values, SEQ, axis=1, tiled=True),
            lax.all_gather(key_tag, SEQ, axis=1, tiled=True),
        ),
        inner=query_side,
    )
    query_low = query_grad.astype(jnp.bfloat16).reshape(rows * shard, width)
    key_low = key_grad.astype(jnp.bfloat16).reshape(rows * shard, width)
    value_low = value_grad.astype(jnp.bfloat16).reshape(rows * shard, width)
    grad_query_weight = product(flat.T, query_low)
    grad_query_bias = column_sum(query_low)
    grad_key_weight = product(flat.T, key_low)
    grad_value_weight = product(flat.T, value_low)
    grad_value_bias = column_sum(value_low)
    states_grad = (
        residual_grad
        + product(query_low, w_query.T)
        + product(key_low, w_key.T)
        + product(value_low, w_value.T)
    ).reshape(rows, shard, width)
    summed = (
        lax.psum_scatter(grad_query_weight, EVERY, scatter_dimension=0, tiled=True),
        lax.psum_scatter(grad_query_bias, EVERY, scatter_dimension=0, tiled=True),
        lax.psum_scatter(grad_key_weight, EVERY, scatter_dimension=0, tiled=True),
        lax.psum_scatter(grad_value_weight, EVERY, scatter_dimension=0, tiled=True),
        lax.psum_scatter(grad_value_bias, EVERY, scatter_dimension=0, tiled=True),
        lax.psum_scatter(
            grad_output_weight, EVERY, scatter_dimension=0, tiled=True
        ),
        lax.psum_scatter(grad_output_bias, EVERY, scatter_dimension=0, tiled=True),
        lax.psum_scatter(grad_attn_gain, EVERY, scatter_dimension=0, tiled=True),
        lax.psum_scatter(grad_attn_shift, EVERY, scatter_dimension=0, tiled=True),
        lax.psum_scatter(grad_inner_weight, EVERY, scatter_dimension=0, tiled=True),
        lax.psum_scatter(grad_inner_bias, EVERY, scatter_dimension=0, tiled=True),
        lax.psum_scatter(grad_outer_weight, EVERY, scatter_dimension=0, tiled=True),
        lax.psum_scatter(grad_outer_bias, EVERY, scatter_dimension=0, tiled=True),
        lax.psum_scatter(grad_final_gain, EVERY, scatter_dimension=0, tiled=True),
        lax.psum_scatter(grad_final_shift, EVERY, scatter_dimension=0, tiled=True),
    )
    return (output, pooled, states_grad) + tuple(summed)


BF = jnp.bfloat16
F32 = jnp.float32
MIB = 1 << 20


def dot(left, right, left_dim=1, right_dim=0):
    return lax.dot_general(
        left,
        right,
        (((left_dim,), (right_dim,)), ((), ())),
        preferred_element_type=F32,
    )


def exact_dot(left, right, left_dim=1, right_dim=0):
    return lax.dot_general(
        left,
        right,
        (((left_dim,), (right_dim,)), ((), ())),
        precision=highest,
        preferred_element_type=F32,
    )


def crop_ends_of(lens_ref):
    ends, total = [], jnp.int32(0)
    for slot in range(lens_ref.shape[0]):
        total = total + lens_ref[slot]
        ends.append(total)
    return ends


def segment_of(ends, places):
    segment = jnp.zeros(places.shape, jnp.int32)
    for end in ends:
        segment = segment + (places >= end).astype(jnp.int32)
    return segment


def window_start(ends, block):
    middle = ends[0] * 0
    for end in ends:
        middle = jnp.maximum(middle, jnp.where(end <= 2 * block, end, 0))
    return jnp.where(middle < block, 0, block)


def pack_kernel(
    place, wq, wk, wv, wo, w1, w2, v0, v1, v2, v3, v4, v5, v6, v7, v96,
    send, keep, small, p1, p2,
):
    x = place[3]
    device = place[4]
    half = wq.shape[1] // 2
    for pair in range(half // 128):
        for index, ref in enumerate((wq, wk, wv)):
            left = ref[:, pair * 128 : pair * 128 + 128].astype(BF)
            right = ref[:, half + pair * 128 : half + pair * 128 + 128].astype(BF)
            begin = (pair * 3 + index) * 128
            keep[:, begin : begin + 128] = jnp.where(x == 0, left, right)
            send[:, begin : begin + 128] = jnp.where(x == 0, right, left)
    width = wo.shape[1]
    tall = keep.shape[1]
    for ref, begin in ((send, tall), (p1, 0)):
        ref[:, begin : begin + width] = wo[...].astype(BF)
        ref[:, begin + width :] = w1[...].astype(BF)
    p2[...] = w2[...].astype(BF)
    part = v0.shape[1]
    row = lax.broadcasted_iota(jnp.int32, (8, part), 0)
    stacked = jnp.zeros((8, part), F32)
    for index, ref in enumerate((v0, v1, v2, v3, v4, v5, v6, v7)):
        stacked = jnp.where(row == index, ref[...], stacked)
    row = lax.broadcasted_iota(jnp.int32, (part, width), 0)
    lane = lax.broadcasted_iota(jnp.int32, (part, width), 1)
    spread = (row + device * part == lane).astype(BF)
    first = dot(stacked.astype(BF), spread)
    part = v96.shape[1]
    row = lax.broadcasted_iota(jnp.int32, (part, width), 0)
    lane = lax.broadcasted_iota(jnp.int32, (part, width), 1)
    rows = []
    for index in range(8):
        if index < v96.shape[1] * 32 // width:
            spread = (row + device * part == lane + index * width).astype(BF)
            rows.append(dot(jnp.broadcast_to(v96[...], (8, part)).astype(BF), spread))
    tall = lax.broadcasted_iota(jnp.int32, (8, width), 0)
    second = jnp.zeros((8, width), F32)
    for index, value in enumerate(rows):
        second = jnp.where(tall == index, value[:1], second)
    small[...] = jnp.concatenate([first, second], axis=0).astype(BF)


def blocks_in(place, parts, store, sems, flips, first=0):
    copies = []
    for part, (ref, offset) in enumerate(zip(parts, flips, strict=True)):
        for slot in range(ref.shape[0]):
            spot = slot_place(place, offset, slot)
            copies.append(
                pltpu.make_async_copy(
                    ref.at[slot], store.at[spot], sems.at[first + part * ref.shape[0] + slot]
                )
            )
    return copies


def xor(value, bits):
    if bits & 1:
        value = value + 1 - 2 * lax.rem(value, 2)
    if bits & 2:
        value = lax.rem(value + 2, 4)
    return value


def slot_place(place, flip, slot):
    flip_y, flip_c, flip_x = flip
    z = xor(place[0], slot % 4)
    y = xor(place[1], flip_y ^ (slot // 4))
    c = xor(place[2], flip_c)
    spot = (z * 2 + y) * 2 + c
    if flip_x is None:
        return spot
    return spot * 2 + xor(place[3], flip_x)


PAIR_FLIPS = ((0, 0, None), (1, 0, None), (0, 1, None), (1, 1, None))
FULL_FLIPS = ((0, 0, 0), (0, 0, 1), (0, 1, 0), (0, 1, 1))


def tag_row(ends, x, own, other):
    half = own.shape[1]
    parts = []
    for index in range(2):
        deleted = jnp.where(x == index, own[...], other[...])
        places = index * half + lax.broadcasted_iota(jnp.int32, (1, half), 1)
        segment = segment_of(ends, places)
        parts.append(jnp.where((deleted == 0) & (segment < len(ends)), segment, -1))
    return parts


def attend_block(ends, tags, q_ref, k_ref, v_ref, index, block, special):
    wide = 3 * block
    lane_low = lax.broadcasted_iota(jnp.int32, (block, 128), 1) < 64
    key_low = lax.broadcasted_iota(jnp.int32, (wide, 128), 1) < 64
    start = jnp.where(index <= 1, 0, jnp.where(index == 2, special, block))
    start = pl.multiple_of(start, block)
    begin = pl.multiple_of(index * block, block)
    places = begin + lax.broadcasted_iota(jnp.int32, (block, 1), 0)
    key_places = start + lax.broadcasted_iota(jnp.int32, (1, wide), 1)
    allowed = (tags[0:1, pl.ds(start, wide)] == segment_of(ends, places)) | (key_places == places)
    bias = jnp.where(allowed, 0.0, -1e30)
    outs = []
    lanes = lax.broadcasted_iota(jnp.int32, (block, 128), 1)
    logs = jnp.zeros((block, 128), F32)
    for pair in range(q_ref.shape[1] // 128):
        columns = slice(pair * 128, pair * 128 + 128)
        queries = q_ref[pl.ds(begin, block), columns] * jnp.asarray(0.125, BF)
        keys = k_ref[pl.ds(start, wide), columns]
        values = v_ref[pl.ds(start, wide), columns]
        total = jnp.zeros((block, 128), F32)
        for side in range(2):
            mine = lane_low if side == 0 else ~lane_low
            key_mine = key_low if side == 0 else ~key_low
            scores = dot(jnp.where(mine, queries, 0), keys, 1, 1) + bias
            top = jnp.max(scores, axis=1, keepdims=True)
            raised = jnp.exp(scores - top)
            amount = jnp.sum(raised, axis=1, keepdims=True)
            probs = (raised * (1.0 / amount)).astype(BF)
            total = total + dot(probs, jnp.where(key_mine, values, 0))
            logs = jnp.where(lanes == pair * 2 + side, top + jnp.log(amount), logs)
        outs.append(total.astype(BF))
    return jnp.concatenate(outs, axis=1), jnp.transpose(logs)[:8]


def attend_half(ends, tags, q_ref, k_ref, v_ref, side, out, logs):
    block = out.shape[0] // 2
    special = window_start(ends, block)

    def turn(step, carry):
        spot = pl.multiple_of(step * block, block)
        mixed, rows = attend_block(
            ends, tags, q_ref, k_ref, v_ref, side * 2 + step, block, special
        )
        out[pl.ds(spot, block), :] = mixed
        logs[:, pl.ds(spot, block)] = rows
        return carry

    lax.fori_loop(0, 2, turn, 0)


def fill_tags(ends, x, del_own, del_other, tags):
    half = del_own.shape[1]
    for index, part in enumerate(tag_row(ends, x, del_own, del_other)):
        tags[0:1, index * half : (index + 1) * half] = part


def attend_kernel(
    place, lens, del_own, del_other, st_own, st_other, a0, a1, a2, a3,
    q_out, k_out, v_out, mixed, logs, small_out,
    store, rows, tags, sems, row_sems,
):
    x = place[3]
    copies = blocks_in(place, (a0, a1, a2, a3), store, sems, PAIR_FLIPS)
    for copy in copies:
        copy.start()
    own_copy = pltpu.make_async_copy(st_own, rows.at[x], row_sems.at[0])
    other_copy = pltpu.make_async_copy(st_other, rows.at[1 - x], row_sems.at[1])
    own_copy.start()
    other_copy.start()
    ends = crop_ends_of(lens)
    half = del_own.shape[1]
    fill_tags(ends, x, del_own, del_other, tags)
    for copy in copies:
        copy.wait()
    own_copy.wait()
    other_copy.wait()

    depth = store.shape[2] // 3
    small_out[...] = jnp.sum(store[:, 48:, :768].astype(F32), axis=0)
    split = pl.multiple_of(x * depth, depth)
    bias_q = small_out[0:1, pl.ds(split, depth)]
    bias_v = small_out[1:2, pl.ds(split, depth)]
    weight = store[:, :48, :].reshape(768, 3 * depth)

    def project(index, carry):
        begin = pl.multiple_of(index * half, half)
        product_ = dot(rows[index], weight)
        for pair in range(depth // 128):
            columns = slice(pair * 128, pair * 128 + 128)
            at = pair * 384
            q_out[pl.ds(begin, half), columns] = (
                product_[:, at : at + 128] + bias_q[:, columns]
            ).astype(BF)
            k_out[pl.ds(begin, half), columns] = product_[:, at + 128 : at + 256].astype(BF)
            v_out[pl.ds(begin, half), columns] = (
                product_[:, at + 256 : at + 384] + bias_v[:, columns]
            ).astype(BF)
        return carry

    lax.fori_loop(0, 2, project, 0)
    attend_half(ends, tags, q_out, k_out, v_out, 1 - x, mixed, logs)


def attend_own_kernel(place, lens, del_own, del_other, q_in, k_in, v_in, mixed, logs, tags):
    x = place[3]
    ends = crop_ends_of(lens)
    fill_tags(ends, x, del_own, del_other, tags)
    attend_half(ends, tags, q_in, k_in, v_in, x, mixed, logs)


def norm_parts(values):
    centered = values - jnp.mean(values, axis=-1, keepdims=True)
    spread = jnp.mean(centered * centered, axis=-1, keepdims=True)
    scale = lax.rsqrt(spread + 1e-06)
    return centered * scale, scale


def norm_back(grad, gain, unit, scale):
    lifted = grad * gain
    return scale * (
        lifted
        - jnp.mean(lifted, axis=-1, keepdims=True)
        - unit * jnp.mean(lifted * unit, axis=-1, keepdims=True)
    )


def gelu_parts(inner):
    phi = 0.5 * (1.0 + lax.erf(inner * 0.7071067811865476))
    density = jnp.exp(inner * inner * -0.5) * 0.3989422804014327
    return inner * phi, phi + inner * density


def feed_kernel(
    place, lens, del_own, del_other, states, mix_own, mix_other, small, cot, pool_cot,
    p0, p1, p2, p3, r0, r1, r2, r3, f0, f1, f2, f3,
    output, pooled, residual_out, mg_own, mg_other, small_out, active, inner_low, low, outer_low, branch_low,
    w1, w2, slope, unit_a, scale_a, outer, grad, sems1, sems2,
):
    x = place[3]
    width = states.shape[1]
    count = states.shape[0]
    hidden = 4 * width
    part = width
    flat = p0.shape[2]
    in1 = blocks_in(place, (p0, p1, p2, p3), w1.at[:, :, :flat], sems1, PAIR_FLIPS)
    in1 += blocks_in(place, (r0, r1, r2, r3), w1.at[:, :, flat:], sems1, PAIR_FLIPS, 16)
    in2 = blocks_in(place, (f0, f1, f2, f3), w2, sems2, FULL_FLIPS)
    for copy in in1 + in2:
        copy.start()
    ends = crop_ends_of(lens)
    tags = tag_row(ends, x, del_own, del_other)
    slots = lax.broadcasted_iota(jnp.int32, (len(ends), count), 0)
    members = [(tag == slots).astype(F32) for tag in tags]
    counts = sum(jnp.sum(member, axis=1, keepdims=True) for member in members)
    divisor = jnp.maximum(counts, 1.0)
    member = jnp.where(x == 0, members[0], members[1])
    for copy in in1:
        copy.wait()

    def out_weight(side):
        return w1[pl.ds(side * 8, 8), :, :width].reshape(width // 2, width)

    branch = dot(mix_own[...], out_weight(x)) + dot(mix_other[...], out_weight(1 - x))
    branch = branch + small[2:3, :]
    unit, scale = norm_parts(states[...].astype(F32) + branch)
    unit_a[...] = unit
    scale_a[...] = scale
    value = unit * small[3:4, :] + small[4:5, :]
    low[...] = value.astype(BF)
    outer[...] = value + small[5:6, :]
    for copy in in2:
        copy.wait()

    def ahead(index, carry):
        begin = pl.multiple_of(index * part, part)
        weight = w1[:, :, pl.ds(width + begin, part)].reshape(width, part)
        inner = dot(low[...], weight) + small[pl.ds(8 + index, 1), :]
        act, bend = gelu_parts(inner)
        act = act.astype(BF)
        active[index] = act
        slope[index] = bend
        outer[...] += dot(act, w2[pl.ds(index * 8, 8)].reshape(part, width))
        return carry

    lax.fori_loop(0, hidden // part, ahead, 0)

    unit, scale = norm_parts(outer[...])
    result = unit * small[6:7, :] + small[7:8, :]
    output[...] = result.astype(BF)
    pooled[...] = exact_dot(member, result) / divisor
    grad_in = cot[...].astype(F32) + exact_dot(member, pool_cot[...] / divisor, 0, 0)
    small_out[0:2, :] = jnp.zeros((2, width), F32)
    small_out[12:16, :] = jnp.zeros((4, width), F32)
    small_out[6:7, :] = jnp.sum(grad_in * unit, axis=0, keepdims=True)
    small_out[7:8, :] = jnp.sum(grad_in, axis=0, keepdims=True)
    total = norm_back(grad_in, small[6:7, :], unit, scale)
    grad[...] = total
    outer_low[...] = total.astype(BF)
    small_out[5:6, :] = jnp.sum(outer_low[...].astype(F32), axis=0, keepdims=True)

    def back(index, carry):
        begin = pl.multiple_of(index * part, part)
        weight = w2[pl.ds(index * 8, 8)].reshape(part, width)
        inner = (dot(outer_low[...], weight, 1, 1) * slope[index]).astype(BF)
        inner_low[index] = inner
        small_out[pl.ds(8 + index, 1), :] = jnp.sum(inner.astype(F32), axis=0, keepdims=True)
        weight = w1[:, :, pl.ds(width + begin, part)].reshape(width, part)
        grad[...] += dot(inner, weight, 1, 1)
        return carry

    lax.fori_loop(0, hidden // part, back, 0)

    total = grad[...]
    unit = unit_a[...]
    small_out[3:4, :] = jnp.sum(total * unit, axis=0, keepdims=True)
    small_out[4:5, :] = jnp.sum(total, axis=0, keepdims=True)
    residual = norm_back(total, small[3:4, :], unit, scale_a[...])
    residual_out[...] = residual
    branch_low[...] = residual.astype(BF)
    small_out[2:3, :] = jnp.sum(branch_low[...].astype(F32), axis=0, keepdims=True)
    mg_own[...] = dot(branch_low[...], out_weight(x), 1, 1).astype(BF)
    mg_other[...] = dot(branch_low[...], out_weight(1 - x), 1, 1).astype(BF)


def outer_sum_kernel(place, active, outer_low, ka, kb, sa, sb, store, sems):
    step = pl.program_id(0)
    width = outer_low.shape[1]
    product_ = dot(active[0], outer_low[...], 0, 0).astype(BF)
    store[pl.ds(step * 8, 8)] = product_.reshape(8, width // 8, width)
    slot = lax.bitwise_xor(step, place[0])
    refs = (ka, kb, sa, sb)

    def copy(part, flip_y, spot, at, sem):
        return pltpu.make_async_copy(store.at[spot], refs[part].at[flip_y * 4 + at], sems.at[sem])

    for part in range(4):
        for flip_y in range(2):
            y = xor(place[1], flip_y)
            c = xor(place[2], part // 2)
            x = xor(place[3], part % 2)
            spot = ((step * 2 + y) * 2 + c) * 2 + x
            copy(part, flip_y, spot, slot, step * 8 + part * 2 + flip_y).start()

    @pl.when(step == 3)
    def _():
        for index in range(32):
            copy(0, 0, index, 0, index).wait()


def inner_sum_kernel(
    place, low, inner_low, branch_low, mix_own, mix_other,
    ka, kb, sa, sb, la, lb, ta, tb, store, low_t, sems,
):
    x = place[3]
    width = low.shape[1]
    copies = []

    def send(chunk):
        begin = chunk * width
        refs = (ka, kb, sa, sb)
        into = begin
        if begin >= ka.shape[2]:
            refs = (la, lb, ta, tb)
            into = begin - ka.shape[2]
        for part, flip in enumerate(PAIR_FLIPS):
            for slot in range(4):
                spot = slot_place(place, flip, slot)
                copy = pltpu.make_async_copy(
                    store.at[spot, :, begin : begin + width],
                    refs[part].at[slot, :, into : into + width],
                    sems.at[chunk * 16 + part * 4 + slot],
                )
                copy.start()
                copies.append(copy)

    low_t[...] = jnp.transpose(low[...])
    for side, mix in ((x, mix_own), (1 - x, mix_other)):
        product_ = dot(mix[...], branch_low[...], 0, 0).astype(BF)
        store[pl.ds(side * 8, 8), :, :width] = product_.reshape(8, width // 16, width)
    send(0)
    for index in range(inner_low.shape[0]):
        begin = (1 + index) * width
        product_ = dot(low_t[...], inner_low[index]).astype(BF)
        store[:, :, begin : begin + width] = product_.reshape(16, width // 16, width)
        send(1 + index)
    for copy in copies:
        copy.wait()


def blocks_out(place, parts, store, sems, flips, first):
    copies = []
    for part, (ref, offset) in enumerate(zip(parts, flips, strict=True)):
        for slot in range(ref.shape[0]):
            spot = slot_place(place, offset, slot)
            copies.append(
                pltpu.make_async_copy(
                    store.at[spot], ref.at[slot], sems.at[first + part * ref.shape[0] + slot]
                )
            )
    return copies


def retreat_kernel(
    place, lens, del_own, del_other, q_in, k_in, v_in, mg_own, mg_other, mix_own, mix_other,
    log_own, log_other, low, tags, dk, dv, *, pair,
):
    x = place[3]
    ends = crop_ends_of(lens)
    half = del_own.shape[1]

    for index, part in enumerate(tag_row(ends, x, del_own, del_other)):
        tall = jnp.transpose(jnp.broadcast_to(part.astype(F32), (8, half)))
        tags[index * half : (index + 1) * half, :] = tall[:, :1]
    dk[...] = jnp.zeros_like(dk)
    dv[...] = jnp.zeros_like(dv)
    block = half // 2
    wide = 3 * block
    special = window_start(ends, block)
    lane_low = lax.broadcasted_iota(jnp.int32, (block, 128), 1) < 64
    key_low = lax.broadcasted_iota(jnp.int32, (wide, 128), 1) < 64
    heads = lax.div(lax.broadcasted_iota(jnp.int32, (8, 128), 1), 64)
    picks = (heads == lax.broadcasted_iota(jnp.int32, (8, 128), 0)).astype(F32)
    eighth = jnp.asarray(0.125, BF)

    def turn(index, carry):
        start = jnp.where(index <= 1, 0, jnp.where(index == 2, special, block))
        start = pl.multiple_of(start, block)
        begin = pl.multiple_of(index * block, block)
        spot = pl.multiple_of(lax.rem(index, 2) * block, block)
        places = begin + lax.broadcasted_iota(jnp.int32, (1, block), 1)
        key_places = start + lax.broadcasted_iota(jnp.int32, (wide, 1), 0)
        allowed = (tags[pl.ds(start, wide), :] == segment_of(ends, places).astype(F32)) | (
            key_places == places
        )
        bias = jnp.where(allowed, 0.0, -1e30)
        queries = q_in[pl.ds(begin, block), :] * eighth
        keys = k_in[pl.ds(start, wide), :]
        values = v_in[pl.ds(start, wide), :]
        near = lax.div(index, 2) == x
        rows = pl.ds(spot, block)
        grads = jnp.where(near, mg_own[rows, :], mg_other[rows, :])
        mixed = jnp.where(near, mix_own[rows, :], mix_other[rows, :])
        deltas = exact_dot(picks, grads.astype(F32) * mixed.astype(F32), 1, 1)
        q_total = jnp.zeros((block, 128), F32)
        k_total = jnp.zeros((wide, 128), F32)
        v_total = jnp.zeros((wide, 128), F32)
        for side in range(2):
            mine = lane_low if side == 0 else ~lane_low
            key_mine = key_low if side == 0 else ~key_low
            q_mine = jnp.where(mine, queries, 0)
            g_mine = jnp.where(mine, grads, 0)
            row = slice(pair * 2 + side, pair * 2 + side + 1)
            log = jnp.where(near, log_own[row, rows], log_other[row, rows])
            probs = jnp.exp(dot(keys, q_mine, 1, 1) + (bias - log))
            prob_grad = dot(values, g_mine, 1, 1) - deltas[side : side + 1, :]
            score_grad = (probs * prob_grad).astype(BF)
            v_total = v_total + dot(probs.astype(BF), g_mine)
            k_total = k_total + dot(score_grad, q_mine)
            q_total = q_total + dot(score_grad, jnp.where(key_mine, keys * eighth, 0), 0, 0)
        low[pl.ds(begin, block), :128] = q_total.astype(BF)
        dk[pl.ds(start, wide), :] += k_total
        dv[pl.ds(start, wide), :] += v_total
        return carry

    lax.fori_loop(0, 4, turn, 0)
    low[:, 128:256] = dk[...].astype(BF)
    low[:, 256:] = dv[...].astype(BF)


def project_sum_kernel(
    place, st_own, st_other, low0, low1, low2, ka, kb, sa, sb, rows, store, rows_t, row_sems, sems
):
    x = place[3]
    row_copies = [
        pltpu.make_async_copy(st_own, rows.at[x], row_sems.at[0]),
        pltpu.make_async_copy(st_other, rows.at[1 - x], row_sems.at[1]),
    ]
    for copy in row_copies:
        copy.start()
    lows = (low0, low1, low2)
    wide = low0.shape[1]
    lane_rows = lax.broadcasted_iota(jnp.int32, (24, 128), 0)
    extra = jnp.zeros((24, 128), F32)
    for index, low in enumerate(lows):
        for kind in range(2):
            begin = kind * 256
            sums = jnp.sum(low[:, begin : begin + 128].astype(F32), axis=0, keepdims=True)
            extra = jnp.where(lane_rows == kind * 3 + index, sums, extra)
    extra = jnp.concatenate([extra, extra], axis=0).astype(BF)
    store[:, :, 3 * wide :] = jnp.broadcast_to(extra[None], (16, 48, 128))
    for copy in row_copies:
        copy.wait()
    rows_t[...] = jnp.transpose(rows[...].reshape(2 * st_own.shape[0], st_own.shape[1]))
    for index, low in enumerate(lows):
        columns = slice(index * wide, (index + 1) * wide)
        store[:, :, columns] = dot(rows_t[...], low[...]).astype(BF).reshape(16, 48, wide)
    copies = blocks_out(place, (ka, kb, sa, sb), store, sems, PAIR_FLIPS, 0)
    for copy in copies:
        copy.start()
    for copy in copies:
        copy.wait()


def states_sum_kernel(
    place, low0, low1, low2, residual, a0, a1, a2, a3, states_out, states_send, store, sems
):
    x = place[3]
    copies = blocks_in(place, (a0, a1, a2, a3), store, sems, PAIR_FLIPS)
    for copy in copies:
        copy.start()
    for copy in copies:
        copy.wait()
    half = residual.shape[0]
    wide = low0.shape[1]
    weight = store[:, :48, :].reshape(768, 3 * wide)

    def share(side):
        begin = pl.multiple_of(side * half, half)
        low = jnp.concatenate([ref[pl.ds(begin, half), :] for ref in (low0, low1, low2)], axis=1)
        return dot(low, weight, 1, 1)

    states_send[...] = share(1 - x).astype(BF)
    states_out[...] = residual[...] + share(x)


def swap(value, axis):
    return lax.ppermute(value, axis, [(0, 1), (1, 0)])


def hop(value, planes, bits):
    return lax.ppermute(value, DP, [(i, i ^ bits) for i in range(planes)])


def add(*terms):
    return sum((term.astype(F32) for term in terms[1:]), terms[0].astype(F32)).astype(BF)


def here():
    dp, c, x = lax.axis_index(DP), lax.axis_index(FSDP), lax.axis_index(SEQ)
    return lax.div(dp, 2), lax.rem(dp, 2), c, x, (dp * 2 + c) * 2 + x


def call(kernel, outs, inputs, specs, scratch, name, grid=()):
    return pl.pallas_call(
        lambda *refs: kernel(here(), *refs),
        out_shape=[jax.ShapeDtypeStruct(shape, kind) for shape, kind, _ in outs],
        in_specs=[spec_of(key) for key in specs],
        out_specs=[spec_of(key) for _, _, key in outs],
        scratch_shapes=scratch,
        grid=grid,
        compiler_params=pltpu.CompilerParams(vmem_limit_bytes=60 * MIB),
        cost_estimate=pl.CostEstimate(flops=0, bytes_accessed=0, transcendentals=0),
        name=name,
    )(*inputs)


def spec_of(key):
    return pl.BlockSpec(memory_space=SPACES[key]) if isinstance(key, str) else key


SPACES = {"s": pltpu.SMEM, "v": pltpu.VMEM, "a": pl.ANY}


def after(value, *others):
    return lax.optimization_barrier((value,) + others)[0]


class Order:
    def __init__(self, last):
        self.last = last

    def take(self, *values):
        values = lax.optimization_barrier(values + (self.last,))[:-1]
        return values if len(values) > 1 else values[0]

    def step(self, value):
        self.last = value
        return value


def column(rows, index):
    return pl.BlockSpec((rows, 128), lambda step: (0, index))


def halves_body(
    states, deleted, crop_lengths,
    query_weight, query_bias, key_weight, value_weight, value_bias, output_weight, output_bias,
    attn_gain, attn_shift, inner_weight, inner_bias, outer_weight, outer_bias, final_gain,
    final_shift, cotangent, pool_cotangent,
):
    planes = 8
    count, width = states.shape[1:]
    half = width // 2
    hidden = inner_weight.shape[1]
    part = query_weight.shape[0]
    long = outer_weight.shape[0]
    crops = crop_lengths.shape[1]
    tall = 3 * half
    flat = width + hidden // 2
    dma = pltpu.SemaphoreType.DMA
    dp, c, x = lax.axis_index(DP), lax.axis_index(FSDP), lax.axis_index(SEQ)
    device = (dp * 2 + c) * 2 + x
    lens = crop_lengths[0]
    own = states[0]

    vectors = [
        vector[None]
        for vector in (
            query_bias, value_bias, output_bias, attn_gain, attn_shift, outer_bias, final_gain,
            final_shift, inner_bias,
        )
    ]
    send, keep, small, p1, p2 = call(
        pack_kernel,
        [
            ((part, tall + width + hidden), BF, "v"),
            ((part, tall), BF, "v"),
            ((16, width), BF, "v"),
            ((part, width + hidden), BF, "v"),
            ((long, width), BF, "v"),
        ],
        (query_weight, key_weight, value_weight, output_weight, inner_weight, outer_weight, *vectors),
        "v" * 15,
        [],
        "pack",
    )

    def pair_up(mine, theirs):
        return jnp.where(
            x == 0,
            jnp.concatenate([mine, theirs], axis=0),
            jnp.concatenate([theirs, mine], axis=0),
        )

    def along_z(block):
        return tuple(hop(block, planes, bits) for bits in (2, 4, 6))

    order = Order(p2)
    sent_2 = along_z(p2)
    del_other, from_x, small_x = order.take(swap(deleted, SEQ), swap(send, SEQ), swap(small, SEQ))
    tail = jnp.pad(add(small, small_x), ((0, 0), (0, tall - width)))
    both_a = jnp.concatenate([pair_up(keep, from_x[:, :tall]), tail], axis=0)
    both_1 = pair_up(p1[:, :flat], from_x[:, tall : tall + flat])
    both_b = pair_up(p1[:, flat:], from_x[:, tall + flat :])
    order.step(both_a)
    sent_a = along_z(both_a)
    other = swap(order.take(own), SEQ)
    quad_2 = order.step(jnp.stack([p2, *order.take(*sent_2)]))
    octet = hop(quad_2, planes, 1)
    quad_a = order.step(jnp.stack([both_a, *order.take(*sent_a)]))
    quad_ay = hop(quad_a, planes, 1)
    sent_1 = along_z(order.take(both_1))
    octet = order.step(jnp.concatenate([quad_2, order.take(octet)], axis=0))
    octet_x = swap(octet, SEQ)
    quad_ay, other = order.take(quad_ay, other)
    order.step(quad_ay)
    quad_1 = order.step(jnp.stack([both_1, *order.take(*sent_1)]))
    parts_a = order.take(swap(quad_a, FSDP), swap(quad_ay, FSDP))
    parts_a = (quad_a, quad_ay) + parts_a
    order.step(parts_a[-1])
    quad_1y = hop(quad_1, planes, 1)
    sent_b = along_z(after(both_b, quad_1))

    marks = (lens, deleted, del_other)
    queries, keys, values, mix_send, log_other, small = call(
        attend_kernel,
        [((2 * count, half), BF, "v")] * 3
        + [((count, half), BF, "v"), ((8, count), F32, "v"), ((16, width), F32, "v")],
        marks + (order.take(own), other) + parts_a,
        "svvaaaaaa",
        [
            pltpu.VMEM((16, 64, tall), BF),
            pltpu.VMEM((2, count, width), BF),
            pltpu.VMEM((1, 2 * count), jnp.int32),
            dma((16,)),
            dma((2,)),
        ],
        "attend",
    )
    order.step(mix_send)
    mix_other = swap(mix_send, SEQ)
    quad_1y = order.step(order.take(quad_1y))
    quad_b = order.step(jnp.stack([both_b, *order.take(*sent_b)]))
    quad_by = hop(quad_b, planes, 1)
    mix_own, log_own = call(
        attend_own_kernel,
        [((count, half), BF, "v"), ((8, count), F32, "v")],
        marks + (order.take(queries), keys, values),
        "svvvvv",
        [pltpu.VMEM((1, 2 * count), jnp.int32)],
        "attend_own",
    )
    order.step(mix_own)
    octet_x, mix_other = order.take(octet_x, mix_other)
    order.step(octet_x)
    parts_2 = (octet, octet_x, swap(octet, FSDP), swap(octet_x, FSDP))
    parts_1 = (quad_1, quad_1y, swap(quad_1, FSDP), swap(quad_1y, FSDP))
    quad_by = order.take(quad_by)
    parts_1 += (quad_b, quad_by, swap(quad_b, FSDP), swap(quad_by, FSDP))
    four = ((hidden // width, count, width), BF, "v")
    tokens = ((count, width), BF, "v")
    (
        output, pooled, residual, mg_own, mg_send, small_grad,
        active, inner_low, low, outer_low, branch_low,
    ) = call(
        feed_kernel,
        [
            tokens,
            ((crops, width), F32, "v"),
            ((count, width), F32, "v"),
            ((count, half), BF, "v"),
            ((count, half), BF, "v"),
            ((16, width), F32, "v"),
            four, four, tokens, tokens, tokens,
        ],
        marks
        + (own, mix_own, mix_other, small, cotangent[0], pool_cotangent[0])
        + parts_1
        + parts_2,
        "svvvvvvvv" + "a" * 12,
        [
            pltpu.VMEM((16, 2 * part, width + hidden), BF),
            pltpu.VMEM((32, long, width), BF),
            pltpu.VMEM((hidden // width, count, width), F32),
            pltpu.VMEM((count, width), F32),
            pltpu.VMEM((count, 1), F32),
            pltpu.VMEM((count, width), F32),
            pltpu.VMEM((count, width), F32),
            dma((32,)),
            dma((32,)),
        ],
        "feed",
    )
    mg_other = swap(mg_send, SEQ)

    blocks_2 = ((8, long, width), BF, "a")
    keep_2a, keep_2b, send_2a, send_2b = call(
        outer_sum_kernel,
        [blocks_2] * 4,
        (active, outer_low),
        [pl.BlockSpec((1, count, width), lambda step: (step, 0, 0)), "v"],
        [pltpu.VMEM((32, long, width), BF), dma((32,))],
        "outer_sum",
        (hidden // width,),
    )
    order.step(send_2b)
    core_2b, core_small = swap(send_2b, FSDP), swap(small_grad, FSDP)
    blocks_a = ((4, 2 * part, flat), BF, "a")
    blocks_b = ((4, 2 * part, width + hidden - flat), BF, "a")
    keep_1a, keep_1b, send_1a, send_1b, keep_3a, keep_3b, send_3a, send_3b = call(
        inner_sum_kernel,
        [blocks_a] * 4 + [blocks_b] * 4,
        (order.take(low), inner_low, branch_low, mix_own, mix_other),
        "vvvvv",
        [
            pltpu.VMEM((16, 2 * part, width + hidden), BF),
            pltpu.VMEM((width, count), BF),
            dma((80,)),
        ],
        "inner_sum",
    )
    order.step(send_1b)
    core_2b, core_small, mg_other = order.take(core_2b, core_small, mg_other)
    t1_2 = order.step(add(keep_2b, core_2b))
    sum_2x = swap(t1_2, SEQ)
    smalls = small_grad + core_small
    small_y = hop(smalls, planes, 1)
    t1_1 = order.step(add(keep_1b, order.take(swap(send_1b, FSDP))))
    sum_1y = hop(t1_1, planes, 1)
    t1_3 = order.step(add(keep_3b, order.take(swap(send_3b, FSDP))))
    sum_3y = hop(t1_3, planes, 1)
    core_2, core_1, core_3 = (
        swap(value, FSDP) for value in order.take(send_2a, send_1a, send_3a)
    )

    def retreat(pair):
        specs = ["s", "v", "v"] + [column(2 * count, pair)] * 3 + [column(count, pair)] * 4
        (result,) = call(
            partial(retreat_kernel, pair=pair),
            [((2 * count, 384), BF, "v")],
            marks
            + (order.take(queries), keys, values)
            + (mg_own, mg_other, mix_own, mix_send, log_own, log_other),
            specs + ["v", "v"],
            [
                pltpu.VMEM((2 * count, 1), F32),
                pltpu.VMEM((2 * count, 128), F32),
                pltpu.VMEM((2 * count, 128), F32),
            ],
            "retreat",
            (1,),
        )
        return order.step(result)

    def split_x(v):
        v = v.reshape((2, part) + v.shape[1:])
        return jnp.where(x == 0, v[0], v[1]), swap(jnp.where(x == 0, v[1], v[0]), SEQ)

    def to_z(u):
        return tuple(hop(u[index], planes, 2 * index) for index in (1, 2, 3))

    def split_x(v):
        v = v.reshape((2, part) + v.shape[1:])
        return jnp.where(x == 0, v[0], v[1]), swap(jnp.where(x == 0, v[1], v[0]), SEQ)

    def to_z(u):
        return tuple(hop(u[index], planes, 2 * index) for index in (1, 2, 3))

    lows = [retreat(0), retreat(1)]
    u_1 = order.step(add(keep_1a, *order.take(core_1, sum_1y)))
    sum_1z = to_z(u_1)
    lows.append(retreat(2))
    u_3 = order.step(add(keep_3a, *order.take(core_3, sum_3y)))
    sum_3z = to_z(u_3)
    u_2 = order.step(add(keep_2a, *order.take(core_2, sum_2x)))
    sum_2y = hop(u_2[4:], planes, 1)
    wide = tall + 128
    keep_a, keep_b, send_a, send_b = call(
        project_sum_kernel,
        [((4, 2 * part, wide), BF, "a")] * 4,
        (order.take(own), other, *lows),
        "aavvv",
        [
            pltpu.VMEM((2, count, width), BF),
            pltpu.VMEM((16, 2 * part, wide), BF),
            pltpu.VMEM((width, 2 * count), BF),
            dma((2,)),
            dma((16,)),
        ],
        "project_sum",
    )
    order.step(send_b)
    core_b, core_a = swap(send_b, FSDP), swap(send_a, FSDP)
    v_1 = order.step(add(u_1[0], *order.take(*sum_1z)))
    smalls = smalls + order.take(small_y)
    small_z = hop(smalls, planes, 2)
    v_2 = order.step(add(u_2[:4], order.take(sum_2y)))
    sum_2z = to_z(v_2)
    t1_a = order.step(add(keep_b, order.take(core_b)))
    sum_ay = hop(t1_a, planes, 1)
    states_part, states_send = call(
        states_sum_kernel,
        [((count, width), F32, "v"), tokens],
        (order.take(lows[0]), lows[1], lows[2], residual) + parts_a,
        "vvvvaaaa",
        [pltpu.VMEM((16, 64, tall), BF), dma((16,))],
        "states_sum",
    )
    order.step(states_send)
    states_x = swap(states_send, SEQ)
    u_a = order.step(add(keep_a, *order.take(core_a, sum_ay)))
    sum_az = to_z(u_a)
    v = order.step(jnp.concatenate([v_1, add(u_3[0], *order.take(*sum_3z))], axis=1))
    mine_1, theirs_1 = split_x(v)
    smalls = order.step(smalls + order.take(small_z))
    small_z = hop(smalls, planes, 4)
    pooled_x = swap(pooled, SEQ)
    states_grad = order.step(states_part + order.take(states_x).astype(F32))
    v = order.step(add(u_a[0], *order.take(*sum_az)))
    mine_a, theirs_a = split_x(v)
    smalls = order.step(smalls + order.take(small_z))
    small_x = swap(smalls, SEQ)
    total = mine_1.astype(F32) + order.take(theirs_1).astype(F32)
    order.step(total)
    grad_output_weight, grad_inner_weight = total[:, :width], total[:, width:]
    sum_2z = order.take(*sum_2z)
    grad_outer_weight = v_2[0].astype(F32) + sum(term.astype(F32) for term in sum_2z)
    order.step(grad_outer_weight)
    pooled = pooled + order.take(pooled_x)
    smalls = smalls + order.take(small_x)
    theirs = order.take(theirs_a)
    left = jnp.where(x == 0, mine_a, theirs).astype(F32)
    right = jnp.where(x == 0, theirs, mine_a).astype(F32)

    def gathered(index):
        columns = [
            side[:, (pair * 3 + index) * 128 : (pair * 3 + index + 1) * 128]
            for side in (left, right)
            for pair in range(half // 128)
        ]
        return jnp.concatenate(columns, axis=1)

    grad_query_weight, grad_key_weight, grad_value_weight = (gathered(i) for i in range(3))
    bias_grads = jnp.stack([left[:6, tall:], right[:6, tall:]]).reshape(2, 2, half)
    bias_grads = jnp.transpose(bias_grads, (1, 0, 2)).reshape(2, width)
    vectors = lax.dynamic_slice(smalls[:8], (0, device * part), (8, part))
    bias_grads = lax.dynamic_slice(bias_grads, (0, device * part), (2, part))
    grad_inner_bias = lax.dynamic_slice(
        smalls[8:12].reshape(hidden), (device * long,), (long,)
    )
    return (
        output[None],
        pooled[None],
        states_grad[None],
        grad_query_weight,
        bias_grads[0],
        grad_key_weight,
        grad_value_weight,
        bias_grads[1],
        grad_output_weight,
        vectors[2],
        vectors[3],
        vectors[4],
        grad_inner_weight,
        grad_inner_bias,
        grad_outer_weight,
        vectors[5],
        vectors[6],
        vectors[7],
    )


def solution(mesh):
    in_specs = (
        P(ROWS, SEQ, None),
        P(ROWS, SEQ),
        P(ROWS, None),
        BY_ROW,
        FLAT,
        BY_ROW,
        BY_ROW,
        FLAT,
        BY_ROW,
        FLAT,
        FLAT,
        FLAT,
        BY_ROW,
        FLAT,
        BY_ROW,
        FLAT,
        FLAT,
        FLAT,
        P(ROWS, SEQ, None),
        P(ROWS, None, None),
    )
    out_specs = (
        P(ROWS, SEQ, None),
        P(ROWS, None, None),
        P(ROWS, SEQ, None),
        BY_ROW,
        FLAT,
        BY_ROW,
        BY_ROW,
        FLAT,
        BY_ROW,
        FLAT,
        FLAT,
        FLAT,
        BY_ROW,
        FLAT,
        BY_ROW,
        FLAT,
        FLAT,
        FLAT,
    )
    shape = mesh.shape
    halves = (shape[DP], shape[FSDP], shape[SEQ]) == (8, 2, 2)
    chosen = halves_body if halves else body
    return jax.shard_map(chosen, mesh=mesh, in_specs=in_specs, out_specs=out_specs, check_vma=False)
```

```python
from functools import partial

import jax
import jax.numpy as jnp
from jax import lax
from jax.experimental import pallas as pl
from jax.experimental.pallas import tpu as pltpu
from jax.sharding import PartitionSpec as P

HEADS = 12
HEAD = 64


highest = lax.Precision.HIGHEST
DP, FSDP, SEQ = "dp", "fsdp", "seq"
EVERY = (DP, FSDP, SEQ)
BY_ROW, FLAT = P(EVERY, None), P(EVERY)
ROWS = (DP, FSDP)


def layer_norm(values, gain, shift):
    centered = values - jnp.mean(values, axis=-1, keepdims=True)
    spread = jnp.mean(centered * centered, axis=-1, keepdims=True)
    return centered * lax.rsqrt(spread + 1e-06) * gain + shift


def crop_layout(lengths, deleted, places):
    crop_ends = jnp.cumsum(lengths, axis=-1, dtype=jnp.int32)
    segment = jnp.sum(
        (places[..., :, None] >= crop_ends[..., None, :]).astype(jnp.int32),
        axis=-1,
        dtype=jnp.int32,
    )
    retained = (deleted == 0) & (segment < lengths.shape[-1])
    key_tag = jnp.where(retained, segment, -1)
    return (segment, retained, key_tag)


def product(left, right):
    return jnp.dot(left, right, preferred_element_type=jnp.float32)


def column_sum(values):
    return jnp.sum(values.astype(jnp.float32), axis=0)


def sweep(carry, pieces, inner):
    count = pieces[0].shape[1]
    width = 256

    def turn(index, totals):
        offset = index * width
        parts = tuple((lax.dynamic_slice_in_dim(piece, offset, width, 1) for piece in pieces))
        return inner(totals, parts, offset)

    return lax.fori_loop(0, count // width, turn, carry)


def scores_at(query_part, key_part):
    return (
        jnp.einsum("rqhd,rkhd->rhqk", query_part, key_part, preferred_element_type=jnp.float32)
        * 0.125
    )


def allowed_at(query_tag, query_place, tags, begin):
    key_place = begin + jnp.arange(tags.shape[1], dtype=jnp.int32)
    same = tags[:, None, :] == query_tag[:, :, None]
    itself = key_place[None, None, :] == query_place[None, :, None]
    return (same | itself)[:, None]


def probs_at(raw, allowed, log_part):
    return jnp.where(allowed, jnp.exp(raw - log_part[..., None]), 0.0)


def body(
    states,
    deleted,
    crop_lengths,
    query_weight,
    query_bias,
    key_weight,
    value_weight,
    value_bias,
    output_weight,
    output_bias,
    attn_gain,
    attn_shift,
    inner_weight,
    inner_bias,
    outer_weight,
    outer_bias,
    final_gain,
    final_shift,
    cotangent,
    pool_cotangent,
):
    rows, shard, width = states.shape
    lowered = [
        master.astype(jnp.bfloat16)
        for master in (
            query_weight,
            query_bias,
            key_weight,
            value_weight,
            value_bias,
            output_weight,
            output_bias,
            attn_gain,
            attn_shift,
            inner_weight,
            inner_bias,
            outer_weight,
            outer_bias,
            final_gain,
            final_shift,
        )
    ]
    (
        w_query,
        b_query,
        w_key,
        w_value,
        b_value,
        w_out,
        b_out,
        g_attn,
        s_attn,
        w_inner,
        b_inner,
        w_outer,
        b_outer,
        g_final,
        s_final,
    ) = (
        lax.all_gather(lowered[0], EVERY, axis=0, tiled=True),
        lax.all_gather(lowered[1], EVERY, axis=0, tiled=True),
        lax.all_gather(lowered[2], EVERY, axis=0, tiled=True),
        lax.all_gather(lowered[3], EVERY, axis=0, tiled=True),
        lax.all_gather(lowered[4], EVERY, axis=0, tiled=True),
        lax.all_gather(lowered[5], EVERY, axis=0, tiled=True),
        lax.all_gather(lowered[6], EVERY, axis=0, tiled=True),
        lax.all_gather(lowered[7], EVERY, axis=0, tiled=True),
        lax.all_gather(lowered[8], EVERY, axis=0, tiled=True),
        lax.all_gather(lowered[9], EVERY, axis=0, tiled=True),
        lax.all_gather(lowered[10], EVERY, axis=0, tiled=True),
        lax.all_gather(lowered[11], EVERY, axis=0, tiled=True),
        lax.all_gather(lowered[12], EVERY, axis=0, tiled=True),
        lax.all_gather(lowered[13], EVERY, axis=0, tiled=True),
        lax.all_gather(lowered[14], EVERY, axis=0, tiled=True),
    )
    own_start = lax.axis_index(SEQ) * shard
    places = own_start + jnp.arange(shard, dtype=jnp.int32)
    segment, retained, key_tag = crop_layout(crop_lengths, deleted, places)
    flat = states.reshape(rows * shard, width)
    split = (rows, shard, HEADS, HEAD)
    queries = (product(flat, w_query) + b_query).astype(jnp.bfloat16).reshape(split)
    keys = product(flat, w_key).astype(jnp.bfloat16).reshape(split)
    values = (product(flat, w_value) + b_value).astype(jnp.bfloat16).reshape(split)

    def scale_step(totals, parts, begin):
        top, total = totals
        key_part, tags = parts
        allowed = allowed_at(segment, places, tags, begin)
        masked = jnp.where(allowed, scores_at(queries, key_part), -1e30)
        new_top = jnp.maximum(top, jnp.max(masked, axis=-1))
        raised = jnp.where(allowed, jnp.exp(masked - new_top[..., None]), 0.0)
        return (new_top, total * jnp.exp(top - new_top) + jnp.sum(raised, axis=-1))

    stat_shape = (rows, HEADS, shard)
    scale_init = (jnp.full(stat_shape, -1e30, jnp.float32), jnp.zeros(stat_shape, jnp.float32))
    top, total = sweep(
        scale_init,
        (
            lax.all_gather(keys, SEQ, axis=1, tiled=True),
            lax.all_gather(key_tag, SEQ, axis=1, tiled=True),
        ),
        inner=scale_step,
    )
    log_total = top + jnp.log(total)

    def mix_step(totals, parts, begin):
        coarse, fine = totals
        key_part, value_part, tags = parts
        probs = probs_at(
            scores_at(queries, key_part), allowed_at(segment, places, tags, begin), log_total
        )
        probs_low = probs.astype(jnp.bfloat16)
        rest = (probs - probs_low.astype(jnp.float32)).astype(jnp.bfloat16)
        coarse = coarse + jnp.einsum(
            "rhqk,rkhd->rqhd", probs_low, value_part, preferred_element_type=jnp.float32
        )
        fine = fine + jnp.einsum(
            "rhqk,rkhd->rqhd", rest, value_part, preferred_element_type=jnp.float32
        )
        return (coarse, fine)

    empty = jnp.zeros(split, jnp.float32)
    coarse, fine = sweep(
        (empty, empty),
        (
            lax.all_gather(keys, SEQ, axis=1, tiled=True),
            lax.all_gather(values, SEQ, axis=1, tiled=True),
            lax.all_gather(key_tag, SEQ, axis=1, tiled=True),
        ),
        inner=mix_step,
    )
    attended = coarse.astype(jnp.bfloat16).reshape(rows * shard, width)
    branch = product(attended, w_out) + b_out
    residual = states.astype(jnp.float32).reshape(rows * shard, width) + branch
    normed, attn_back = jax.vjp(
        layer_norm, residual, g_attn.astype(jnp.float32), s_attn.astype(jnp.float32)
    )
    normed_low = normed.astype(jnp.bfloat16)
    inner = product(normed_low, w_inner) + b_inner
    active_full, gelu_back = jax.vjp(partial(jax.nn.gelu, approximate=False), inner)
    active = active_full.astype(jnp.bfloat16)
    outer = product(active, w_outer) + b_outer
    result, final_back = jax.vjp(
        layer_norm, normed + outer, g_final.astype(jnp.float32), s_final.astype(jnp.float32)
    )
    output = result.astype(jnp.bfloat16).reshape(rows, shard, width)
    crops = crop_lengths.shape[1]
    member = (
        (segment[..., None] == jnp.arange(crops, dtype=jnp.int32)) & retained[..., None]
    ).astype(jnp.float32)
    partial_sums = jnp.einsum(
        "rnc,rnd->rcd",
        member,
        result.reshape(rows, shard, width),
        precision=highest,
        preferred_element_type=jnp.float32,
    )
    sums, counts = lax.psum((partial_sums, jnp.sum(member, axis=1)), SEQ)
    divisor = jnp.maximum(counts, 1.0)[..., None]
    pooled = sums / divisor
    w_query, w_key, w_value, w_out, w_inner, w_outer = (
        lax.all_gather(lowered[0], EVERY, axis=0, tiled=True),
        lax.all_gather(lowered[2], EVERY, axis=0, tiled=True),
        lax.all_gather(lowered[3], EVERY, axis=0, tiled=True),
        lax.all_gather(lowered[5], EVERY, axis=0, tiled=True),
        lax.all_gather(lowered[9], EVERY, axis=0, tiled=True),
        lax.all_gather(lowered[11], EVERY, axis=0, tiled=True),
    )
    result_grad = cotangent.astype(jnp.float32) + jnp.einsum(
        "rnc,rcd->rnd",
        member,
        pool_cotangent / divisor,
        precision=highest,
        preferred_element_type=jnp.float32,
    )
    sum_grad, grad_final_gain, grad_final_shift = final_back(
        result_grad.reshape(rows * shard, width)
    )
    outer_grad = sum_grad.astype(jnp.bfloat16)
    grad_outer_bias = column_sum(outer_grad)
    grad_outer_weight = product(active.T, outer_grad)
    inner_grad = gelu_back(product(outer_grad, w_outer.T))[0].astype(jnp.bfloat16)
    grad_inner_bias = column_sum(inner_grad)
    grad_inner_weight = product(normed_low.T, inner_grad)
    normed_grad = sum_grad + product(inner_grad, w_inner.T)
    residual_grad, grad_attn_gain, grad_attn_shift = attn_back(normed_grad)
    branch_grad = residual_grad.astype(jnp.bfloat16)
    grad_output_bias = column_sum(branch_grad)
    grad_output_weight = product(attended.T, branch_grad)
    mixed_grad = product(branch_grad, w_out.T).astype(jnp.bfloat16).reshape(split)
    delta = jnp.sum(mixed_grad.astype(jnp.float32) * (coarse + fine), axis=-1)
    delta_local = jnp.transpose(delta, (0, 2, 1))
    all_log, all_delta = (
        lax.all_gather(jnp.transpose(log_total, (0, 2, 1)), SEQ, axis=1, tiled=True),
        lax.all_gather(delta, SEQ, axis=1, tiled=True),
    )

    def key_side(totals, parts, begin):
        key_grad, value_grad = totals
        query_part, grad_part, tags_part = parts
        count = tags_part.shape[1]
        log_part = jnp.transpose(lax.dynamic_slice_in_dim(all_log, begin, count, 1), (0, 2, 1))
        delta_part = jnp.transpose(lax.dynamic_slice_in_dim(all_delta, begin, count, 1), (0, 2, 1))
        query_place = begin + jnp.arange(count, dtype=jnp.int32)
        allowed = allowed_at(tags_part, query_place, key_tag, own_start)
        probs = probs_at(scores_at(query_part, keys), allowed, log_part)
        value_grad = value_grad + jnp.einsum(
            "rhqk,rqhd->rkhd",
            probs.astype(jnp.bfloat16),
            grad_part,
            preferred_element_type=jnp.float32,
        )
        prob_grad = jnp.einsum(
            "rqhd,rkhd->rhqk", grad_part, values, preferred_element_type=jnp.float32
        )
        score_grad = (probs * (prob_grad - delta_part[..., None]) * 0.125).astype(jnp.bfloat16)
        key_grad = key_grad + jnp.einsum(
            "rhqk,rqhd->rkhd", score_grad, query_part, preferred_element_type=jnp.float32
        )
        return (key_grad, value_grad)

    key_grad, value_grad = sweep(
        (empty, empty),
        (
            lax.all_gather(queries, SEQ, axis=1, tiled=True),
            lax.all_gather(mixed_grad, SEQ, axis=1, tiled=True),
            lax.all_gather(segment, SEQ, axis=1, tiled=True),
        ),
        inner=key_side,
    )

    def query_side(query_grad, parts, begin):
        key_part, value_part, tags = parts
        probs = probs_at(
            scores_at(queries, key_part), allowed_at(segment, places, tags, begin), log_total
        )
        prob_grad = jnp.einsum(
            "rqhd,rkhd->rhqk", mixed_grad, value_part, preferred_element_type=jnp.float32
        )
        score_grad = (probs * (prob_grad - delta_local[..., None]) * 0.125).astype(jnp.bfloat16)
        return query_grad + jnp.einsum(
            "rhqk,rkhd->rqhd", score_grad, key_part, preferred_element_type=jnp.float32
        )

    query_grad = sweep(
        empty,
        (
            lax.all_gather(keys, SEQ, axis=1, tiled=True),
            lax.all_gather(values, SEQ, axis=1, tiled=True),
            lax.all_gather(key_tag, SEQ, axis=1, tiled=True),
        ),
        inner=query_side,
    )
    query_low = query_grad.astype(jnp.bfloat16).reshape(rows * shard, width)
    key_low = key_grad.astype(jnp.bfloat16).reshape(rows * shard, width)
    value_low = value_grad.astype(jnp.bfloat16).reshape(rows * shard, width)
    grad_query_weight = product(flat.T, query_low)
    grad_query_bias = column_sum(query_low)
    grad_key_weight = product(flat.T, key_low)
    grad_value_weight = product(flat.T, value_low)
    grad_value_bias = column_sum(value_low)
    states_grad = (
        residual_grad
        + product(query_low, w_query.T)
        + product(key_low, w_key.T)
        + product(value_low, w_value.T)
    ).reshape(rows, shard, width)
    summed = (
        lax.psum_scatter(grad_query_weight, EVERY, scatter_dimension=0, tiled=True),
        lax.psum_scatter(grad_query_bias, EVERY, scatter_dimension=0, tiled=True),
        lax.psum_scatter(grad_key_weight, EVERY, scatter_dimension=0, tiled=True),
        lax.psum_scatter(grad_value_weight, EVERY, scatter_dimension=0, tiled=True),
        lax.psum_scatter(grad_value_bias, EVERY, scatter_dimension=0, tiled=True),
        lax.psum_scatter(
            grad_output_weight, EVERY, scatter_dimension=0, tiled=True
        ),
        lax.psum_scatter(grad_output_bias, EVERY, scatter_dimension=0, tiled=True),
        lax.psum_scatter(grad_attn_gain, EVERY, scatter_dimension=0, tiled=True),
        lax.psum_scatter(grad_attn_shift, EVERY, scatter_dimension=0, tiled=True),
        lax.psum_scatter(grad_inner_weight, EVERY, scatter_dimension=0, tiled=True),
        lax.psum_scatter(grad_inner_bias, EVERY, scatter_dimension=0, tiled=True),
        lax.psum_scatter(grad_outer_weight, EVERY, scatter_dimension=0, tiled=True),
        lax.psum_scatter(grad_outer_bias, EVERY, scatter_dimension=0, tiled=True),
        lax.psum_scatter(grad_final_gain, EVERY, scatter_dimension=0, tiled=True),
        lax.psum_scatter(grad_final_shift, EVERY, scatter_dimension=0, tiled=True),
    )
    return (output, pooled, states_grad) + tuple(summed)


BF = jnp.bfloat16
F32 = jnp.float32
MIB = 1 << 20


def dot(left, right, left_dim=1, right_dim=0):
    return lax.dot_general(
        left,
        right,
        (((left_dim,), (right_dim,)), ((), ())),
        preferred_element_type=F32,
    )


def exact_dot(left, right, left_dim=1, right_dim=0):
    return lax.dot_general(
        left,
        right,
        (((left_dim,), (right_dim,)), ((), ())),
        precision=highest,
        preferred_element_type=F32,
    )


def crop_ends_of(lens_ref):
    ends, total = [], jnp.int32(0)
    for slot in range(lens_ref.shape[0]):
        total = total + lens_ref[slot]
        ends.append(total)
    return ends


def segment_of(ends, places):
    segment = jnp.zeros(places.shape, jnp.int32)
    for end in ends:
        segment = segment + (places >= end).astype(jnp.int32)
    return segment


def for_windows(ends, block, first, last, turn):
    begin = ends[0] * 0
    for end in ends:
        begin = jnp.maximum(begin, jnp.where(end <= 2 * block, end, 0))
    single = (begin < block).astype(jnp.int32)

    def three(index, carry):
        start = jnp.where(index == 2, 1 - single, 0) * block
        turn(index, pl.multiple_of(start, block), 3)
        return carry

    def two(index, carry):
        start = jnp.where(index == 0, 0, 2) * block
        turn(index, pl.multiple_of(start, block), 2)
        return carry

    def one(index, carry):
        turn(index, pl.multiple_of(index * block, block), 1)
        return carry

    low = jnp.maximum(first, 1 - single)
    lax.fori_loop(low, jnp.minimum(last, 3), three, 0)
    lax.fori_loop(first, jnp.where((first == 0) & (single == 0), 1, first), two, 0)
    final = jnp.where(last == 4, 1, 0)
    lax.fori_loop(3, 3 + final * (1 - single), two, 0)
    lax.fori_loop(3, 3 + final * single, one, 0)


def pack_kernel(
    place, wq, wk, wv, wo, w1, w2, v0, v1, v2, v3, v4, v5, v6, v7, v96,
    send, keep, small, p1, p2,
):
    x = place[3]
    device = place[4]
    half = wq.shape[1] // 2
    for pair in range(half // 128):
        for index, ref in enumerate((wq, wk, wv)):
            left = ref[:, pair * 128 : pair * 128 + 128].astype(BF)
            right = ref[:, half + pair * 128 : half + pair * 128 + 128].astype(BF)
            begin = (pair * 3 + index) * 128
            keep[:, begin : begin + 128] = jnp.where(x == 0, left, right)
            send[:, begin : begin + 128] = jnp.where(x == 0, right, left)
    width = wo.shape[1]
    tall = keep.shape[1]
    for ref, begin in ((send, tall), (p1, 0)):
        ref[:, begin : begin + width] = wo[...].astype(BF)
        ref[:, begin + width :] = w1[...].astype(BF)
    p2[...] = w2[...].astype(BF)
    part = v0.shape[1]
    row = lax.broadcasted_iota(jnp.int32, (8, part), 0)
    stacked = jnp.zeros((8, part), F32)
    for index, ref in enumerate((v0, v1, v2, v3, v4, v5, v6, v7)):
        stacked = jnp.where(row == index, ref[...], stacked)
    row = lax.broadcasted_iota(jnp.int32, (part, width), 0)
    lane = lax.broadcasted_iota(jnp.int32, (part, width), 1)
    spread = (row + device * part == lane).astype(BF)
    first = dot(stacked.astype(BF), spread)
    part = v96.shape[1]
    row = lax.broadcasted_iota(jnp.int32, (part, width), 0)
    lane = lax.broadcasted_iota(jnp.int32, (part, width), 1)
    rows = []
    for index in range(8):
        if index < v96.shape[1] * 32 // width:
            spread = (row + device * part == lane + index * width).astype(BF)
            rows.append(dot(jnp.broadcast_to(v96[...], (8, part)).astype(BF), spread))
    tall = lax.broadcasted_iota(jnp.int32, (8, width), 0)
    second = jnp.zeros((8, width), F32)
    for index, value in enumerate(rows):
        second = jnp.where(tall == index, value[:1], second)
    small[...] = jnp.concatenate([first, second], axis=0).astype(BF)


def blocks_in(place, parts, store, sems, flips, first=0):
    copies = []
    for part, (ref, offset) in enumerate(zip(parts, flips, strict=True)):
        for slot in range(ref.shape[0]):
            spot = slot_place(place, offset, slot)
            copies.append(
                pltpu.make_async_copy(
                    ref.at[slot], store.at[spot], sems.at[first + part * ref.shape[0] + slot]
                )
            )
    return copies


def xor(value, bits):
    if bits & 1:
        value = value + 1 - 2 * lax.rem(value, 2)
    if bits & 2:
        value = lax.rem(value + 2, 4)
    return value


def slot_place(place, flip, slot):
    flip_y, flip_c, flip_x = flip
    z = xor(place[0], slot % 4)
    y = xor(place[1], flip_y ^ (slot // 4))
    c = xor(place[2], flip_c)
    spot = (z * 2 + y) * 2 + c
    if flip_x is None:
        return spot
    return spot * 2 + xor(place[3], flip_x)


PAIR_FLIPS = ((0, 0, None), (1, 0, None), (0, 1, None), (1, 1, None))
FULL_FLIPS = ((0, 0, 0), (0, 0, 1), (0, 1, 0), (0, 1, 1))


def tag_row(ends, x, own, other):
    half = own.shape[1]
    parts = []
    for index in range(2):
        deleted = jnp.where(x == index, own[...], other[...])
        places = index * half + lax.broadcasted_iota(jnp.int32, (1, half), 1)
        segment = segment_of(ends, places)
        parts.append(jnp.where((deleted == 0) & (segment < len(ends)), segment, -1))
    return parts


def attend_block(ends, tags, q_ref, k_ref, v_ref, index, block, start, wide):
    wide = wide * block
    lane_low = lax.broadcasted_iota(jnp.int32, (block, 128), 1) < 64
    key_low = lax.broadcasted_iota(jnp.int32, (wide, 128), 1) < 64
    begin = pl.multiple_of(index * block, block)
    places = begin + lax.broadcasted_iota(jnp.int32, (block, 1), 0)
    key_places = start + lax.broadcasted_iota(jnp.int32, (1, wide), 1)
    allowed = (tags[0:1, pl.ds(start, wide)] == segment_of(ends, places)) | (key_places == places)
    bias = jnp.where(allowed, 0.0, -1e30)
    outs = []
    lanes = lax.broadcasted_iota(jnp.int32, (block, 128), 1)
    logs = jnp.zeros((block, 128), F32)
    for pair in range(q_ref.shape[1] // 128):
        columns = slice(pair * 128, pair * 128 + 128)
        queries = q_ref[pl.ds(begin, block), columns] * jnp.asarray(0.125, BF)
        keys = k_ref[pl.ds(start, wide), columns]
        values = v_ref[pl.ds(start, wide), columns]
        total = jnp.zeros((block, 128), F32)
        for side in range(2):
            mine = lane_low if side == 0 else ~lane_low
            key_mine = key_low if side == 0 else ~key_low
            scores = dot(jnp.where(mine, queries, 0), keys, 1, 1) + bias
            top = jnp.max(scores, axis=1, keepdims=True)
            raised = jnp.exp(scores - top)
            amount = jnp.sum(raised, axis=1, keepdims=True)
            probs = (raised * (1.0 / amount)).astype(BF)
            total = total + dot(probs, jnp.where(key_mine, values, 0))
            logs = jnp.where(lanes == pair * 2 + side, top + jnp.log(amount), logs)
        outs.append(total.astype(BF))
    return jnp.concatenate(outs, axis=1), jnp.transpose(logs)[:8]


def attend_half(ends, tags, q_ref, k_ref, v_ref, side, out, logs):
    block = out.shape[0] // 2

    def turn(index, start, wide):
        spot = pl.multiple_of((index - side * 2) * block, block)
        mixed, rows = attend_block(ends, tags, q_ref, k_ref, v_ref, index, block, start, wide)
        out[pl.ds(spot, block), :] = mixed
        logs[:, pl.ds(spot, block)] = rows

    for_windows(ends, block, side * 2, side * 2 + 2, turn)


def fill_tags(ends, x, del_own, del_other, tags):
    half = del_own.shape[1]
    for index, part in enumerate(tag_row(ends, x, del_own, del_other)):
        tags[0:1, index * half : (index + 1) * half] = part


def attend_kernel(
    place, lens, del_own, del_other, st_own, st_other, a0, a1, a2, a3,
    q_out, k_out, v_out, mixed, logs, small_out,
    store, rows, tags, sems, row_sems,
):
    x = place[3]
    copies = blocks_in(place, (a0, a1, a2, a3), store, sems, PAIR_FLIPS)
    for copy in copies:
        copy.start()
    own_copy = pltpu.make_async_copy(st_own, rows.at[x], row_sems.at[0])
    other_copy = pltpu.make_async_copy(st_other, rows.at[1 - x], row_sems.at[1])
    own_copy.start()
    other_copy.start()
    ends = crop_ends_of(lens)
    half = del_own.shape[1]
    fill_tags(ends, x, del_own, del_other, tags)
    for copy in copies:
        copy.wait()
    own_copy.wait()
    other_copy.wait()

    depth = store.shape[2] // 3
    small_out[...] = jnp.sum(store[:, 48:, :768].astype(F32), axis=0)
    split = pl.multiple_of(x * depth, depth)
    bias_q = small_out[0:1, pl.ds(split, depth)]
    bias_v = small_out[1:2, pl.ds(split, depth)]
    weight = store[:, :48, :].reshape(768, 3 * depth)

    def project(index, carry):
        begin = pl.multiple_of(index * half, half)
        product_ = dot(rows[index], weight)
        for pair in range(depth // 128):
            columns = slice(pair * 128, pair * 128 + 128)
            at = pair * 384
            q_out[pl.ds(begin, half), columns] = (
                product_[:, at : at + 128] + bias_q[:, columns]
            ).astype(BF)
            k_out[pl.ds(begin, half), columns] = product_[:, at + 128 : at + 256].astype(BF)
            v_out[pl.ds(begin, half), columns] = (
                product_[:, at + 256 : at + 384] + bias_v[:, columns]
            ).astype(BF)
        return carry

    lax.fori_loop(0, 2, project, 0)
    attend_half(ends, tags, q_out, k_out, v_out, 1 - x, mixed, logs)


def attend_own_kernel(place, lens, del_own, del_other, q_in, k_in, v_in, mixed, logs, tags):
    x = place[3]
    ends = crop_ends_of(lens)
    fill_tags(ends, x, del_own, del_other, tags)
    attend_half(ends, tags, q_in, k_in, v_in, x, mixed, logs)


def norm_parts(values):
    centered = values - jnp.mean(values, axis=-1, keepdims=True)
    spread = jnp.mean(centered * centered, axis=-1, keepdims=True)
    scale = lax.rsqrt(spread + 1e-06)
    return centered * scale, scale


def norm_back(grad, gain, unit, scale):
    lifted = grad * gain
    return scale * (
        lifted
        - jnp.mean(lifted, axis=-1, keepdims=True)
        - unit * jnp.mean(lifted * unit, axis=-1, keepdims=True)
    )


def gelu_parts(inner):
    phi = 0.5 * (1.0 + lax.erf(inner * 0.7071067811865476))
    density = jnp.exp(inner * inner * -0.5) * 0.3989422804014327
    return inner * phi, phi + inner * density


def feed_kernel(
    place, lens, del_own, del_other, states, mix_own, mix_other, small, cot, pool_cot,
    p0, p1, p2, p3, r0, r1, r2, r3, f0, f1, f2, f3,
    output, pooled, residual_out, mg_own, mg_other, small_out, active, inner_low, low, outer_low, branch_low,
    w1, w2, slope, unit_a, scale_a, outer, grad, acts, inners, sems1, sems2, sems_o,
):
    x = place[3]
    width = states.shape[1]
    count = states.shape[0]
    hidden = 4 * width
    part = width
    flat = p0.shape[2]
    in1 = blocks_in(place, (p0, p1, p2, p3), w1.at[:, :, :flat], sems1, PAIR_FLIPS)
    in1 += blocks_in(place, (r0, r1, r2, r3), w1.at[:, :, flat:], sems1, PAIR_FLIPS, 16)
    in2 = blocks_in(place, (f0, f1, f2, f3), w2, sems2, FULL_FLIPS)
    for copy in in1 + in2:
        copy.start()
    ends = crop_ends_of(lens)
    tags = tag_row(ends, x, del_own, del_other)
    slots = lax.broadcasted_iota(jnp.int32, (len(ends), count), 0)
    members = [(tag == slots).astype(F32) for tag in tags]
    counts = sum(jnp.sum(member, axis=1, keepdims=True) for member in members)
    divisor = jnp.maximum(counts, 1.0)
    member = jnp.where(x == 0, members[0], members[1])
    for copy in in1:
        copy.wait()

    def out_weight(side):
        return w1[pl.ds(side * 8, 8), :, :width].reshape(width // 2, width)

    branch = dot(mix_own[...], out_weight(x)) + dot(mix_other[...], out_weight(1 - x))
    branch = branch + small[2:3, :]
    unit, scale = norm_parts(states[...].astype(F32) + branch)
    unit_a[...] = unit
    scale_a[...] = scale
    value = unit * small[3:4, :] + small[4:5, :]
    low[...] = value.astype(BF)
    outer[...] = value + small[5:6, :]
    for copy in in2:
        copy.wait()

    def leave(here, there, index, sem):
        return pltpu.make_async_copy(here.at[index], there.at[index], sems_o.at[sem])

    def ahead(index, carry):
        begin = pl.multiple_of(index * part, part)
        weight = w1[:, :, pl.ds(width + begin, part)].reshape(width, part)
        inner = dot(low[...], weight) + small[pl.ds(8 + index, 1), :]
        act, bend = gelu_parts(inner)
        act = act.astype(BF)
        acts[index] = act
        leave(acts, active, index, index).start()
        slope[index] = bend
        outer[...] += dot(act, w2[pl.ds(index * 8, 8)].reshape(part, width))
        return carry

    lax.fori_loop(0, hidden // part, ahead, 0)

    unit, scale = norm_parts(outer[...])
    result = unit * small[6:7, :] + small[7:8, :]
    output[...] = result.astype(BF)
    pooled[...] = exact_dot(member, result) / divisor
    grad_in = cot[...].astype(F32) + exact_dot(member, pool_cot[...] / divisor, 0, 0)
    small_out[0:2, :] = jnp.zeros((2, width), F32)
    small_out[12:16, :] = jnp.zeros((4, width), F32)
    small_out[6:7, :] = jnp.sum(grad_in * unit, axis=0, keepdims=True)
    small_out[7:8, :] = jnp.sum(grad_in, axis=0, keepdims=True)
    total = norm_back(grad_in, small[6:7, :], unit, scale)
    grad[...] = total
    outer_low[...] = total.astype(BF)
    small_out[5:6, :] = jnp.sum(outer_low[...].astype(F32), axis=0, keepdims=True)

    def back(index, carry):
        begin = pl.multiple_of(index * part, part)
        weight = w2[pl.ds(index * 8, 8)].reshape(part, width)
        inner = (dot(outer_low[...], weight, 1, 1) * slope[index]).astype(BF)
        inners[index] = inner
        leave(inners, inner_low, index, hidden // part + index).start()
        small_out[pl.ds(8 + index, 1), :] = jnp.sum(inner.astype(F32), axis=0, keepdims=True)
        weight = w1[:, :, pl.ds(width + begin, part)].reshape(width, part)
        grad[...] += dot(inner, weight, 1, 1)
        return carry

    lax.fori_loop(0, hidden // part, back, 0)

    total = grad[...]
    unit = unit_a[...]
    small_out[3:4, :] = jnp.sum(total * unit, axis=0, keepdims=True)
    small_out[4:5, :] = jnp.sum(total, axis=0, keepdims=True)
    residual = norm_back(total, small[3:4, :], unit, scale_a[...])
    residual_out[...] = residual
    branch_low[...] = residual.astype(BF)
    small_out[2:3, :] = jnp.sum(branch_low[...].astype(F32), axis=0, keepdims=True)
    mg_own[...] = dot(branch_low[...], out_weight(x), 1, 1).astype(BF)
    mg_other[...] = dot(branch_low[...], out_weight(1 - x), 1, 1).astype(BF)
    for index in range(hidden // part):
        leave(acts, active, index, index).wait()
        leave(inners, inner_low, index, hidden // part + index).wait()


def outer_sum_kernel(place, active, outer_low, ka, kb, sa, sb, store, sems):
    step = pl.program_id(0)
    width = outer_low.shape[1]
    product_ = dot(active[0], outer_low[...], 0, 0).astype(BF)
    store[pl.ds(step * 8, 8)] = product_.reshape(8, width // 8, width)
    slot = lax.bitwise_xor(step, place[0])
    refs = (ka, kb, sa, sb)

    def copy(part, flip_y, spot, at, sem):
        return pltpu.make_async_copy(store.at[spot], refs[part].at[flip_y * 4 + at], sems.at[sem])

    for part in range(4):
        for flip_y in range(2):
            y = xor(place[1], flip_y)
            c = xor(place[2], part // 2)
            x = xor(place[3], part % 2)
            spot = ((step * 2 + y) * 2 + c) * 2 + x
            copy(part, flip_y, spot, slot, step * 8 + part * 2 + flip_y).start()

    @pl.when(step == 3)
    def _():
        for index in range(32):
            copy(0, 0, index, 0, index).wait()


def inner_sum_kernel(
    place, low, inner_low, branch_low, mix_own, mix_other, small,
    ka, kb, sa, sb, la, lb, ta, tb, store, low_t, rows, sems,
):
    x = place[3]
    width = low.shape[1]
    copies = []

    def send(chunk):
        begin = chunk * width
        refs = (ka, kb, sa, sb)
        into = begin
        end = begin + width if chunk < inner_low.shape[0] else store.shape[2]
        if begin >= ka.shape[2]:
            refs = (la, lb, ta, tb)
            into = begin - ka.shape[2]
        for part, flip in enumerate(PAIR_FLIPS):
            for slot in range(4):
                spot = slot_place(place, flip, slot)
                copy = pltpu.make_async_copy(
                    store.at[spot, :, begin:end],
                    refs[part].at[slot, :, into : into + end - begin],
                    sems.at[chunk * 16 + part * 4 + slot],
                )
                copy.start()
                copies.append(copy)

    rows[...] = jnp.zeros(rows.shape, F32)
    for vector in range(12):
        for third in range(3):
            row = vector * 3 + third
            rows[row : row + 1, :] = small[vector : vector + 1, third * 256 : third * 256 + 256]
    store[:, :, 5 * width :] = jnp.broadcast_to(rows[...].astype(BF)[None], (16, 48, 256))
    low_t[...] = jnp.transpose(low[...])
    for side, mix in ((x, mix_own), (1 - x, mix_other)):
        product_ = dot(mix[...], branch_low[...], 0, 0).astype(BF)
        store[pl.ds(side * 8, 8), :, :width] = product_.reshape(8, width // 16, width)
    send(0)
    for index in range(inner_low.shape[0]):
        begin = (1 + index) * width
        product_ = dot(low_t[...], inner_low[index]).astype(BF)
        store[:, :, begin : begin + width] = product_.reshape(16, width // 16, width)
        send(1 + index)
    for copy in copies:
        copy.wait()


def blocks_out(place, parts, store, sems, flips, first):
    copies = []
    for part, (ref, offset) in enumerate(zip(parts, flips, strict=True)):
        for slot in range(ref.shape[0]):
            spot = slot_place(place, offset, slot)
            copies.append(
                pltpu.make_async_copy(
                    store.at[spot], ref.at[slot], sems.at[first + part * ref.shape[0] + slot]
                )
            )
    return copies


def retreat_kernel(
    place, lens, del_own, del_other, q_in, k_in, v_in, mg_own, mg_other, mix_own, mix_other,
    log_own, log_other, low, tags, dk, dv, *, pair,
):
    x = place[3]
    ends = crop_ends_of(lens)
    half = del_own.shape[1]

    for index, part in enumerate(tag_row(ends, x, del_own, del_other)):
        tall = jnp.transpose(jnp.broadcast_to(part.astype(F32), (8, half)))
        tags[index * half : (index + 1) * half, :] = tall[:, :1]
    dk[...] = jnp.zeros_like(dk)
    dv[...] = jnp.zeros_like(dv)
    block = half // 2
    lane_low = lax.broadcasted_iota(jnp.int32, (block, 128), 1) < 64
    heads = lax.div(lax.broadcasted_iota(jnp.int32, (8, 128), 1), 64)
    picks = (heads == lax.broadcasted_iota(jnp.int32, (8, 128), 0)).astype(F32)
    eighth = jnp.asarray(0.125, BF)

    def turn(index, start, wide):
        wide = wide * block
        key_low = lax.broadcasted_iota(jnp.int32, (wide, 128), 1) < 64
        begin = pl.multiple_of(index * block, block)
        spot = pl.multiple_of(lax.rem(index, 2) * block, block)
        places = begin + lax.broadcasted_iota(jnp.int32, (1, block), 1)
        key_places = start + lax.broadcasted_iota(jnp.int32, (wide, 1), 0)
        allowed = (tags[pl.ds(start, wide), :] == segment_of(ends, places).astype(F32)) | (
            key_places == places
        )
        bias = jnp.where(allowed, 0.0, -1e30)
        queries = q_in[pl.ds(begin, block), :] * eighth
        keys = k_in[pl.ds(start, wide), :]
        values = v_in[pl.ds(start, wide), :]
        near = lax.div(index, 2) == x
        rows = pl.ds(spot, block)
        grads = jnp.where(near, mg_own[rows, :], mg_other[rows, :])
        mixed = jnp.where(near, mix_own[rows, :], mix_other[rows, :])
        deltas = exact_dot(picks, grads.astype(F32) * mixed.astype(F32), 1, 1)
        q_total = jnp.zeros((block, 128), F32)
        k_total = jnp.zeros((wide, 128), F32)
        v_total = jnp.zeros((wide, 128), F32)
        for side in range(2):
            mine = lane_low if side == 0 else ~lane_low
            key_mine = key_low if side == 0 else ~key_low
            q_mine = jnp.where(mine, queries, 0)
            g_mine = jnp.where(mine, grads, 0)
            row = slice(pair * 2 + side, pair * 2 + side + 1)
            log = jnp.where(near, log_own[row, rows], log_other[row, rows])
            probs = jnp.exp(dot(keys, q_mine, 1, 1) + (bias - log))
            prob_grad = dot(values, g_mine, 1, 1) - deltas[side : side + 1, :]
            score_grad = (probs * prob_grad).astype(BF)
            v_total = v_total + dot(probs.astype(BF), g_mine)
            k_total = k_total + dot(score_grad, q_mine)
            q_total = q_total + dot(score_grad, jnp.where(key_mine, keys * eighth, 0), 0, 0)
        low[pl.ds(begin, block), :128] = q_total.astype(BF)
        dk[pl.ds(start, wide), :] += k_total
        dv[pl.ds(start, wide), :] += v_total

    for_windows(ends, block, jnp.int32(0), jnp.int32(4), turn)
    low[:, 128:256] = dk[...].astype(BF)
    low[:, 256:] = dv[...].astype(BF)


def project_sum_kernel(
    place, st_own, st_other, low0, low1, low2, ka, kb, sa, sb, rows, store, rows_t, row_sems, sems
):
    x = place[3]
    row_copies = [
        pltpu.make_async_copy(st_own, rows.at[x], row_sems.at[0]),
        pltpu.make_async_copy(st_other, rows.at[1 - x], row_sems.at[1]),
    ]
    for copy in row_copies:
        copy.start()
    lows = (low0, low1, low2)
    wide = low0.shape[1]
    lane_rows = lax.broadcasted_iota(jnp.int32, (24, 128), 0)
    extra = jnp.zeros((24, 128), F32)
    for index, low in enumerate(lows):
        for kind in range(2):
            begin = kind * 256
            sums = jnp.sum(low[:, begin : begin + 128].astype(F32), axis=0, keepdims=True)
            extra = jnp.where(lane_rows == kind * 3 + index, sums, extra)
    extra = jnp.concatenate([extra, extra], axis=0).astype(BF)
    store[:, :, 3 * wide :] = jnp.broadcast_to(extra[None], (16, 48, 128))
    for copy in row_copies:
        copy.wait()
    rows_t[...] = jnp.transpose(rows[...].reshape(2 * st_own.shape[0], st_own.shape[1]))
    for index, low in enumerate(lows):
        columns = slice(index * wide, (index + 1) * wide)
        store[:, :, columns] = dot(rows_t[...], low[...]).astype(BF).reshape(16, 48, wide)
    copies = blocks_out(place, (ka, kb, sa, sb), store, sems, PAIR_FLIPS, 0)
    for copy in copies:
        copy.start()
    for copy in copies:
        copy.wait()


def states_sum_kernel(
    place, low0, low1, low2, residual, a0, a1, a2, a3, states_out, states_send, store, sems
):
    x = place[3]
    copies = blocks_in(place, (a0, a1, a2, a3), store, sems, PAIR_FLIPS)
    for copy in copies:
        copy.start()
    for copy in copies:
        copy.wait()
    half = residual.shape[0]
    wide = low0.shape[1]
    weight = store[:, :48, :].reshape(768, 3 * wide)

    def share(side):
        begin = pl.multiple_of(side * half, half)
        low = jnp.concatenate([ref[pl.ds(begin, half), :] for ref in (low0, low1, low2)], axis=1)
        return dot(low, weight, 1, 1)

    states_send[...] = share(1 - x).astype(BF)
    states_out[...] = residual[...] + share(x)


def swap(value, axis):
    return lax.ppermute(value, axis, [(0, 1), (1, 0)])


def hop(value, planes, bits):
    return lax.ppermute(value, DP, [(i, i ^ bits) for i in range(planes)])


def add32(*terms):
    return sum((term.astype(F32) for term in terms[1:]), terms[0].astype(F32))


def add(*terms):
    return add32(*terms).astype(BF)


def here():
    dp, c, x = lax.axis_index(DP), lax.axis_index(FSDP), lax.axis_index(SEQ)
    return lax.div(dp, 2), lax.rem(dp, 2), c, x, (dp * 2 + c) * 2 + x


def call(kernel, outs, inputs, specs, scratch, name, grid=()):
    return pl.pallas_call(
        lambda *refs: kernel(here(), *refs),
        out_shape=[jax.ShapeDtypeStruct(shape, kind) for shape, kind, _ in outs],
        in_specs=[spec_of(key) for key in specs],
        out_specs=[spec_of(key) for _, _, key in outs],
        scratch_shapes=scratch,
        grid=grid,
        compiler_params=pltpu.CompilerParams(vmem_limit_bytes=60 * MIB),
        cost_estimate=pl.CostEstimate(flops=0, bytes_accessed=0, transcendentals=0),
        name=name,
    )(*inputs)


def spec_of(key):
    return pl.BlockSpec(memory_space=SPACES[key]) if isinstance(key, str) else key


SPACES = {"s": pltpu.SMEM, "v": pltpu.VMEM, "a": pl.ANY}


def after(value, *others):
    return lax.optimization_barrier((value,) + others)[0]


class Order:
    def __init__(self, last):
        self.last = last

    def take(self, *values):
        values = lax.optimization_barrier(values + (self.last,))[:-1]
        return values if len(values) > 1 else values[0]

    def step(self, value):
        self.last = value
        return value


def column(rows, index):
    return pl.BlockSpec((rows, 128), lambda step: (0, index))


def halves_body(
    states, deleted, crop_lengths,
    query_weight, query_bias, key_weight, value_weight, value_bias, output_weight, output_bias,
    attn_gain, attn_shift, inner_weight, inner_bias, outer_weight, outer_bias, final_gain,
    final_shift, cotangent, pool_cotangent,
):
    planes = 8
    count, width = states.shape[1:]
    half = width // 2
    hidden = inner_weight.shape[1]
    part = query_weight.shape[0]
    long = outer_weight.shape[0]
    crops = crop_lengths.shape[1]
    tall = 3 * half
    flat = width + hidden // 2
    dma = pltpu.SemaphoreType.DMA
    dp, c, x = lax.axis_index(DP), lax.axis_index(FSDP), lax.axis_index(SEQ)
    device = (dp * 2 + c) * 2 + x
    lens = crop_lengths[0]
    own = states[0]

    vectors = [
        vector[None]
        for vector in (
            query_bias, value_bias, output_bias, attn_gain, attn_shift, outer_bias, final_gain,
            final_shift, inner_bias,
        )
    ]
    send, keep, small, p1, p2 = call(
        pack_kernel,
        [
            ((part, tall + width + hidden), BF, "v"),
            ((part, tall), BF, "v"),
            ((16, width), BF, "v"),
            ((part, width + hidden), BF, "v"),
            ((long, width), BF, "v"),
        ],
        (query_weight, key_weight, value_weight, output_weight, inner_weight, outer_weight, *vectors),
        "v" * 15,
        [],
        "pack",
    )

    def pair_up(mine, theirs):
        return jnp.where(
            x == 0,
            jnp.concatenate([mine, theirs], axis=0),
            jnp.concatenate([theirs, mine], axis=0),
        )

    def along_z(block):
        return tuple(hop(block, planes, bits) for bits in (2, 4, 6))

    order = Order(p2)
    sent_2 = along_z(p2)
    del_other, from_x, small_x = order.take(swap(deleted, SEQ), swap(send, SEQ), swap(small, SEQ))
    tail = jnp.pad(add(small, small_x), ((0, 0), (0, tall - width)))
    both_a = jnp.concatenate([pair_up(keep, from_x[:, :tall]), tail], axis=0)
    both_1 = pair_up(p1[:, :flat], from_x[:, tall : tall + flat])
    both_b = pair_up(p1[:, flat:], from_x[:, tall + flat :])
    order.step(both_a)
    sent_a = along_z(both_a)
    order.step(both_b)
    other = swap(order.take(own), SEQ)
    quad_2 = order.step(jnp.stack([p2, *order.take(*sent_2)]))
    octet = hop(quad_2, planes, 1)
    quad_a = order.step(jnp.stack([both_a, *order.take(*sent_a)]))
    quad_ay = hop(quad_a, planes, 1)
    sent_1 = along_z(order.take(both_1))
    octet = order.step(jnp.concatenate([quad_2, order.take(octet)], axis=0))
    octet_x = swap(octet, SEQ)
    quad_ay, other = order.take(quad_ay, other)
    order.step(quad_ay)
    quad_1 = order.step(jnp.stack([both_1, *order.take(*sent_1)]))
    parts_a = order.take(swap(quad_a, FSDP), swap(quad_ay, FSDP))
    parts_a = (quad_a, quad_ay) + parts_a
    order.step(parts_a[-1])
    quad_1y = hop(quad_1, planes, 1)
    sent_b = along_z(after(both_b, quad_1))

    marks = (lens, deleted, del_other)
    queries, keys, values, mix_send, log_other, small = call(
        attend_kernel,
        [((2 * count, half), BF, "v")] * 3
        + [((count, half), BF, "v"), ((8, count), F32, "v"), ((16, width), F32, "v")],
        marks + (order.take(own), other) + parts_a,
        "svvaaaaaa",
        [
            pltpu.VMEM((16, 64, tall), BF),
            pltpu.VMEM((2, count, width), BF),
            pltpu.VMEM((1, 2 * count), jnp.int32),
            dma((16,)),
            dma((2,)),
        ],
        "attend",
    )
    order.step(mix_send)
    mix_other = swap(mix_send, SEQ)
    quad_1y = order.step(order.take(quad_1y))
    quad_b = order.step(jnp.stack([both_b, *order.take(*sent_b)]))
    quad_by = hop(quad_b, planes, 1)
    mix_own, log_own = call(
        attend_own_kernel,
        [((count, half), BF, "v"), ((8, count), F32, "v")],
        marks + (order.take(queries), keys, values),
        "svvvvv",
        [pltpu.VMEM((1, 2 * count), jnp.int32)],
        "attend_own",
    )
    order.step(mix_own)
    octet_x, mix_other = order.take(octet_x, mix_other)
    order.step(octet_x)
    parts_2 = (octet, octet_x, swap(octet, FSDP), swap(octet_x, FSDP))
    parts_1 = (quad_1, quad_1y, swap(quad_1, FSDP), swap(quad_1y, FSDP))
    quad_by = order.take(quad_by)
    parts_1 += (quad_b, quad_by, swap(quad_b, FSDP), swap(quad_by, FSDP))
    four = ((hidden // width, count, width), BF, "a")
    tokens = ((count, width), BF, "v")
    (
        output, pooled, residual, mg_own, mg_send, small_grad,
        active, inner_low, low, outer_low, branch_low,
    ) = call(
        feed_kernel,
        [
            tokens,
            ((crops, width), F32, "v"),
            ((count, width), F32, "v"),
            ((count, half), BF, "v"),
            ((count, half), BF, "v"),
            ((16, width), F32, "v"),
            four, four, tokens, tokens, tokens,
        ],
        marks
        + (own, mix_own, mix_other, small, cotangent[0], pool_cotangent[0])
        + parts_1
        + parts_2,
        "svvvvvvvv" + "a" * 12,
        [
            pltpu.VMEM((16, 2 * part, width + hidden), BF),
            pltpu.VMEM((32, long, width), BF),
            pltpu.VMEM((hidden // width, count, width), F32),
            pltpu.VMEM((count, width), F32),
            pltpu.VMEM((count, 1), F32),
            pltpu.VMEM((count, width), F32),
            pltpu.VMEM((count, width), F32),
            pltpu.VMEM((hidden // width, count, width), BF),
            pltpu.VMEM((hidden // width, count, width), BF),
            dma((32,)),
            dma((32,)),
            dma((2 * hidden // width,)),
        ],
        "feed",
    )
    mg_other = swap(mg_send, SEQ)

    blocks_2 = ((8, long, width), BF, "a")
    keep_2a, keep_2b, send_2a, send_2b = call(
        outer_sum_kernel,
        [blocks_2] * 4,
        (active, outer_low),
        [pl.BlockSpec((1, count, width), lambda step: (step, 0, 0)), "v"],
        [pltpu.VMEM((32, long, width), BF), dma((32,))],
        "outer_sum",
        (hidden // width,),
    )
    order.step(send_2b)
    mg_other = order.step(order.take(mg_other))
    core_2b = swap(order.take(send_2b), FSDP)
    blocks_a = ((4, 2 * part, flat), BF, "a")
    blocks_b = ((4, 2 * part, width + hidden - flat + 256), BF, "a")
    keep_1a, keep_1b, send_1a, send_1b, keep_3a, keep_3b, send_3a, send_3b = call(
        inner_sum_kernel,
        [blocks_a] * 4 + [blocks_b] * 4,
        (order.take(low), inner_low, branch_low, mix_own, mix_other, small_grad),
        "vvvvvv",
        [
            pltpu.VMEM((16, 2 * part, width + hidden + 256), BF),
            pltpu.VMEM((width, count), BF),
            pltpu.VMEM((2 * part, 256), F32),
            dma((80,)),
        ],
        "inner_sum",
    )
    order.step(send_1b)
    t1_2 = order.step(add(keep_2b, order.take(core_2b)))
    sum_2x = swap(t1_2, SEQ)
    t1_1 = order.step(add(keep_1b, order.take(swap(send_1b, FSDP))))
    sum_1y = hop(t1_1, planes, 1)
    t1_3 = order.step(add(keep_3b, order.take(swap(send_3b, FSDP))))
    sum_3y = hop(t1_3, planes, 1)
    core_2, core_1, core_3 = (
        swap(value, FSDP) for value in order.take(send_2a, send_1a, send_3a)
    )

    def retreat(pair):
        specs = ["s", "v", "v"] + [column(2 * count, pair)] * 3 + [column(count, pair)] * 4
        (result,) = call(
            partial(retreat_kernel, pair=pair),
            [((2 * count, 384), BF, "v")],
            marks
            + (order.take(queries), keys, values)
            + (mg_own, mg_other, mix_own, mix_send, log_own, log_other),
            specs + ["v", "v"],
            [
                pltpu.VMEM((2 * count, 1), F32),
                pltpu.VMEM((2 * count, 128), F32),
                pltpu.VMEM((2 * count, 128), F32),
            ],
            "retreat",
            (1,),
        )
        return order.step(result)

    def split_x(v):
        v = v.reshape((2, part) + v.shape[1:])
        return jnp.where(x == 0, v[0], v[1]), jnp.where(x == 0, v[1], v[0])

    def to_z(u):
        return tuple(hop(u[index], planes, 2 * index) for index in (1, 2, 3))

    lows = [retreat(0), retreat(1)]
    u_1 = add(keep_1a, *order.take(core_1, sum_1y))
    order.step(u_1)
    sum_1z = to_z(u_1)
    lows.append(retreat(2))
    u_2 = order.step(add(keep_2a, *order.take(core_2, sum_2x)))
    sum_2y = hop(u_2[4:], planes, 1)
    wide = tall + 128
    keep_a, keep_b, send_a, send_b = call(
        project_sum_kernel,
        [((4, 2 * part, wide), BF, "a")] * 4,
        (order.take(own), other, *lows),
        "aavvv",
        [
            pltpu.VMEM((2, count, width), BF),
            pltpu.VMEM((16, 2 * part, wide), BF),
            pltpu.VMEM((width, 2 * count), BF),
            dma((2,)),
            dma((16,)),
        ],
        "project_sum",
    )
    order.step(send_b)
    core_b, core_a = swap(send_b, FSDP), swap(send_a, FSDP)
    u_3 = add(keep_3a, *order.take(core_3, sum_3y))
    order.step(u_3)
    sum_3z = to_z(u_3)
    t1_a = order.step(add(keep_b, order.take(core_b)))
    sum_ay = hop(t1_a, planes, 1)
    v_1 = order.step(add(u_1[0], *order.take(*sum_1z)))
    v_2 = add(u_2[:4], order.take(sum_2y))
    order.step(v_2)
    sum_2z = to_z(v_2)
    states_part, states_send = call(
        states_sum_kernel,
        [((count, width), F32, "v"), tokens],
        (order.take(lows[0]), lows[1], lows[2], residual) + parts_a,
        "vvvvaaaa",
        [pltpu.VMEM((16, 64, tall), BF), dma((16,))],
        "states_sum",
    )
    order.step(states_send)
    states_x = swap(states_send, SEQ)
    pooled_x = swap(pooled, SEQ)
    v_3 = order.step(add(u_3[0], *order.take(*sum_3z)))
    grad_outer_weight = order.step(add32(v_2[0], *order.take(*sum_2z)))
    u_a = add(keep_a, *order.take(core_a, sum_ay))
    order.step(u_a)
    sum_az = to_z(u_a)
    small = v_3[:, width + hidden - flat :]
    small = jnp.concatenate([small[:part], small[part:]], axis=1)
    mine_1, theirs_1 = split_x(
        jnp.concatenate([v_1, v_3[:, : width + hidden - flat]], axis=1)
    )
    sent_1x = swap(jnp.concatenate([theirs_1, small], axis=1), SEQ)
    v = order.step(add(u_a[0], *order.take(*sum_az)))
    mine_a, theirs_a = split_x(v)
    sent_ax = swap(theirs_a, SEQ)
    states_grad = order.step(add32(states_part, order.take(states_x)))
    pooled = pooled + order.take(pooled_x)
    sent_1x = order.take(sent_1x)
    total = mine_1.astype(F32) + sent_1x[:, : width + hidden].astype(F32)
    grad_output_weight, grad_inner_weight = total[:, :width], total[:, width:]
    small = small.astype(F32) + sent_1x[:, width + hidden :].astype(F32)
    small = jnp.concatenate([small[:, :256], small[:, 256:]], axis=0)
    smalls = small[:36].reshape(12, width)
    theirs = order.take(sent_ax)
    left = jnp.where(x == 0, mine_a, theirs).astype(F32)
    right = jnp.where(x == 0, theirs, mine_a).astype(F32)

    def gathered(index):
        columns = [
            side[:, (pair * 3 + index) * 128 : (pair * 3 + index + 1) * 128]
            for side in (left, right)
            for pair in range(half // 128)
        ]
        return jnp.concatenate(columns, axis=1)

    grad_query_weight, grad_key_weight, grad_value_weight = (gathered(i) for i in range(3))
    bias_grads = jnp.stack([left[:6, tall:], right[:6, tall:]]).reshape(2, 2, half)
    bias_grads = jnp.transpose(bias_grads, (1, 0, 2)).reshape(2, width)
    vectors = lax.dynamic_slice(smalls[:8], (0, device * part), (8, part))
    bias_grads = lax.dynamic_slice(bias_grads, (0, device * part), (2, part))
    grad_inner_bias = lax.dynamic_slice(
        smalls[8:12].reshape(hidden), (device * long,), (long,)
    )
    return (
        output[None],
        pooled[None],
        states_grad[None],
        grad_query_weight,
        bias_grads[0],
        grad_key_weight,
        grad_value_weight,
        bias_grads[1],
        grad_output_weight,
        vectors[2],
        vectors[3],
        vectors[4],
        grad_inner_weight,
        grad_inner_bias,
        grad_outer_weight,
        vectors[5],
        vectors[6],
        vectors[7],
    )


def solution(mesh):
    in_specs = (
        P(ROWS, SEQ, None),
        P(ROWS, SEQ),
        P(ROWS, None),
        BY_ROW,
        FLAT,
        BY_ROW,
        BY_ROW,
        FLAT,
        BY_ROW,
        FLAT,
        FLAT,
        FLAT,
        BY_ROW,
        FLAT,
        BY_ROW,
        FLAT,
        FLAT,
        FLAT,
        P(ROWS, SEQ, None),
        P(ROWS, None, None),
    )
    out_specs = (
        P(ROWS, SEQ, None),
        P(ROWS, None, None),
        P(ROWS, SEQ, None),
        BY_ROW,
        FLAT,
        BY_ROW,
        BY_ROW,
        FLAT,
        BY_ROW,
        FLAT,
        FLAT,
        FLAT,
        BY_ROW,
        FLAT,
        BY_ROW,
        FLAT,
        FLAT,
        FLAT,
    )
    shape = mesh.shape
    halves = (shape[DP], shape[FSDP], shape[SEQ]) == (8, 2, 2)
    chosen = halves_body if halves else body
    return jax.shard_map(chosen, mesh=mesh, in_specs=in_specs, out_specs=out_specs, check_vma=False)
```

```python
from functools import partial

import jax
import jax.numpy as jnp
from jax import lax
from jax.experimental import pallas as pl
from jax.experimental.pallas import tpu as pltpu
from jax.sharding import PartitionSpec as P

HEADS = 12
HEAD = 64


highest = lax.Precision.HIGHEST
DP, FSDP, SEQ = "dp", "fsdp", "seq"
EVERY = (DP, FSDP, SEQ)
BY_ROW, FLAT = P(EVERY, None), P(EVERY)
ROWS = (DP, FSDP)


def layer_norm(values, gain, shift):
    centered = values - jnp.mean(values, axis=-1, keepdims=True)
    spread = jnp.mean(centered * centered, axis=-1, keepdims=True)
    return centered * lax.rsqrt(spread + 1e-06) * gain + shift


def crop_layout(lengths, deleted, places):
    crop_ends = jnp.cumsum(lengths, axis=-1, dtype=jnp.int32)
    segment = jnp.sum(
        (places[..., :, None] >= crop_ends[..., None, :]).astype(jnp.int32),
        axis=-1,
        dtype=jnp.int32,
    )
    retained = (deleted == 0) & (segment < lengths.shape[-1])
    key_tag = jnp.where(retained, segment, -1)
    return (segment, retained, key_tag)


def product(left, right):
    return jnp.dot(left, right, preferred_element_type=jnp.float32)


def column_sum(values):
    return jnp.sum(values.astype(jnp.float32), axis=0)


def sweep(carry, pieces, inner):
    count = pieces[0].shape[1]
    width = 256

    def turn(index, totals):
        offset = index * width
        parts = tuple((lax.dynamic_slice_in_dim(piece, offset, width, 1) for piece in pieces))
        return inner(totals, parts, offset)

    return lax.fori_loop(0, count // width, turn, carry)


def scores_at(query_part, key_part):
    return (
        jnp.einsum("rqhd,rkhd->rhqk", query_part, key_part, preferred_element_type=jnp.float32)
        * 0.125
    )


def allowed_at(query_tag, query_place, tags, begin):
    key_place = begin + jnp.arange(tags.shape[1], dtype=jnp.int32)
    same = tags[:, None, :] == query_tag[:, :, None]
    itself = key_place[None, None, :] == query_place[None, :, None]
    return (same | itself)[:, None]


def probs_at(raw, allowed, log_part):
    return jnp.where(allowed, jnp.exp(raw - log_part[..., None]), 0.0)


def body(
    states,
    deleted,
    crop_lengths,
    query_weight,
    query_bias,
    key_weight,
    value_weight,
    value_bias,
    output_weight,
    output_bias,
    attn_gain,
    attn_shift,
    inner_weight,
    inner_bias,
    outer_weight,
    outer_bias,
    final_gain,
    final_shift,
    cotangent,
    pool_cotangent,
):
    rows, shard, width = states.shape
    lowered = [
        master.astype(jnp.bfloat16)
        for master in (
            query_weight,
            query_bias,
            key_weight,
            value_weight,
            value_bias,
            output_weight,
            output_bias,
            attn_gain,
            attn_shift,
            inner_weight,
            inner_bias,
            outer_weight,
            outer_bias,
            final_gain,
            final_shift,
        )
    ]
    (
        w_query,
        b_query,
        w_key,
        w_value,
        b_value,
        w_out,
        b_out,
        g_attn,
        s_attn,
        w_inner,
        b_inner,
        w_outer,
        b_outer,
        g_final,
        s_final,
    ) = (
        lax.all_gather(lowered[0], EVERY, axis=0, tiled=True),
        lax.all_gather(lowered[1], EVERY, axis=0, tiled=True),
        lax.all_gather(lowered[2], EVERY, axis=0, tiled=True),
        lax.all_gather(lowered[3], EVERY, axis=0, tiled=True),
        lax.all_gather(lowered[4], EVERY, axis=0, tiled=True),
        lax.all_gather(lowered[5], EVERY, axis=0, tiled=True),
        lax.all_gather(lowered[6], EVERY, axis=0, tiled=True),
        lax.all_gather(lowered[7], EVERY, axis=0, tiled=True),
        lax.all_gather(lowered[8], EVERY, axis=0, tiled=True),
        lax.all_gather(lowered[9], EVERY, axis=0, tiled=True),
        lax.all_gather(lowered[10], EVERY, axis=0, tiled=True),
        lax.all_gather(lowered[11], EVERY, axis=0, tiled=True),
        lax.all_gather(lowered[12], EVERY, axis=0, tiled=True),
        lax.all_gather(lowered[13], EVERY, axis=0, tiled=True),
        lax.all_gather(lowered[14], EVERY, axis=0, tiled=True),
    )
    own_start = lax.axis_index(SEQ) * shard
    places = own_start + jnp.arange(shard, dtype=jnp.int32)
    segment, retained, key_tag = crop_layout(crop_lengths, deleted, places)
    flat = states.reshape(rows * shard, width)
    split = (rows, shard, HEADS, HEAD)
    queries = (product(flat, w_query) + b_query).astype(jnp.bfloat16).reshape(split)
    keys = product(flat, w_key).astype(jnp.bfloat16).reshape(split)
    values = (product(flat, w_value) + b_value).astype(jnp.bfloat16).reshape(split)

    def scale_step(totals, parts, begin):
        top, total = totals
        key_part, tags = parts
        allowed = allowed_at(segment, places, tags, begin)
        masked = jnp.where(allowed, scores_at(queries, key_part), -1e30)
        new_top = jnp.maximum(top, jnp.max(masked, axis=-1))
        raised = jnp.where(allowed, jnp.exp(masked - new_top[..., None]), 0.0)
        return (new_top, total * jnp.exp(top - new_top) + jnp.sum(raised, axis=-1))

    stat_shape = (rows, HEADS, shard)
    scale_init = (jnp.full(stat_shape, -1e30, jnp.float32), jnp.zeros(stat_shape, jnp.float32))
    top, total = sweep(
        scale_init,
        (
            lax.all_gather(keys, SEQ, axis=1, tiled=True),
            lax.all_gather(key_tag, SEQ, axis=1, tiled=True),
        ),
        inner=scale_step,
    )
    log_total = top + jnp.log(total)

    def mix_step(totals, parts, begin):
        coarse, fine = totals
        key_part, value_part, tags = parts
        probs = probs_at(
            scores_at(queries, key_part), allowed_at(segment, places, tags, begin), log_total
        )
        probs_low = probs.astype(jnp.bfloat16)
        rest = (probs - probs_low.astype(jnp.float32)).astype(jnp.bfloat16)
        coarse = coarse + jnp.einsum(
            "rhqk,rkhd->rqhd", probs_low, value_part, preferred_element_type=jnp.float32
        )
        fine = fine + jnp.einsum(
            "rhqk,rkhd->rqhd", rest, value_part, preferred_element_type=jnp.float32
        )
        return (coarse, fine)

    empty = jnp.zeros(split, jnp.float32)
    coarse, fine = sweep(
        (empty, empty),
        (
            lax.all_gather(keys, SEQ, axis=1, tiled=True),
            lax.all_gather(values, SEQ, axis=1, tiled=True),
            lax.all_gather(key_tag, SEQ, axis=1, tiled=True),
        ),
        inner=mix_step,
    )
    attended = coarse.astype(jnp.bfloat16).reshape(rows * shard, width)
    branch = product(attended, w_out) + b_out
    residual = states.astype(jnp.float32).reshape(rows * shard, width) + branch
    normed, attn_back = jax.vjp(
        layer_norm, residual, g_attn.astype(jnp.float32), s_attn.astype(jnp.float32)
    )
    normed_low = normed.astype(jnp.bfloat16)
    inner = product(normed_low, w_inner) + b_inner
    active_full, gelu_back = jax.vjp(partial(jax.nn.gelu, approximate=False), inner)
    active = active_full.astype(jnp.bfloat16)
    outer = product(active, w_outer) + b_outer
    result, final_back = jax.vjp(
        layer_norm, normed + outer, g_final.astype(jnp.float32), s_final.astype(jnp.float32)
    )
    output = result.astype(jnp.bfloat16).reshape(rows, shard, width)
    crops = crop_lengths.shape[1]
    member = (
        (segment[..., None] == jnp.arange(crops, dtype=jnp.int32)) & retained[..., None]
    ).astype(jnp.float32)
    partial_sums = jnp.einsum(
        "rnc,rnd->rcd",
        member,
        result.reshape(rows, shard, width),
        precision=highest,
        preferred_element_type=jnp.float32,
    )
    sums, counts = lax.psum((partial_sums, jnp.sum(member, axis=1)), SEQ)
    divisor = jnp.maximum(counts, 1.0)[..., None]
    pooled = sums / divisor
    w_query, w_key, w_value, w_out, w_inner, w_outer = (
        lax.all_gather(lowered[0], EVERY, axis=0, tiled=True),
        lax.all_gather(lowered[2], EVERY, axis=0, tiled=True),
        lax.all_gather(lowered[3], EVERY, axis=0, tiled=True),
        lax.all_gather(lowered[5], EVERY, axis=0, tiled=True),
        lax.all_gather(lowered[9], EVERY, axis=0, tiled=True),
        lax.all_gather(lowered[11], EVERY, axis=0, tiled=True),
    )
    result_grad = cotangent.astype(jnp.float32) + jnp.einsum(
        "rnc,rcd->rnd",
        member,
        pool_cotangent / divisor,
        precision=highest,
        preferred_element_type=jnp.float32,
    )
    sum_grad, grad_final_gain, grad_final_shift = final_back(
        result_grad.reshape(rows * shard, width)
    )
    outer_grad = sum_grad.astype(jnp.bfloat16)
    grad_outer_bias = column_sum(outer_grad)
    grad_outer_weight = product(active.T, outer_grad)
    inner_grad = gelu_back(product(outer_grad, w_outer.T))[0].astype(jnp.bfloat16)
    grad_inner_bias = column_sum(inner_grad)
    grad_inner_weight = product(normed_low.T, inner_grad)
    normed_grad = sum_grad + product(inner_grad, w_inner.T)
    residual_grad, grad_attn_gain, grad_attn_shift = attn_back(normed_grad)
    branch_grad = residual_grad.astype(jnp.bfloat16)
    grad_output_bias = column_sum(branch_grad)
    grad_output_weight = product(attended.T, branch_grad)
    mixed_grad = product(branch_grad, w_out.T).astype(jnp.bfloat16).reshape(split)
    delta = jnp.sum(mixed_grad.astype(jnp.float32) * (coarse + fine), axis=-1)
    delta_local = jnp.transpose(delta, (0, 2, 1))
    all_log, all_delta = (
        lax.all_gather(jnp.transpose(log_total, (0, 2, 1)), SEQ, axis=1, tiled=True),
        lax.all_gather(delta, SEQ, axis=1, tiled=True),
    )

    def key_side(totals, parts, begin):
        key_grad, value_grad = totals
        query_part, grad_part, tags_part = parts
        count = tags_part.shape[1]
        log_part = jnp.transpose(lax.dynamic_slice_in_dim(all_log, begin, count, 1), (0, 2, 1))
        delta_part = jnp.transpose(lax.dynamic_slice_in_dim(all_delta, begin, count, 1), (0, 2, 1))
        query_place = begin + jnp.arange(count, dtype=jnp.int32)
        allowed = allowed_at(tags_part, query_place, key_tag, own_start)
        probs = probs_at(scores_at(query_part, keys), allowed, log_part)
        value_grad = value_grad + jnp.einsum(
            "rhqk,rqhd->rkhd",
            probs.astype(jnp.bfloat16),
            grad_part,
            preferred_element_type=jnp.float32,
        )
        prob_grad = jnp.einsum(
            "rqhd,rkhd->rhqk", grad_part, values, preferred_element_type=jnp.float32
        )
        score_grad = (probs * (prob_grad - delta_part[..., None]) * 0.125).astype(jnp.bfloat16)
        key_grad = key_grad + jnp.einsum(
            "rhqk,rqhd->rkhd", score_grad, query_part, preferred_element_type=jnp.float32
        )
        return (key_grad, value_grad)

    key_grad, value_grad = sweep(
        (empty, empty),
        (
            lax.all_gather(queries, SEQ, axis=1, tiled=True),
            lax.all_gather(mixed_grad, SEQ, axis=1, tiled=True),
            lax.all_gather(segment, SEQ, axis=1, tiled=True),
        ),
        inner=key_side,
    )

    def query_side(query_grad, parts, begin):
        key_part, value_part, tags = parts
        probs = probs_at(
            scores_at(queries, key_part), allowed_at(segment, places, tags, begin), log_total
        )
        prob_grad = jnp.einsum(
            "rqhd,rkhd->rhqk", mixed_grad, value_part, preferred_element_type=jnp.float32
        )
        score_grad = (probs * (prob_grad - delta_local[..., None]) * 0.125).astype(jnp.bfloat16)
        return query_grad + jnp.einsum(
            "rhqk,rkhd->rqhd", score_grad, key_part, preferred_element_type=jnp.float32
        )

    query_grad = sweep(
        empty,
        (
            lax.all_gather(keys, SEQ, axis=1, tiled=True),
            lax.all_gather(values, SEQ, axis=1, tiled=True),
            lax.all_gather(key_tag, SEQ, axis=1, tiled=True),
        ),
        inner=query_side,
    )
    query_low = query_grad.astype(jnp.bfloat16).reshape(rows * shard, width)
    key_low = key_grad.astype(jnp.bfloat16).reshape(rows * shard, width)
    value_low = value_grad.astype(jnp.bfloat16).reshape(rows * shard, width)
    grad_query_weight = product(flat.T, query_low)
    grad_query_bias = column_sum(query_low)
    grad_key_weight = product(flat.T, key_low)
    grad_value_weight = product(flat.T, value_low)
    grad_value_bias = column_sum(value_low)
    states_grad = (
        residual_grad
        + product(query_low, w_query.T)
        + product(key_low, w_key.T)
        + product(value_low, w_value.T)
    ).reshape(rows, shard, width)
    summed = (
        lax.psum_scatter(grad_query_weight, EVERY, scatter_dimension=0, tiled=True),
        lax.psum_scatter(grad_query_bias, EVERY, scatter_dimension=0, tiled=True),
        lax.psum_scatter(grad_key_weight, EVERY, scatter_dimension=0, tiled=True),
        lax.psum_scatter(grad_value_weight, EVERY, scatter_dimension=0, tiled=True),
        lax.psum_scatter(grad_value_bias, EVERY, scatter_dimension=0, tiled=True),
        lax.psum_scatter(
            grad_output_weight, EVERY, scatter_dimension=0, tiled=True
        ),
        lax.psum_scatter(grad_output_bias, EVERY, scatter_dimension=0, tiled=True),
        lax.psum_scatter(grad_attn_gain, EVERY, scatter_dimension=0, tiled=True),
        lax.psum_scatter(grad_attn_shift, EVERY, scatter_dimension=0, tiled=True),
        lax.psum_scatter(grad_inner_weight, EVERY, scatter_dimension=0, tiled=True),
        lax.psum_scatter(grad_inner_bias, EVERY, scatter_dimension=0, tiled=True),
        lax.psum_scatter(grad_outer_weight, EVERY, scatter_dimension=0, tiled=True),
        lax.psum_scatter(grad_outer_bias, EVERY, scatter_dimension=0, tiled=True),
        lax.psum_scatter(grad_final_gain, EVERY, scatter_dimension=0, tiled=True),
        lax.psum_scatter(grad_final_shift, EVERY, scatter_dimension=0, tiled=True),
    )
    return (output, pooled, states_grad) + tuple(summed)


BF = jnp.bfloat16
F32 = jnp.float32
MIB = 1 << 20


def dot(left, right, left_dim=1, right_dim=0):
    return lax.dot_general(
        left,
        right,
        (((left_dim,), (right_dim,)), ((), ())),
        preferred_element_type=F32,
    )


def exact_dot(left, right, left_dim=1, right_dim=0):
    return lax.dot_general(
        left,
        right,
        (((left_dim,), (right_dim,)), ((), ())),
        precision=highest,
        preferred_element_type=F32,
    )


def crop_ends_of(lens_ref):
    ends, total = [], jnp.int32(0)
    for slot in range(lens_ref.shape[0]):
        total = total + lens_ref[slot]
        ends.append(total)
    return ends


def segment_of(ends, places):
    segment = jnp.zeros(places.shape, jnp.int32)
    for end in ends:
        segment = segment + (places >= end).astype(jnp.int32)
    return segment


def for_windows(ends, block, first, last, turn):
    begin = ends[0] * 0
    for end in ends:
        begin = jnp.maximum(begin, jnp.where(end <= 2 * block, end, 0))
    single = (begin < block).astype(jnp.int32)

    def three(index, carry):
        start = jnp.where(index == 2, 1 - single, 0) * block
        turn(index, pl.multiple_of(start, block), 3)
        return carry

    def two(index, carry):
        start = jnp.where(index == 0, 0, 2) * block
        turn(index, pl.multiple_of(start, block), 2)
        return carry

    def one(index, carry):
        turn(index, pl.multiple_of(index * block, block), 1)
        return carry

    low = jnp.maximum(first, 1 - single)
    lax.fori_loop(low, jnp.minimum(last, 3), three, 0)
    lax.fori_loop(first, jnp.where((first == 0) & (single == 0), 1, first), two, 0)
    final = jnp.where(last == 4, 1, 0)
    lax.fori_loop(3, 3 + final * (1 - single), two, 0)
    lax.fori_loop(3, 3 + final * single, one, 0)


def pack_kernel(
    place, wq, wk, wv, wo, w1, w2, v0, v1, v2, v3, v4, v5, v6, v7, v96,
    send, keep, small, p1, p2,
):
    x = place[3]
    device = place[4]
    half = wq.shape[1] // 2
    for pair in range(half // 128):
        for index, ref in enumerate((wq, wk, wv)):
            left = ref[:, pair * 128 : pair * 128 + 128].astype(BF)
            right = ref[:, half + pair * 128 : half + pair * 128 + 128].astype(BF)
            begin = (pair * 3 + index) * 128
            keep[:, begin : begin + 128] = jnp.where(x == 0, left, right)
            send[:, begin : begin + 128] = jnp.where(x == 0, right, left)
    width = wo.shape[1]
    tall = keep.shape[1]
    for ref, begin in ((send, tall), (p1, 0)):
        ref[:, begin : begin + width] = wo[...].astype(BF)
        ref[:, begin + width :] = w1[...].astype(BF)
    p2[...] = w2[...].astype(BF)
    part = v0.shape[1]
    row = lax.broadcasted_iota(jnp.int32, (8, part), 0)
    stacked = jnp.zeros((8, part), F32)
    for index, ref in enumerate((v0, v1, v2, v3, v4, v5, v6, v7)):
        stacked = jnp.where(row == index, ref[...], stacked)
    row = lax.broadcasted_iota(jnp.int32, (part, width), 0)
    lane = lax.broadcasted_iota(jnp.int32, (part, width), 1)
    spread = (row + device * part == lane).astype(BF)
    first = dot(stacked.astype(BF), spread)
    part = v96.shape[1]
    row = lax.broadcasted_iota(jnp.int32, (part, width), 0)
    lane = lax.broadcasted_iota(jnp.int32, (part, width), 1)
    rows = []
    for index in range(8):
        if index < v96.shape[1] * 32 // width:
            spread = (row + device * part == lane + index * width).astype(BF)
            rows.append(dot(jnp.broadcast_to(v96[...], (8, part)).astype(BF), spread))
    tall = lax.broadcasted_iota(jnp.int32, (8, width), 0)
    second = jnp.zeros((8, width), F32)
    for index, value in enumerate(rows):
        second = jnp.where(tall == index, value[:1], second)
    small[...] = jnp.concatenate([first, second], axis=0).astype(BF)


def blocks_in(place, parts, store, sems, flips, first=0):
    copies = []
    for part, (ref, offset) in enumerate(zip(parts, flips, strict=True)):
        for slot in range(ref.shape[0]):
            spot = slot_place(place, offset, slot)
            copies.append(
                pltpu.make_async_copy(
                    ref.at[slot], store.at[spot], sems.at[first + part * ref.shape[0] + slot]
                )
            )
    return copies


def xor(value, bits):
    if bits & 1:
        value = value + 1 - 2 * lax.rem(value, 2)
    if bits & 2:
        value = lax.rem(value + 2, 4)
    return value


def slot_place(place, flip, slot):
    flip_y, flip_c, flip_x = flip
    z = xor(place[0], slot % 4)
    y = xor(place[1], flip_y ^ (slot // 4))
    c = xor(place[2], flip_c)
    spot = (z * 2 + y) * 2 + c
    if flip_x is None:
        return spot
    return spot * 2 + xor(place[3], flip_x)


PAIR_FLIPS = ((0, 0, None), (1, 0, None), (0, 1, None), (1, 1, None))
FULL_FLIPS = ((0, 0, 0), (0, 0, 1), (0, 1, 0), (0, 1, 1))


def tag_row(ends, x, own, other):
    half = own.shape[1]
    parts = []
    for index in range(2):
        deleted = jnp.where(x == index, own[...], other[...])
        places = index * half + lax.broadcasted_iota(jnp.int32, (1, half), 1)
        segment = segment_of(ends, places)
        parts.append(jnp.where((deleted == 0) & (segment < len(ends)), segment, -1))
    return parts


def attend_block(ends, tags, q_ref, k_ref, v_ref, index, block, start, wide):
    wide = wide * block
    lane_low = lax.broadcasted_iota(jnp.int32, (block, 128), 1) < 64
    key_low = lax.broadcasted_iota(jnp.int32, (wide, 128), 1) < 64
    begin = pl.multiple_of(index * block, block)
    places = begin + lax.broadcasted_iota(jnp.int32, (block, 1), 0)
    key_places = start + lax.broadcasted_iota(jnp.int32, (1, wide), 1)
    allowed = (tags[0:1, pl.ds(start, wide)] == segment_of(ends, places)) | (key_places == places)
    bias = jnp.where(allowed, 0.0, -1e30)
    outs = []
    lanes = lax.broadcasted_iota(jnp.int32, (block, 128), 1)
    logs = jnp.zeros((block, 128), F32)
    for pair in range(q_ref.shape[1] // 128):
        columns = slice(pair * 128, pair * 128 + 128)
        queries = q_ref[pl.ds(begin, block), columns] * jnp.asarray(0.125, BF)
        keys = k_ref[pl.ds(start, wide), columns]
        values = v_ref[pl.ds(start, wide), columns]
        total = jnp.zeros((block, 128), F32)
        for side in range(2):
            mine = lane_low if side == 0 else ~lane_low
            key_mine = key_low if side == 0 else ~key_low
            scores = dot(jnp.where(mine, queries, 0), keys, 1, 1) + bias
            top = jnp.max(scores, axis=1, keepdims=True)
            raised = jnp.exp(scores - top)
            amount = jnp.sum(raised, axis=1, keepdims=True)
            probs = (raised * (1.0 / amount)).astype(BF)
            total = total + dot(probs, jnp.where(key_mine, values, 0))
            logs = jnp.where(lanes == pair * 2 + side, top + jnp.log(amount), logs)
        outs.append(total.astype(BF))
    return jnp.concatenate(outs, axis=1), jnp.transpose(logs)[:8]


def attend_half(ends, tags, q_ref, k_ref, v_ref, side, out, logs):
    block = out.shape[0] // 2

    def turn(index, start, wide):
        spot = pl.multiple_of((index - side * 2) * block, block)
        mixed, rows = attend_block(ends, tags, q_ref, k_ref, v_ref, index, block, start, wide)
        out[pl.ds(spot, block), :] = mixed
        logs[:, pl.ds(spot, block)] = rows

    for_windows(ends, block, side * 2, side * 2 + 2, turn)


def fill_tags(ends, x, del_own, del_other, tags):
    half = del_own.shape[1]
    for index, part in enumerate(tag_row(ends, x, del_own, del_other)):
        tags[0:1, index * half : (index + 1) * half] = part


def attend_kernel(
    place, lens, del_own, del_other, st_own, st_other, a0, a1, a2, a3,
    q_out, k_out, v_out, mixed, logs, small_out,
    store, rows, tags, sems, row_sems,
):
    x = place[3]
    copies = blocks_in(place, (a0, a1, a2, a3), store, sems, PAIR_FLIPS)
    for copy in copies:
        copy.start()
    own_copy = pltpu.make_async_copy(st_own, rows.at[x], row_sems.at[0])
    other_copy = pltpu.make_async_copy(st_other, rows.at[1 - x], row_sems.at[1])
    own_copy.start()
    other_copy.start()
    ends = crop_ends_of(lens)
    half = del_own.shape[1]
    fill_tags(ends, x, del_own, del_other, tags)
    for copy in copies:
        copy.wait()
    own_copy.wait()
    other_copy.wait()

    depth = store.shape[2] // 3
    small_out[...] = jnp.sum(store[:, 48:, :768].astype(F32), axis=0)
    split = pl.multiple_of(x * depth, depth)
    bias_q = small_out[0:1, pl.ds(split, depth)]
    bias_v = small_out[1:2, pl.ds(split, depth)]
    weight = store[:, :48, :].reshape(768, 3 * depth)

    def project(index, carry):
        begin = pl.multiple_of(index * half, half)
        product_ = dot(rows[index], weight)
        for pair in range(depth // 128):
            columns = slice(pair * 128, pair * 128 + 128)
            at = pair * 384
            q_out[pl.ds(begin, half), columns] = (
                product_[:, at : at + 128] + bias_q[:, columns]
            ).astype(BF)
            k_out[pl.ds(begin, half), columns] = product_[:, at + 128 : at + 256].astype(BF)
            v_out[pl.ds(begin, half), columns] = (
                product_[:, at + 256 : at + 384] + bias_v[:, columns]
            ).astype(BF)
        return carry

    lax.fori_loop(0, 2, project, 0)
    attend_half(ends, tags, q_out, k_out, v_out, 1 - x, mixed, logs)


def attend_own_kernel(place, lens, del_own, del_other, q_in, k_in, v_in, mixed, logs, tags):
    x = place[3]
    ends = crop_ends_of(lens)
    fill_tags(ends, x, del_own, del_other, tags)
    attend_half(ends, tags, q_in, k_in, v_in, x, mixed, logs)


def norm_parts(values):
    centered = values - jnp.mean(values, axis=-1, keepdims=True)
    spread = jnp.mean(centered * centered, axis=-1, keepdims=True)
    scale = lax.rsqrt(spread + 1e-06)
    return centered * scale, scale


def norm_back(grad, gain, unit, scale):
    lifted = grad * gain
    return scale * (
        lifted
        - jnp.mean(lifted, axis=-1, keepdims=True)
        - unit * jnp.mean(lifted * unit, axis=-1, keepdims=True)
    )


def gelu_parts(inner):
    phi = 0.5 * (1.0 + lax.erf(inner * 0.7071067811865476))
    density = jnp.exp(inner * inner * -0.5) * 0.3989422804014327
    return inner * phi, phi + inner * density


def feed_kernel(
    place, lens, del_own, del_other, states, mix_own, mix_other, small, cot, pool_cot,
    p0, p1, p2, p3, r0, r1, r2, r3, f0, f1, f2, f3,
    output, pooled, residual_out, mg_own, mg_other, small_out, active, inner_low, low, outer_low, branch_low,
    w1, w2, slope, unit_a, scale_a, outer, grad, acts, inners, sems1, sems2, sems_o,
):
    x = place[3]
    width = states.shape[1]
    count = states.shape[0]
    hidden = 4 * width
    part = width
    flat = p0.shape[2]
    in1 = blocks_in(place, (p0, p1, p2, p3), w1.at[:, :, :flat], sems1, PAIR_FLIPS)
    in1 += blocks_in(place, (r0, r1, r2, r3), w1.at[:, :, flat:], sems1, PAIR_FLIPS, 16)
    in2 = blocks_in(place, (f0, f1, f2, f3), w2, sems2, FULL_FLIPS)
    for copy in in1 + in2:
        copy.start()
    ends = crop_ends_of(lens)
    tags = tag_row(ends, x, del_own, del_other)
    slots = lax.broadcasted_iota(jnp.int32, (len(ends), count), 0)
    members = [(tag == slots).astype(F32) for tag in tags]
    counts = sum(jnp.sum(member, axis=1, keepdims=True) for member in members)
    divisor = jnp.maximum(counts, 1.0)
    member = jnp.where(x == 0, members[0], members[1])
    for copy in in1:
        copy.wait()

    def out_weight(side):
        return w1[pl.ds(side * 8, 8), :, :width].reshape(width // 2, width)

    branch = dot(mix_own[...], out_weight(x)) + dot(mix_other[...], out_weight(1 - x))
    branch = branch + small[2:3, :]
    unit, scale = norm_parts(states[...].astype(F32) + branch)
    unit_a[...] = unit
    scale_a[...] = scale
    value = unit * small[3:4, :] + small[4:5, :]
    low[...] = value.astype(BF)
    outer[...] = value + small[5:6, :]
    for copy in in2:
        copy.wait()

    def leave(here, there, index, sem):
        return pltpu.make_async_copy(here.at[index], there.at[index], sems_o.at[sem])

    def ahead(index, carry):
        begin = pl.multiple_of(index * part, part)
        weight = w1[:, :, pl.ds(width + begin, part)].reshape(width, part)
        inner = dot(low[...], weight) + small[pl.ds(8 + index, 1), :]
        act, bend = gelu_parts(inner)
        act = act.astype(BF)
        acts[index] = act
        leave(acts, active, index, index).start()
        slope[index] = bend
        outer[...] += dot(act, w2[pl.ds(index * 8, 8)].reshape(part, width))
        return carry

    lax.fori_loop(0, hidden // part, ahead, 0)

    unit, scale = norm_parts(outer[...])
    result = unit * small[6:7, :] + small[7:8, :]
    output[...] = result.astype(BF)
    pooled[...] = exact_dot(member, result) / divisor
    grad_in = cot[...].astype(F32) + exact_dot(member, pool_cot[...] / divisor, 0, 0)
    small_out[0:2, :] = jnp.zeros((2, width), F32)
    small_out[12:16, :] = jnp.zeros((4, width), F32)
    small_out[6:7, :] = jnp.sum(grad_in * unit, axis=0, keepdims=True)
    small_out[7:8, :] = jnp.sum(grad_in, axis=0, keepdims=True)
    total = norm_back(grad_in, small[6:7, :], unit, scale)
    grad[...] = total
    outer_low[...] = total.astype(BF)
    small_out[5:6, :] = jnp.sum(outer_low[...].astype(F32), axis=0, keepdims=True)

    def back(index, carry):
        begin = pl.multiple_of(index * part, part)
        weight = w2[pl.ds(index * 8, 8)].reshape(part, width)
        inner = (dot(outer_low[...], weight, 1, 1) * slope[index]).astype(BF)
        inners[index] = inner
        leave(inners, inner_low, index, hidden // part + index).start()
        small_out[pl.ds(8 + index, 1), :] = jnp.sum(inner.astype(F32), axis=0, keepdims=True)
        weight = w1[:, :, pl.ds(width + begin, part)].reshape(width, part)
        grad[...] += dot(inner, weight, 1, 1)
        return carry

    lax.fori_loop(0, hidden // part, back, 0)

    total = grad[...]
    unit = unit_a[...]
    small_out[3:4, :] = jnp.sum(total * unit, axis=0, keepdims=True)
    small_out[4:5, :] = jnp.sum(total, axis=0, keepdims=True)
    residual = norm_back(total, small[3:4, :], unit, scale_a[...])
    residual_out[...] = residual
    branch_low[...] = residual.astype(BF)
    small_out[2:3, :] = jnp.sum(branch_low[...].astype(F32), axis=0, keepdims=True)
    mg_own[...] = dot(branch_low[...], out_weight(x), 1, 1).astype(BF)
    mg_other[...] = dot(branch_low[...], out_weight(1 - x), 1, 1).astype(BF)
    for index in range(hidden // part):
        leave(acts, active, index, index).wait()
        leave(inners, inner_low, index, hidden // part + index).wait()


def outer_sum_kernel(place, active, outer_low, ka, kb, sa, sb, store, sems):
    step = pl.program_id(0)
    width = outer_low.shape[1]
    product_ = dot(active[0], outer_low[...], 0, 0).astype(BF)
    store[pl.ds(step * 8, 8)] = product_.reshape(8, width // 8, width)
    slot = lax.bitwise_xor(step, place[0])
    refs = (ka, kb, sa, sb)

    def copy(part, flip_y, spot, at, sem):
        return pltpu.make_async_copy(store.at[spot], refs[part].at[flip_y * 4 + at], sems.at[sem])

    for part in range(4):
        for flip_y in range(2):
            y = xor(place[1], flip_y)
            c = xor(place[2], part // 2)
            x = xor(place[3], part % 2)
            spot = ((step * 2 + y) * 2 + c) * 2 + x
            copy(part, flip_y, spot, slot, step * 8 + part * 2 + flip_y).start()

    @pl.when(step == 3)
    def _():
        for index in range(32):
            copy(0, 0, index, 0, index).wait()


def inner_sum_kernel(
    place, low, inner_low, branch_low, mix_own, mix_other, small,
    ka, kb, sa, sb, la, lb, ta, tb, store, low_t, rows, sems,
):
    x = place[3]
    width = low.shape[1]
    copies = []

    def send(chunk):
        begin = chunk * width
        refs = (ka, kb, sa, sb)
        into = begin
        end = begin + width if chunk < inner_low.shape[0] else store.shape[2]
        if begin >= ka.shape[2]:
            refs = (la, lb, ta, tb)
            into = begin - ka.shape[2]
        for part, flip in enumerate(PAIR_FLIPS):
            for slot in range(4):
                spot = slot_place(place, flip, slot)
                copy = pltpu.make_async_copy(
                    store.at[spot, :, begin:end],
                    refs[part].at[slot, :, into : into + end - begin],
                    sems.at[chunk * 16 + part * 4 + slot],
                )
                copy.start()
                copies.append(copy)

    rows[...] = jnp.zeros(rows.shape, F32)
    for vector in range(12):
        for third in range(3):
            row = vector * 3 + third
            rows[row : row + 1, :] = small[vector : vector + 1, third * 256 : third * 256 + 256]
    store[:, :, 5 * width :] = jnp.broadcast_to(rows[...].astype(BF)[None], (16, 48, 256))
    low_t[...] = jnp.transpose(low[...])
    for side, mix in ((x, mix_own), (1 - x, mix_other)):
        product_ = dot(mix[...], branch_low[...], 0, 0).astype(BF)
        store[pl.ds(side * 8, 8), :, :width] = product_.reshape(8, width // 16, width)
    send(0)
    for index in range(inner_low.shape[0]):
        begin = (1 + index) * width
        product_ = dot(low_t[...], inner_low[index]).astype(BF)
        store[:, :, begin : begin + width] = product_.reshape(16, width // 16, width)
        send(1 + index)
    for copy in copies:
        copy.wait()


def blocks_out(place, parts, store, sems, flips, first):
    copies = []
    for part, (ref, offset) in enumerate(zip(parts, flips, strict=True)):
        for slot in range(ref.shape[0]):
            spot = slot_place(place, offset, slot)
            copies.append(
                pltpu.make_async_copy(
                    store.at[spot], ref.at[slot], sems.at[first + part * ref.shape[0] + slot]
                )
            )
    return copies


def retreat_kernel(
    place, lens, del_own, del_other, q_in, k_in, v_in, mg_own, mg_other, mix_own, mix_other,
    log_own, log_other, low, tags, dk, dv,
):
    x = place[3]
    ends = crop_ends_of(lens)
    half = del_own.shape[1]

    pair = pl.program_id(0)

    @pl.when(pair == 0)
    def _():
        for index, part in enumerate(tag_row(ends, x, del_own, del_other)):
            tall = jnp.transpose(jnp.broadcast_to(part.astype(F32), (8, half)))
            tags[index * half : (index + 1) * half, :] = tall[:, :1]

    dk[...] = jnp.zeros_like(dk)
    dv[...] = jnp.zeros_like(dv)
    block = half // 2
    lane_low = lax.broadcasted_iota(jnp.int32, (block, 128), 1) < 64
    heads = lax.div(lax.broadcasted_iota(jnp.int32, (8, 128), 1), 64)
    picks = (heads == lax.broadcasted_iota(jnp.int32, (8, 128), 0)).astype(F32)
    eighth = jnp.asarray(0.125, BF)

    def turn(index, start, wide):
        wide = wide * block
        key_low = lax.broadcasted_iota(jnp.int32, (wide, 128), 1) < 64
        begin = pl.multiple_of(index * block, block)
        spot = pl.multiple_of(lax.rem(index, 2) * block, block)
        places = begin + lax.broadcasted_iota(jnp.int32, (1, block), 1)
        key_places = start + lax.broadcasted_iota(jnp.int32, (wide, 1), 0)
        allowed = (tags[pl.ds(start, wide), :] == segment_of(ends, places).astype(F32)) | (
            key_places == places
        )
        bias = jnp.where(allowed, 0.0, -1e30)
        queries = q_in[pl.ds(begin, block), :] * eighth
        keys = k_in[pl.ds(start, wide), :]
        values = v_in[pl.ds(start, wide), :]
        near = lax.div(index, 2) == x
        rows = pl.ds(spot, block)
        grads = jnp.where(near, mg_own[rows, :], mg_other[rows, :])
        mixed = jnp.where(near, mix_own[rows, :], mix_other[rows, :])
        deltas = exact_dot(picks, grads.astype(F32) * mixed.astype(F32), 1, 1)
        q_total = jnp.zeros((block, 128), F32)
        k_total = jnp.zeros((wide, 128), F32)
        v_total = jnp.zeros((wide, 128), F32)
        for side in range(2):
            mine = lane_low if side == 0 else ~lane_low
            key_mine = key_low if side == 0 else ~key_low
            q_mine = jnp.where(mine, queries, 0)
            g_mine = jnp.where(mine, grads, 0)
            row = pl.ds(pair * 2 + side, 1)
            log = jnp.where(near, log_own[row, rows], log_other[row, rows])
            probs = jnp.exp(dot(keys, q_mine, 1, 1) + (bias - log))
            prob_grad = dot(values, g_mine, 1, 1) - deltas[side : side + 1, :]
            score_grad = (probs * prob_grad).astype(BF)
            v_total = v_total + dot(probs.astype(BF), g_mine)
            k_total = k_total + dot(score_grad, q_mine)
            q_total = q_total + dot(score_grad, jnp.where(key_mine, keys * eighth, 0), 0, 0)
        low[pl.ds(begin, block), :128] = q_total.astype(BF)
        dk[pl.ds(start, wide), :] += k_total
        dv[pl.ds(start, wide), :] += v_total

    for_windows(ends, block, jnp.int32(0), jnp.int32(4), turn)
    low[:, 128:256] = dk[...].astype(BF)
    low[:, 256:] = dv[...].astype(BF)


def project_sum_kernel(
    place, st_own, st_other, low, ka, kb, sa, sb, rows, store, rows_t, row_sems, sems
):
    x = place[3]
    row_copies = [
        pltpu.make_async_copy(st_own, rows.at[x], row_sems.at[0]),
        pltpu.make_async_copy(st_other, rows.at[1 - x], row_sems.at[1]),
    ]
    for copy in row_copies:
        copy.start()
    wide = low.shape[1] // 3
    lane_rows = lax.broadcasted_iota(jnp.int32, (24, 128), 0)
    extra = jnp.zeros((24, 128), F32)
    for index in range(3):
        for kind in range(2):
            begin = index * wide + kind * 256
            sums = jnp.sum(low[:, begin : begin + 128].astype(F32), axis=0, keepdims=True)
            extra = jnp.where(lane_rows == kind * 3 + index, sums, extra)
    extra = jnp.concatenate([extra, extra], axis=0).astype(BF)
    store[:, :, 3 * wide :] = jnp.broadcast_to(extra[None], (16, 48, 128))
    for copy in row_copies:
        copy.wait()
    rows_t[...] = jnp.transpose(rows[...].reshape(2 * st_own.shape[0], st_own.shape[1]))
    for index in range(3):
        columns = slice(index * wide, (index + 1) * wide)
        store[:, :, columns] = dot(rows_t[...], low[:, columns]).astype(BF).reshape(16, 48, wide)
    copies = blocks_out(place, (ka, kb, sa, sb), store, sems, PAIR_FLIPS, 0)
    for copy in copies:
        copy.start()
    for copy in copies:
        copy.wait()


def states_sum_kernel(
    place, low, residual, a0, a1, a2, a3, states_out, states_send, store, sems
):
    x = place[3]
    copies = blocks_in(place, (a0, a1, a2, a3), store, sems, PAIR_FLIPS)
    for copy in copies:
        copy.start()
    for copy in copies:
        copy.wait()
    half = residual.shape[0]
    weight = store[:, :48, :].reshape(768, low.shape[1])

    def share(side):
        begin = pl.multiple_of(side * half, half)
        return dot(low[pl.ds(begin, half), :], weight, 1, 1)

    states_send[...] = share(1 - x).astype(BF)
    states_out[...] = residual[...] + share(x)


def swap(value, axis):
    return lax.ppermute(value, axis, [(0, 1), (1, 0)])


def hop(value, planes, bits):
    return lax.ppermute(value, DP, [(i, i ^ bits) for i in range(planes)])


def add32(*terms):
    return sum((term.astype(F32) for term in terms[1:]), terms[0].astype(F32))


def add(*terms):
    return add32(*terms).astype(BF)


def here():
    dp, c, x = lax.axis_index(DP), lax.axis_index(FSDP), lax.axis_index(SEQ)
    return lax.div(dp, 2), lax.rem(dp, 2), c, x, (dp * 2 + c) * 2 + x


def call(kernel, outs, inputs, specs, scratch, name, grid=()):
    return pl.pallas_call(
        lambda *refs: kernel(here(), *refs),
        out_shape=[jax.ShapeDtypeStruct(shape, kind) for shape, kind, _ in outs],
        in_specs=[spec_of(key) for key in specs],
        out_specs=[spec_of(key) for _, _, key in outs],
        scratch_shapes=scratch,
        grid=grid,
        compiler_params=pltpu.CompilerParams(vmem_limit_bytes=60 * MIB),
        cost_estimate=pl.CostEstimate(flops=0, bytes_accessed=0, transcendentals=0),
        name=name,
    )(*inputs)


def spec_of(key):
    return pl.BlockSpec(memory_space=SPACES[key]) if isinstance(key, str) else key


SPACES = {"s": pltpu.SMEM, "v": pltpu.VMEM, "a": pl.ANY}


def after(value, *others):
    return lax.optimization_barrier((value,) + others)[0]


class Order:
    def __init__(self, last):
        self.last = last

    def take(self, *values):
        values = lax.optimization_barrier(values + (self.last,))[:-1]
        return values if len(values) > 1 else values[0]

    def step(self, value):
        self.last = value
        return value


def column(rows, wide=128):
    return pl.BlockSpec((rows, wide), lambda step: (0, step))


def halves_body(
    states, deleted, crop_lengths,
    query_weight, query_bias, key_weight, value_weight, value_bias, output_weight, output_bias,
    attn_gain, attn_shift, inner_weight, inner_bias, outer_weight, outer_bias, final_gain,
    final_shift, cotangent, pool_cotangent,
):
    planes = 8
    count, width = states.shape[1:]
    half = width // 2
    hidden = inner_weight.shape[1]
    part = query_weight.shape[0]
    long = outer_weight.shape[0]
    crops = crop_lengths.shape[1]
    tall = 3 * half
    flat = width + hidden // 2
    dma = pltpu.SemaphoreType.DMA
    dp, c, x = lax.axis_index(DP), lax.axis_index(FSDP), lax.axis_index(SEQ)
    device = (dp * 2 + c) * 2 + x
    lens = crop_lengths[0]
    own = states[0]

    vectors = [
        vector[None]
        for vector in (
            query_bias, value_bias, output_bias, attn_gain, attn_shift, outer_bias, final_gain,
            final_shift, inner_bias,
        )
    ]
    send, keep, small, p1, p2 = call(
        pack_kernel,
        [
            ((part, tall + width + hidden), BF, "v"),
            ((part, tall), BF, "v"),
            ((16, width), BF, "v"),
            ((part, width + hidden), BF, "v"),
            ((long, width), BF, "v"),
        ],
        (query_weight, key_weight, value_weight, output_weight, inner_weight, outer_weight, *vectors),
        "v" * 15,
        [],
        "pack",
    )

    def pair_up(mine, theirs):
        return jnp.where(
            x == 0,
            jnp.concatenate([mine, theirs], axis=0),
            jnp.concatenate([theirs, mine], axis=0),
        )

    def along_z(block):
        return tuple(hop(block, planes, bits) for bits in (2, 4, 6))

    order = Order(p2)
    sent_2 = along_z(p2)
    del_other, from_x, small_x = order.take(swap(deleted, SEQ), swap(send, SEQ), swap(small, SEQ))
    tail = jnp.pad(add(small, small_x), ((0, 0), (0, tall - width)))
    both_a = jnp.concatenate([pair_up(keep, from_x[:, :tall]), tail], axis=0)
    both_1 = pair_up(p1[:, :flat], from_x[:, tall : tall + flat])
    both_b = pair_up(p1[:, flat:], from_x[:, tall + flat :])
    order.step(both_a)
    sent_a = along_z(both_a)
    order.step(both_b)
    other = swap(order.take(own), SEQ)
    quad_2 = order.step(jnp.stack([p2, *order.take(*sent_2)]))
    octet = hop(quad_2, planes, 1)
    quad_a = order.step(jnp.stack([both_a, *order.take(*sent_a)]))
    quad_ay = hop(quad_a, planes, 1)
    sent_1 = along_z(order.take(both_1))
    octet = order.step(jnp.concatenate([quad_2, order.take(octet)], axis=0))
    octet_x = swap(octet, SEQ)
    quad_ay, other = order.take(quad_ay, other)
    order.step(quad_ay)
    quad_1 = order.step(jnp.stack([both_1, *order.take(*sent_1)]))
    parts_a = order.take(swap(quad_a, FSDP), swap(quad_ay, FSDP))
    parts_a = (quad_a, quad_ay) + parts_a
    order.step(parts_a[-1])
    quad_1y = hop(quad_1, planes, 1)
    sent_b = along_z(after(both_b, quad_1))

    marks = (lens, deleted, del_other)
    queries, keys, values, mix_send, log_other, small = call(
        attend_kernel,
        [((2 * count, half), BF, "v")] * 3
        + [((count, half), BF, "v"), ((8, count), F32, "v"), ((16, width), F32, "v")],
        marks + (order.take(own), other) + parts_a,
        "svvaaaaaa",
        [
            pltpu.VMEM((16, 64, tall), BF),
            pltpu.VMEM((2, count, width), BF),
            pltpu.VMEM((1, 2 * count), jnp.int32),
            dma((16,)),
            dma((2,)),
        ],
        "attend",
    )
    order.step(mix_send)
    mix_other = swap(mix_send, SEQ)
    quad_1y = order.step(order.take(quad_1y))
    quad_b = order.step(jnp.stack([both_b, *order.take(*sent_b)]))
    quad_by = hop(quad_b, planes, 1)
    mix_own, log_own = call(
        attend_own_kernel,
        [((count, half), BF, "v"), ((8, count), F32, "v")],
        marks + (order.take(queries), keys, values),
        "svvvvv",
        [pltpu.VMEM((1, 2 * count), jnp.int32)],
        "attend_own",
    )
    order.step(mix_own)
    octet_x, mix_other = order.take(octet_x, mix_other)
    order.step(octet_x)
    parts_2 = (octet, octet_x, swap(octet, FSDP), swap(octet_x, FSDP))
    parts_1 = (quad_1, quad_1y, swap(quad_1, FSDP), swap(quad_1y, FSDP))
    quad_by = order.take(quad_by)
    parts_1 += (quad_b, quad_by, swap(quad_b, FSDP), swap(quad_by, FSDP))
    four = ((hidden // width, count, width), BF, "a")
    tokens = ((count, width), BF, "v")
    (
        output, pooled, residual, mg_own, mg_send, small_grad,
        active, inner_low, low, outer_low, branch_low,
    ) = call(
        feed_kernel,
        [
            tokens,
            ((crops, width), F32, "v"),
            ((count, width), F32, "v"),
            ((count, half), BF, "v"),
            ((count, half), BF, "v"),
            ((16, width), F32, "v"),
            four, four, tokens, tokens, tokens,
        ],
        marks
        + (own, mix_own, mix_other, small, cotangent[0], pool_cotangent[0])
        + parts_1
        + parts_2,
        "svvvvvvvv" + "a" * 12,
        [
            pltpu.VMEM((16, 2 * part, width + hidden), BF),
            pltpu.VMEM((32, long, width), BF),
            pltpu.VMEM((hidden // width, count, width), F32),
            pltpu.VMEM((count, width), F32),
            pltpu.VMEM((count, 1), F32),
            pltpu.VMEM((count, width), F32),
            pltpu.VMEM((count, width), F32),
            pltpu.VMEM((hidden // width, count, width), BF),
            pltpu.VMEM((hidden // width, count, width), BF),
            dma((32,)),
            dma((32,)),
            dma((2 * hidden // width,)),
        ],
        "feed",
    )
    mg_other = swap(mg_send, SEQ)

    blocks_2 = ((8, long, width), BF, "a")
    keep_2a, keep_2b, send_2a, send_2b = call(
        outer_sum_kernel,
        [blocks_2] * 4,
        (active, outer_low),
        [pl.BlockSpec((1, count, width), lambda step: (step, 0, 0)), "v"],
        [pltpu.VMEM((32, long, width), BF), dma((32,))],
        "outer_sum",
        (hidden // width,),
    )
    order.step(send_2b)
    mg_other = order.step(order.take(mg_other))
    core_2b = swap(order.take(send_2b), FSDP)
    blocks_a = ((4, 2 * part, flat), BF, "a")
    blocks_b = ((4, 2 * part, width + hidden - flat + 256), BF, "a")
    keep_1a, keep_1b, send_1a, send_1b, keep_3a, keep_3b, send_3a, send_3b = call(
        inner_sum_kernel,
        [blocks_a] * 4 + [blocks_b] * 4,
        (order.take(low), inner_low, branch_low, mix_own, mix_other, small_grad),
        "vvvvvv",
        [
            pltpu.VMEM((16, 2 * part, width + hidden + 256), BF),
            pltpu.VMEM((width, count), BF),
            pltpu.VMEM((2 * part, 256), F32),
            dma((80,)),
        ],
        "inner_sum",
    )
    order.step(send_1b)
    t1_2 = order.step(add(keep_2b, order.take(core_2b)))
    sum_2x = swap(t1_2, SEQ)
    t1_1 = order.step(add(keep_1b, order.take(swap(send_1b, FSDP))))
    sum_1y = hop(t1_1, planes, 1)
    t1_3 = order.step(add(keep_3b, order.take(swap(send_3b, FSDP))))
    sum_3y = hop(t1_3, planes, 1)
    core_2, core_1, core_3 = (
        swap(value, FSDP) for value in order.take(send_2a, send_1a, send_3a)
    )

    def split_x(v):
        v = v.reshape((2, part) + v.shape[1:])
        return jnp.where(x == 0, v[0], v[1]), jnp.where(x == 0, v[1], v[0])

    def to_z(u):
        return tuple(hop(u[index], planes, 2 * index) for index in (1, 2, 3))

    specs = ["s", "v", "v"] + [column(2 * count)] * 3 + [column(count)] * 4 + ["v", "v"]
    (lows,) = call(
        retreat_kernel,
        [((2 * count, tall), BF, column(2 * count, 384))],
        marks
        + (order.take(queries), keys, values)
        + (mg_own, mg_other, mix_own, mix_send, log_own, log_other),
        specs,
        [
            pltpu.VMEM((2 * count, 1), F32),
            pltpu.VMEM((2 * count, 128), F32),
            pltpu.VMEM((2 * count, 128), F32),
        ],
        "retreat",
        (half // 128,),
    )
    order.step(lows)
    u_1 = add(keep_1a, *order.take(core_1, sum_1y))
    order.step(u_1)
    sum_1z = to_z(u_1)
    u_2 = order.step(add(keep_2a, *order.take(core_2, sum_2x)))
    sum_2y = hop(u_2[4:], planes, 1)
    wide = tall + 128
    keep_a, keep_b, send_a, send_b = call(
        project_sum_kernel,
        [((4, 2 * part, wide), BF, "a")] * 4,
        (order.take(own), other, lows),
        "aav",
        [
            pltpu.VMEM((2, count, width), BF),
            pltpu.VMEM((16, 2 * part, wide), BF),
            pltpu.VMEM((width, 2 * count), BF),
            dma((2,)),
            dma((16,)),
        ],
        "project_sum",
    )
    order.step(send_b)
    core_b, core_a = swap(send_b, FSDP), swap(send_a, FSDP)
    u_3 = add(keep_3a, *order.take(core_3, sum_3y))
    order.step(u_3)
    sum_3z = to_z(u_3)
    t1_a = order.step(add(keep_b, order.take(core_b)))
    sum_ay = hop(t1_a, planes, 1)
    v_1 = order.step(add(u_1[0], *order.take(*sum_1z)))
    v_2 = add(u_2[:4], order.take(sum_2y))
    order.step(v_2)
    sum_2z = to_z(v_2)
    v_3 = order.step(add(u_3[0], *order.take(*sum_3z)))
    states_part, states_send = call(
        states_sum_kernel,
        [((count, width), F32, "v"), tokens],
        (order.take(lows), residual) + parts_a,
        "vvaaaa",
        [pltpu.VMEM((16, 64, tall), BF), dma((16,))],
        "states_sum",
    )
    order.step(states_send)
    states_x = swap(states_send, SEQ)
    pooled_x = swap(pooled, SEQ)
    grad_outer_weight = order.step(add32(v_2[0], *order.take(*sum_2z)))
    u_a = add(keep_a, *order.take(core_a, sum_ay))
    order.step(u_a)
    sum_az = to_z(u_a)
    small = v_3[:, width + hidden - flat :]
    small = jnp.concatenate([small[:part], small[part:]], axis=1)
    mine_1, theirs_1 = split_x(
        jnp.concatenate([v_1, v_3[:, : width + hidden - flat]], axis=1)
    )
    sent_1x = swap(jnp.concatenate([theirs_1, small], axis=1), SEQ)
    v = order.step(add(u_a[0], *order.take(*sum_az)))
    mine_a, theirs_a = split_x(v)
    sent_ax = swap(theirs_a, SEQ)
    states_grad = order.step(add32(states_part, order.take(states_x)))
    pooled = pooled + order.take(pooled_x)
    sent_1x = order.take(sent_1x)
    total = mine_1.astype(F32) + sent_1x[:, : width + hidden].astype(F32)
    grad_output_weight, grad_inner_weight = total[:, :width], total[:, width:]
    small = small.astype(F32) + sent_1x[:, width + hidden :].astype(F32)
    small = jnp.concatenate([small[:, :256], small[:, 256:]], axis=0)
    smalls = small[:36].reshape(12, width)
    theirs = order.take(sent_ax)
    left = jnp.where(x == 0, mine_a, theirs).astype(F32)
    right = jnp.where(x == 0, theirs, mine_a).astype(F32)

    def gathered(index):
        columns = [
            side[:, (pair * 3 + index) * 128 : (pair * 3 + index + 1) * 128]
            for side in (left, right)
            for pair in range(half // 128)
        ]
        return jnp.concatenate(columns, axis=1)

    grad_query_weight, grad_key_weight, grad_value_weight = (gathered(i) for i in range(3))
    bias_grads = jnp.stack([left[:6, tall:], right[:6, tall:]]).reshape(2, 2, half)
    bias_grads = jnp.transpose(bias_grads, (1, 0, 2)).reshape(2, width)
    vectors = lax.dynamic_slice(smalls[:8], (0, device * part), (8, part))
    bias_grads = lax.dynamic_slice(bias_grads, (0, device * part), (2, part))
    grad_inner_bias = lax.dynamic_slice(
        smalls[8:12].reshape(hidden), (device * long,), (long,)
    )
    return (
        output[None],
        pooled[None],
        states_grad[None],
        grad_query_weight,
        bias_grads[0],
        grad_key_weight,
        grad_value_weight,
        bias_grads[1],
        grad_output_weight,
        vectors[2],
        vectors[3],
        vectors[4],
        grad_inner_weight,
        grad_inner_bias,
        grad_outer_weight,
        vectors[5],
        vectors[6],
        vectors[7],
    )


def solution(mesh):
    in_specs = (
        P(ROWS, SEQ, None),
        P(ROWS, SEQ),
        P(ROWS, None),
        BY_ROW,
        FLAT,
        BY_ROW,
        BY_ROW,
        FLAT,
        BY_ROW,
        FLAT,
        FLAT,
        FLAT,
        BY_ROW,
        FLAT,
        BY_ROW,
        FLAT,
        FLAT,
        FLAT,
        P(ROWS, SEQ, None),
        P(ROWS, None, None),
    )
    out_specs = (
        P(ROWS, SEQ, None),
        P(ROWS, None, None),
        P(ROWS, SEQ, None),
        BY_ROW,
        FLAT,
        BY_ROW,
        BY_ROW,
        FLAT,
        BY_ROW,
        FLAT,
        FLAT,
        FLAT,
        BY_ROW,
        FLAT,
        BY_ROW,
        FLAT,
        FLAT,
        FLAT,
    )
    shape = mesh.shape
    halves = (shape[DP], shape[FSDP], shape[SEQ]) == (8, 2, 2)
    chosen = halves_body if halves else body
    return jax.shard_map(chosen, mesh=mesh, in_specs=in_specs, out_specs=out_specs, check_vma=False)
```

```python
from functools import partial

import jax
import jax.numpy as jnp
from jax import lax
from jax.experimental import pallas as pl
from jax.experimental.pallas import tpu as pltpu
from jax.sharding import PartitionSpec as P

HEADS = 12
HEAD = 64


highest = lax.Precision.HIGHEST
DP, FSDP, SEQ = "dp", "fsdp", "seq"
EVERY = (DP, FSDP, SEQ)
BY_ROW, FLAT = P(EVERY, None), P(EVERY)
ROWS = (DP, FSDP)


def layer_norm(values, gain, shift):
    centered = values - jnp.mean(values, axis=-1, keepdims=True)
    spread = jnp.mean(centered * centered, axis=-1, keepdims=True)
    return centered * lax.rsqrt(spread + 1e-06) * gain + shift


def crop_layout(lengths, deleted, places):
    crop_ends = jnp.cumsum(lengths, axis=-1, dtype=jnp.int32)
    segment = jnp.sum(
        (places[..., :, None] >= crop_ends[..., None, :]).astype(jnp.int32),
        axis=-1,
        dtype=jnp.int32,
    )
    retained = (deleted == 0) & (segment < lengths.shape[-1])
    key_tag = jnp.where(retained, segment, -1)
    return (segment, retained, key_tag)


def product(left, right):
    return jnp.dot(left, right, preferred_element_type=jnp.float32)


def column_sum(values):
    return jnp.sum(values.astype(jnp.float32), axis=0)


def sweep(carry, pieces, inner):
    count = pieces[0].shape[1]
    width = 256

    def turn(index, totals):
        offset = index * width
        parts = tuple((lax.dynamic_slice_in_dim(piece, offset, width, 1) for piece in pieces))
        return inner(totals, parts, offset)

    return lax.fori_loop(0, count // width, turn, carry)


def scores_at(query_part, key_part):
    return (
        jnp.einsum("rqhd,rkhd->rhqk", query_part, key_part, preferred_element_type=jnp.float32)
        * 0.125
    )


def allowed_at(query_tag, query_place, tags, begin):
    key_place = begin + jnp.arange(tags.shape[1], dtype=jnp.int32)
    same = tags[:, None, :] == query_tag[:, :, None]
    itself = key_place[None, None, :] == query_place[None, :, None]
    return (same | itself)[:, None]


def probs_at(raw, allowed, log_part):
    return jnp.where(allowed, jnp.exp(raw - log_part[..., None]), 0.0)


def body(
    states,
    deleted,
    crop_lengths,
    query_weight,
    query_bias,
    key_weight,
    value_weight,
    value_bias,
    output_weight,
    output_bias,
    attn_gain,
    attn_shift,
    inner_weight,
    inner_bias,
    outer_weight,
    outer_bias,
    final_gain,
    final_shift,
    cotangent,
    pool_cotangent,
):
    rows, shard, width = states.shape
    lowered = [
        master.astype(jnp.bfloat16)
        for master in (
            query_weight,
            query_bias,
            key_weight,
            value_weight,
            value_bias,
            output_weight,
            output_bias,
            attn_gain,
            attn_shift,
            inner_weight,
            inner_bias,
            outer_weight,
            outer_bias,
            final_gain,
            final_shift,
        )
    ]
    (
        w_query,
        b_query,
        w_key,
        w_value,
        b_value,
        w_out,
        b_out,
        g_attn,
        s_attn,
        w_inner,
        b_inner,
        w_outer,
        b_outer,
        g_final,
        s_final,
    ) = (
        lax.all_gather(lowered[0], EVERY, axis=0, tiled=True),
        lax.all_gather(lowered[1], EVERY, axis=0, tiled=True),
        lax.all_gather(lowered[2], EVERY, axis=0, tiled=True),
        lax.all_gather(lowered[3], EVERY, axis=0, tiled=True),
        lax.all_gather(lowered[4], EVERY, axis=0, tiled=True),
        lax.all_gather(lowered[5], EVERY, axis=0, tiled=True),
        lax.all_gather(lowered[6], EVERY, axis=0, tiled=True),
        lax.all_gather(lowered[7], EVERY, axis=0, tiled=True),
        lax.all_gather(lowered[8], EVERY, axis=0, tiled=True),
        lax.all_gather(lowered[9], EVERY, axis=0, tiled=True),
        lax.all_gather(lowered[10], EVERY, axis=0, tiled=True),
        lax.all_gather(lowered[11], EVERY, axis=0, tiled=True),
        lax.all_gather(lowered[12], EVERY, axis=0, tiled=True),
        lax.all_gather(lowered[13], EVERY, axis=0, tiled=True),
        lax.all_gather(lowered[14], EVERY, axis=0, tiled=True),
    )
    own_start = lax.axis_index(SEQ) * shard
    places = own_start + jnp.arange(shard, dtype=jnp.int32)
    segment, retained, key_tag = crop_layout(crop_lengths, deleted, places)
    flat = states.reshape(rows * shard, width)
    split = (rows, shard, HEADS, HEAD)
    queries = (product(flat, w_query) + b_query).astype(jnp.bfloat16).reshape(split)
    keys = product(flat, w_key).astype(jnp.bfloat16).reshape(split)
    values = (product(flat, w_value) + b_value).astype(jnp.bfloat16).reshape(split)

    def scale_step(totals, parts, begin):
        top, total = totals
        key_part, tags = parts
        allowed = allowed_at(segment, places, tags, begin)
        masked = jnp.where(allowed, scores_at(queries, key_part), -1e30)
        new_top = jnp.maximum(top, jnp.max(masked, axis=-1))
        raised = jnp.where(allowed, jnp.exp(masked - new_top[..., None]), 0.0)
        return (new_top, total * jnp.exp(top - new_top) + jnp.sum(raised, axis=-1))

    stat_shape = (rows, HEADS, shard)
    scale_init = (jnp.full(stat_shape, -1e30, jnp.float32), jnp.zeros(stat_shape, jnp.float32))
    top, total = sweep(
        scale_init,
        (
            lax.all_gather(keys, SEQ, axis=1, tiled=True),
            lax.all_gather(key_tag, SEQ, axis=1, tiled=True),
        ),
        inner=scale_step,
    )
    log_total = top + jnp.log(total)

    def mix_step(totals, parts, begin):
        coarse, fine = totals
        key_part, value_part, tags = parts
        probs = probs_at(
            scores_at(queries, key_part), allowed_at(segment, places, tags, begin), log_total
        )
        probs_low = probs.astype(jnp.bfloat16)
        rest = (probs - probs_low.astype(jnp.float32)).astype(jnp.bfloat16)
        coarse = coarse + jnp.einsum(
            "rhqk,rkhd->rqhd", probs_low, value_part, preferred_element_type=jnp.float32
        )
        fine = fine + jnp.einsum(
            "rhqk,rkhd->rqhd", rest, value_part, preferred_element_type=jnp.float32
        )
        return (coarse, fine)

    empty = jnp.zeros(split, jnp.float32)
    coarse, fine = sweep(
        (empty, empty),
        (
            lax.all_gather(keys, SEQ, axis=1, tiled=True),
            lax.all_gather(values, SEQ, axis=1, tiled=True),
            lax.all_gather(key_tag, SEQ, axis=1, tiled=True),
        ),
        inner=mix_step,
    )
    attended = coarse.astype(jnp.bfloat16).reshape(rows * shard, width)
    branch = product(attended, w_out) + b_out
    residual = states.astype(jnp.float32).reshape(rows * shard, width) + branch
    normed, attn_back = jax.vjp(
        layer_norm, residual, g_attn.astype(jnp.float32), s_attn.astype(jnp.float32)
    )
    normed_low = normed.astype(jnp.bfloat16)
    inner = product(normed_low, w_inner) + b_inner
    active_full, gelu_back = jax.vjp(partial(jax.nn.gelu, approximate=False), inner)
    active = active_full.astype(jnp.bfloat16)
    outer = product(active, w_outer) + b_outer
    result, final_back = jax.vjp(
        layer_norm, normed + outer, g_final.astype(jnp.float32), s_final.astype(jnp.float32)
    )
    output = result.astype(jnp.bfloat16).reshape(rows, shard, width)
    crops = crop_lengths.shape[1]
    member = (
        (segment[..., None] == jnp.arange(crops, dtype=jnp.int32)) & retained[..., None]
    ).astype(jnp.float32)
    partial_sums = jnp.einsum(
        "rnc,rnd->rcd",
        member,
        result.reshape(rows, shard, width),
        precision=highest,
        preferred_element_type=jnp.float32,
    )
    sums, counts = lax.psum((partial_sums, jnp.sum(member, axis=1)), SEQ)
    divisor = jnp.maximum(counts, 1.0)[..., None]
    pooled = sums / divisor
    w_query, w_key, w_value, w_out, w_inner, w_outer = (
        lax.all_gather(lowered[0], EVERY, axis=0, tiled=True),
        lax.all_gather(lowered[2], EVERY, axis=0, tiled=True),
        lax.all_gather(lowered[3], EVERY, axis=0, tiled=True),
        lax.all_gather(lowered[5], EVERY, axis=0, tiled=True),
        lax.all_gather(lowered[9], EVERY, axis=0, tiled=True),
        lax.all_gather(lowered[11], EVERY, axis=0, tiled=True),
    )
    result_grad = cotangent.astype(jnp.float32) + jnp.einsum(
        "rnc,rcd->rnd",
        member,
        pool_cotangent / divisor,
        precision=highest,
        preferred_element_type=jnp.float32,
    )
    sum_grad, grad_final_gain, grad_final_shift = final_back(
        result_grad.reshape(rows * shard, width)
    )
    outer_grad = sum_grad.astype(jnp.bfloat16)
    grad_outer_bias = column_sum(outer_grad)
    grad_outer_weight = product(active.T, outer_grad)
    inner_grad = gelu_back(product(outer_grad, w_outer.T))[0].astype(jnp.bfloat16)
    grad_inner_bias = column_sum(inner_grad)
    grad_inner_weight = product(normed_low.T, inner_grad)
    normed_grad = sum_grad + product(inner_grad, w_inner.T)
    residual_grad, grad_attn_gain, grad_attn_shift = attn_back(normed_grad)
    branch_grad = residual_grad.astype(jnp.bfloat16)
    grad_output_bias = column_sum(branch_grad)
    grad_output_weight = product(attended.T, branch_grad)
    mixed_grad = product(branch_grad, w_out.T).astype(jnp.bfloat16).reshape(split)
    delta = jnp.sum(mixed_grad.astype(jnp.float32) * (coarse + fine), axis=-1)
    delta_local = jnp.transpose(delta, (0, 2, 1))
    all_log, all_delta = (
        lax.all_gather(jnp.transpose(log_total, (0, 2, 1)), SEQ, axis=1, tiled=True),
        lax.all_gather(delta, SEQ, axis=1, tiled=True),
    )

    def key_side(totals, parts, begin):
        key_grad, value_grad = totals
        query_part, grad_part, tags_part = parts
        count = tags_part.shape[1]
        log_part = jnp.transpose(lax.dynamic_slice_in_dim(all_log, begin, count, 1), (0, 2, 1))
        delta_part = jnp.transpose(lax.dynamic_slice_in_dim(all_delta, begin, count, 1), (0, 2, 1))
        query_place = begin + jnp.arange(count, dtype=jnp.int32)
        allowed = allowed_at(tags_part, query_place, key_tag, own_start)
        probs = probs_at(scores_at(query_part, keys), allowed, log_part)
        value_grad = value_grad + jnp.einsum(
            "rhqk,rqhd->rkhd",
            probs.astype(jnp.bfloat16),
            grad_part,
            preferred_element_type=jnp.float32,
        )
        prob_grad = jnp.einsum(
            "rqhd,rkhd->rhqk", grad_part, values, preferred_element_type=jnp.float32
        )
        score_grad = (probs * (prob_grad - delta_part[..., None]) * 0.125).astype(jnp.bfloat16)
        key_grad = key_grad + jnp.einsum(
            "rhqk,rqhd->rkhd", score_grad, query_part, preferred_element_type=jnp.float32
        )
        return (key_grad, value_grad)

    key_grad, value_grad = sweep(
        (empty, empty),
        (
            lax.all_gather(queries, SEQ, axis=1, tiled=True),
            lax.all_gather(mixed_grad, SEQ, axis=1, tiled=True),
            lax.all_gather(segment, SEQ, axis=1, tiled=True),
        ),
        inner=key_side,
    )

    def query_side(query_grad, parts, begin):
        key_part, value_part, tags = parts
        probs = probs_at(
            scores_at(queries, key_part), allowed_at(segment, places, tags, begin), log_total
        )
        prob_grad = jnp.einsum(
            "rqhd,rkhd->rhqk", mixed_grad, value_part, preferred_element_type=jnp.float32
        )
        score_grad = (probs * (prob_grad - delta_local[..., None]) * 0.125).astype(jnp.bfloat16)
        return query_grad + jnp.einsum(
            "rhqk,rkhd->rqhd", score_grad, key_part, preferred_element_type=jnp.float32
        )

    query_grad = sweep(
        empty,
        (
            lax.all_gather(keys, SEQ, axis=1, tiled=True),
            lax.all_gather(values, SEQ, axis=1, tiled=True),
            lax.all_gather(key_tag, SEQ, axis=1, tiled=True),
        ),
        inner=query_side,
    )
    query_low = query_grad.astype(jnp.bfloat16).reshape(rows * shard, width)
    key_low = key_grad.astype(jnp.bfloat16).reshape(rows * shard, width)
    value_low = value_grad.astype(jnp.bfloat16).reshape(rows * shard, width)
    grad_query_weight = product(flat.T, query_low)
    grad_query_bias = column_sum(query_low)
    grad_key_weight = product(flat.T, key_low)
    grad_value_weight = product(flat.T, value_low)
    grad_value_bias = column_sum(value_low)
    states_grad = (
        residual_grad
        + product(query_low, w_query.T)
        + product(key_low, w_key.T)
        + product(value_low, w_value.T)
    ).reshape(rows, shard, width)
    summed = (
        lax.psum_scatter(grad_query_weight, EVERY, scatter_dimension=0, tiled=True),
        lax.psum_scatter(grad_query_bias, EVERY, scatter_dimension=0, tiled=True),
        lax.psum_scatter(grad_key_weight, EVERY, scatter_dimension=0, tiled=True),
        lax.psum_scatter(grad_value_weight, EVERY, scatter_dimension=0, tiled=True),
        lax.psum_scatter(grad_value_bias, EVERY, scatter_dimension=0, tiled=True),
        lax.psum_scatter(
            grad_output_weight, EVERY, scatter_dimension=0, tiled=True
        ),
        lax.psum_scatter(grad_output_bias, EVERY, scatter_dimension=0, tiled=True),
        lax.psum_scatter(grad_attn_gain, EVERY, scatter_dimension=0, tiled=True),
        lax.psum_scatter(grad_attn_shift, EVERY, scatter_dimension=0, tiled=True),
        lax.psum_scatter(grad_inner_weight, EVERY, scatter_dimension=0, tiled=True),
        lax.psum_scatter(grad_inner_bias, EVERY, scatter_dimension=0, tiled=True),
        lax.psum_scatter(grad_outer_weight, EVERY, scatter_dimension=0, tiled=True),
        lax.psum_scatter(grad_outer_bias, EVERY, scatter_dimension=0, tiled=True),
        lax.psum_scatter(grad_final_gain, EVERY, scatter_dimension=0, tiled=True),
        lax.psum_scatter(grad_final_shift, EVERY, scatter_dimension=0, tiled=True),
    )
    return (output, pooled, states_grad) + tuple(summed)


BF = jnp.bfloat16
F32 = jnp.float32
MIB = 1 << 20


def dot(left, right, left_dim=1, right_dim=0):
    return lax.dot_general(
        left,
        right,
        (((left_dim,), (right_dim,)), ((), ())),
        preferred_element_type=F32,
    )


def exact_dot(left, right, left_dim=1, right_dim=0):
    return lax.dot_general(
        left,
        right,
        (((left_dim,), (right_dim,)), ((), ())),
        precision=highest,
        preferred_element_type=F32,
    )


def crop_ends_of(lens_ref):
    ends, total = [], jnp.int32(0)
    for slot in range(lens_ref.shape[0]):
        total = total + lens_ref[slot]
        ends.append(total)
    return ends


def segment_of(ends, places):
    segment = jnp.zeros(places.shape, jnp.int32)
    for end in ends:
        segment = segment + (places >= end).astype(jnp.int32)
    return segment


def for_windows(ends, block, first, last, turn):
    begin = ends[0] * 0
    for end in ends:
        begin = jnp.maximum(begin, jnp.where(end <= 2 * block, end, 0))
    single = (begin < block).astype(jnp.int32)

    def three(index, carry):
        start = jnp.where(index == 2, 1 - single, 0) * block
        turn(index, pl.multiple_of(start, block), 3)
        return carry

    def two(index, carry):
        start = jnp.where(index == 0, 0, 2) * block
        turn(index, pl.multiple_of(start, block), 2)
        return carry

    def one(index, carry):
        turn(index, pl.multiple_of(index * block, block), 1)
        return carry

    low = jnp.maximum(first, 1 - single)
    lax.fori_loop(low, jnp.minimum(last, 3), three, 0)
    lax.fori_loop(first, jnp.where((first == 0) & (single == 0), 1, first), two, 0)
    final = jnp.where(last == 4, 1, 0)
    lax.fori_loop(3, 3 + final * (1 - single), two, 0)
    lax.fori_loop(3, 3 + final * single, one, 0)


def pack_kernel(
    place, wq, wk, wv, wo, w1, w2, v0, v1, v2, v3, v4, v5, v6, v7, v96,
    send, keep, small, p1, p2,
):
    x = place[3]
    device = place[4]
    half = wq.shape[1] // 2
    for pair in range(half // 128):
        for index, ref in enumerate((wq, wk, wv)):
            left = ref[:, pair * 128 : pair * 128 + 128].astype(BF)
            right = ref[:, half + pair * 128 : half + pair * 128 + 128].astype(BF)
            begin = (pair * 3 + index) * 128
            keep[:, begin : begin + 128] = jnp.where(x == 0, left, right)
            send[:, begin : begin + 128] = jnp.where(x == 0, right, left)
    width = wo.shape[1]
    tall = keep.shape[1]
    for ref, begin in ((send, tall), (p1, 0)):
        ref[:, begin : begin + width] = wo[...].astype(BF)
        ref[:, begin + width :] = w1[...].astype(BF)
    p2[...] = w2[...].astype(BF)
    part = v0.shape[1]
    row = lax.broadcasted_iota(jnp.int32, (8, part), 0)
    stacked = jnp.zeros((8, part), F32)
    for index, ref in enumerate((v0, v1, v2, v3, v4, v5, v6, v7)):
        stacked = jnp.where(row == index, ref[...], stacked)
    row = lax.broadcasted_iota(jnp.int32, (part, width), 0)
    lane = lax.broadcasted_iota(jnp.int32, (part, width), 1)
    spread = (row + device * part == lane).astype(BF)
    first = dot(stacked.astype(BF), spread)
    part = v96.shape[1]
    row = lax.broadcasted_iota(jnp.int32, (part, width), 0)
    lane = lax.broadcasted_iota(jnp.int32, (part, width), 1)
    rows = []
    for index in range(8):
        if index < v96.shape[1] * 32 // width:
            spread = (row + device * part == lane + index * width).astype(BF)
            rows.append(dot(jnp.broadcast_to(v96[...], (8, part)).astype(BF), spread))
    tall = lax.broadcasted_iota(jnp.int32, (8, width), 0)
    second = jnp.zeros((8, width), F32)
    for index, value in enumerate(rows):
        second = jnp.where(tall == index, value[:1], second)
    small[...] = jnp.concatenate([first, second], axis=0).astype(BF)


def blocks_in(place, parts, store, sems, flips, first=0):
    copies = []
    for part, (ref, offset) in enumerate(zip(parts, flips, strict=True)):
        for slot in range(ref.shape[0]):
            spot = slot_place(place, offset, slot)
            copies.append(
                pltpu.make_async_copy(
                    ref.at[slot], store.at[spot], sems.at[first + part * ref.shape[0] + slot]
                )
            )
    return copies


def xor(value, bits):
    if bits & 1:
        value = value + 1 - 2 * lax.rem(value, 2)
    if bits & 2:
        value = lax.rem(value + 2, 4)
    return value


def slot_place(place, flip, slot):
    flip_y, flip_c, flip_x = flip
    z = xor(place[0], slot % 4)
    y = xor(place[1], flip_y ^ (slot // 4))
    c = xor(place[2], flip_c)
    spot = (z * 2 + y) * 2 + c
    if flip_x is None:
        return spot
    return spot * 2 + xor(place[3], flip_x)


PAIR_FLIPS = ((0, 0, None), (1, 0, None), (0, 1, None), (1, 1, None))
FULL_FLIPS = ((0, 0, 0), (0, 0, 1), (0, 1, 0), (0, 1, 1))


def tag_row(ends, x, own, other):
    half = own.shape[1]
    parts = []
    for index in range(2):
        deleted = jnp.where(x == index, own[...], other[...])
        places = index * half + lax.broadcasted_iota(jnp.int32, (1, half), 1)
        segment = segment_of(ends, places)
        parts.append(jnp.where((deleted == 0) & (segment < len(ends)), segment, -1))
    return parts


def attend_block(ends, tags, q_ref, k_ref, v_ref, index, block, start, wide):
    wide = wide * block
    lane_low = lax.broadcasted_iota(jnp.int32, (block, 128), 1) < 64
    key_low = lax.broadcasted_iota(jnp.int32, (wide, 128), 1) < 64
    begin = pl.multiple_of(index * block, block)
    places = begin + lax.broadcasted_iota(jnp.int32, (block, 1), 0)
    key_places = start + lax.broadcasted_iota(jnp.int32, (1, wide), 1)
    allowed = (tags[0:1, pl.ds(start, wide)] == segment_of(ends, places)) | (key_places == places)
    bias = jnp.where(allowed, 0.0, -1e30)
    outs = []
    lanes = lax.broadcasted_iota(jnp.int32, (block, 128), 1)
    logs = jnp.zeros((block, 128), F32)
    for pair in range(q_ref.shape[1] // 128):
        columns = slice(pair * 128, pair * 128 + 128)
        queries = q_ref[pl.ds(begin, block), columns] * jnp.asarray(0.125, BF)
        keys = k_ref[pl.ds(start, wide), columns]
        values = v_ref[pl.ds(start, wide), columns]
        total = jnp.zeros((block, 128), F32)
        for side in range(2):
            mine = lane_low if side == 0 else ~lane_low
            key_mine = key_low if side == 0 else ~key_low
            scores = dot(jnp.where(mine, queries, 0), keys, 1, 1) + bias
            top = jnp.max(scores, axis=1, keepdims=True)
            raised = jnp.exp(scores - top)
            amount = jnp.sum(raised, axis=1, keepdims=True)
            probs = (raised * (1.0 / amount)).astype(BF)
            total = total + dot(probs, jnp.where(key_mine, values, 0))
            logs = jnp.where(lanes == pair * 2 + side, top + jnp.log(amount), logs)
        outs.append(total.astype(BF))
    return jnp.concatenate(outs, axis=1), jnp.transpose(logs)[:8]


def attend_half(ends, tags, q_ref, k_ref, v_ref, side, out, logs):
    block = out.shape[0] // 2

    def turn(index, start, wide):
        spot = pl.multiple_of((index - side * 2) * block, block)
        mixed, rows = attend_block(ends, tags, q_ref, k_ref, v_ref, index, block, start, wide)
        out[pl.ds(spot, block), :] = mixed
        logs[:, pl.ds(spot, block)] = rows

    for_windows(ends, block, side * 2, side * 2 + 2, turn)


def fill_tags(ends, x, del_own, del_other, tags):
    half = del_own.shape[1]
    for index, part in enumerate(tag_row(ends, x, del_own, del_other)):
        tags[0:1, index * half : (index + 1) * half] = part


def attend_kernel(
    place, lens, del_own, del_other, st_own, st_other, a0, a1, a2, a3,
    q_out, k_out, v_out, mixed, logs, small_out,
    store, rows, tags, sems, row_sems,
):
    x = place[3]
    copies = blocks_in(place, (a0, a1, a2, a3), store, sems, PAIR_FLIPS)
    for copy in copies:
        copy.start()
    own_copy = pltpu.make_async_copy(st_own, rows.at[x], row_sems.at[0])
    other_copy = pltpu.make_async_copy(st_other, rows.at[1 - x], row_sems.at[1])
    own_copy.start()
    other_copy.start()
    ends = crop_ends_of(lens)
    half = del_own.shape[1]
    fill_tags(ends, x, del_own, del_other, tags)
    for copy in copies:
        copy.wait()
    own_copy.wait()
    other_copy.wait()

    depth = store.shape[2] // 3
    small_out[...] = jnp.sum(store[:, 48:, :768].astype(F32), axis=0)
    split = pl.multiple_of(x * depth, depth)
    bias_q = small_out[0:1, pl.ds(split, depth)]
    bias_v = small_out[1:2, pl.ds(split, depth)]
    weight = store[:, :48, :].reshape(768, 3 * depth)

    def project(index, carry):
        begin = pl.multiple_of(index * half, half)
        product_ = dot(rows[index], weight)
        for pair in range(depth // 128):
            columns = slice(pair * 128, pair * 128 + 128)
            at = pair * 384
            q_out[pl.ds(begin, half), columns] = (
                product_[:, at : at + 128] + bias_q[:, columns]
            ).astype(BF)
            k_out[pl.ds(begin, half), columns] = product_[:, at + 128 : at + 256].astype(BF)
            v_out[pl.ds(begin, half), columns] = (
                product_[:, at + 256 : at + 384] + bias_v[:, columns]
            ).astype(BF)
        return carry

    lax.fori_loop(0, 2, project, 0)
    attend_half(ends, tags, q_out, k_out, v_out, 1 - x, mixed, logs)


def attend_own_kernel(place, lens, del_own, del_other, q_in, k_in, v_in, mixed, logs, tags):
    x = place[3]
    ends = crop_ends_of(lens)
    fill_tags(ends, x, del_own, del_other, tags)
    attend_half(ends, tags, q_in, k_in, v_in, x, mixed, logs)


def norm_parts(values):
    centered = values - jnp.mean(values, axis=-1, keepdims=True)
    spread = jnp.mean(centered * centered, axis=-1, keepdims=True)
    scale = lax.rsqrt(spread + 1e-06)
    return centered * scale, scale


def norm_back(grad, gain, unit, scale):
    lifted = grad * gain
    return scale * (
        lifted
        - jnp.mean(lifted, axis=-1, keepdims=True)
        - unit * jnp.mean(lifted * unit, axis=-1, keepdims=True)
    )


def gelu_parts(inner):
    phi = 0.5 * (1.0 + lax.erf(inner * 0.7071067811865476))
    density = jnp.exp(inner * inner * -0.5) * 0.3989422804014327
    return inner * phi, phi + inner * density


def feed_kernel(
    place, lens, del_own, del_other, states, mix_own, mix_other, small, cot, pool_cot,
    p0, p1, p2, p3, r0, r1, r2, r3, f0, f1, f2, f3,
    output, pooled, residual_out, mg_own, mg_other, small_out, active, inner_low, low, outer_low, branch_low,
    w1, w2, slope, unit_a, scale_a, outer, grad, acts, inners, sems1, sems2, sems_o,
):
    x = place[3]
    width = states.shape[1]
    count = states.shape[0]
    hidden = 4 * width
    part = width
    flat = p0.shape[2]
    in1 = blocks_in(place, (p0, p1, p2, p3), w1.at[:, :, :flat], sems1, PAIR_FLIPS)
    in1 += blocks_in(place, (r0, r1, r2, r3), w1.at[:, :, flat:], sems1, PAIR_FLIPS, 16)
    in2 = blocks_in(place, (f0, f1, f2, f3), w2, sems2, FULL_FLIPS)
    for copy in in1 + in2:
        copy.start()
    ends = crop_ends_of(lens)
    tags = tag_row(ends, x, del_own, del_other)
    slots = lax.broadcasted_iota(jnp.int32, (len(ends), count), 0)
    members = [(tag == slots).astype(F32) for tag in tags]
    counts = sum(jnp.sum(member, axis=1, keepdims=True) for member in members)
    divisor = jnp.maximum(counts, 1.0)
    member = jnp.where(x == 0, members[0], members[1])
    for copy in in1:
        copy.wait()

    def out_weight(side):
        return w1[pl.ds(side * 8, 8), :, :width].reshape(width // 2, width)

    branch = dot(mix_own[...], out_weight(x)) + dot(mix_other[...], out_weight(1 - x))
    branch = branch + small[2:3, :]
    unit, scale = norm_parts(states[...].astype(F32) + branch)
    unit_a[...] = unit
    scale_a[...] = scale
    value = unit * small[3:4, :] + small[4:5, :]
    low[...] = value.astype(BF)
    outer[...] = value + small[5:6, :]
    for copy in in2:
        copy.wait()

    def leave(here, there, index, sem):
        return pltpu.make_async_copy(here.at[index], there.at[index], sems_o.at[sem])

    def ahead(index, carry):
        begin = pl.multiple_of(index * part, part)
        weight = w1[:, :, pl.ds(width + begin, part)].reshape(width, part)
        inner = dot(low[...], weight) + small[pl.ds(8 + index, 1), :]
        act, bend = gelu_parts(inner)
        act = act.astype(BF)
        acts[index] = act
        leave(acts, active, index, index).start()
        slope[index] = bend
        outer[...] += dot(act, w2[pl.ds(index * 8, 8)].reshape(part, width))
        return carry

    lax.fori_loop(0, hidden // part, ahead, 0)

    unit, scale = norm_parts(outer[...])
    result = unit * small[6:7, :] + small[7:8, :]
    output[...] = result.astype(BF)
    pooled[...] = exact_dot(member, result) / divisor
    grad_in = cot[...].astype(F32) + exact_dot(member, pool_cot[...] / divisor, 0, 0)
    small_out[0:2, :] = jnp.zeros((2, width), F32)
    small_out[12:16, :] = jnp.zeros((4, width), F32)
    small_out[6:7, :] = jnp.sum(grad_in * unit, axis=0, keepdims=True)
    small_out[7:8, :] = jnp.sum(grad_in, axis=0, keepdims=True)
    total = norm_back(grad_in, small[6:7, :], unit, scale)
    grad[...] = total
    outer_low[...] = total.astype(BF)
    small_out[5:6, :] = jnp.sum(outer_low[...].astype(F32), axis=0, keepdims=True)

    def back(index, carry):
        begin = pl.multiple_of(index * part, part)
        weight = w2[pl.ds(index * 8, 8)].reshape(part, width)
        inner = (dot(outer_low[...], weight, 1, 1) * slope[index]).astype(BF)
        inners[index] = inner
        leave(inners, inner_low, index, hidden // part + index).start()
        small_out[pl.ds(8 + index, 1), :] = jnp.sum(inner.astype(F32), axis=0, keepdims=True)
        weight = w1[:, :, pl.ds(width + begin, part)].reshape(width, part)
        grad[...] += dot(inner, weight, 1, 1)
        return carry

    lax.fori_loop(0, hidden // part, back, 0)

    total = grad[...]
    unit = unit_a[...]
    small_out[3:4, :] = jnp.sum(total * unit, axis=0, keepdims=True)
    small_out[4:5, :] = jnp.sum(total, axis=0, keepdims=True)
    residual = norm_back(total, small[3:4, :], unit, scale_a[...])
    residual_out[...] = residual
    branch_low[...] = residual.astype(BF)
    small_out[2:3, :] = jnp.sum(branch_low[...].astype(F32), axis=0, keepdims=True)
    mg_own[...] = dot(branch_low[...], out_weight(x), 1, 1).astype(BF)
    mg_other[...] = dot(branch_low[...], out_weight(1 - x), 1, 1).astype(BF)
    for index in range(hidden // part):
        leave(acts, active, index, index).wait()
        leave(inners, inner_low, index, hidden // part + index).wait()


def outer_sum_kernel(place, active, outer_low, ka, kb, sa, sb, store, sems):
    step = pl.program_id(0)
    width = outer_low.shape[1]
    product_ = dot(active[0], outer_low[...], 0, 0).astype(BF)
    store[pl.ds(step * 8, 8)] = product_.reshape(8, width // 8, width)
    slot = lax.bitwise_xor(step, place[0])
    refs = (ka, kb, sa, sb)

    def copy(part, flip_y, spot, at, sem):
        return pltpu.make_async_copy(store.at[spot], refs[part].at[flip_y * 4 + at], sems.at[sem])

    for part in range(4):
        for flip_y in range(2):
            y = xor(place[1], flip_y)
            c = xor(place[2], part // 2)
            x = xor(place[3], part % 2)
            spot = ((step * 2 + y) * 2 + c) * 2 + x
            copy(part, flip_y, spot, slot, step * 8 + part * 2 + flip_y).start()

    @pl.when(step == 3)
    def _():
        for index in range(32):
            copy(0, 0, index, 0, index).wait()


def inner_sum_kernel(
    place, low, inner_low, branch_low, mix_own, mix_other, small,
    ka, kb, sa, sb, la, lb, ta, tb, store, low_t, rows, sems,
):
    x = place[3]
    width = low.shape[1]
    copies = []

    def send(chunk):
        begin = chunk * width
        refs = (ka, kb, sa, sb)
        into = begin
        end = begin + width if chunk < inner_low.shape[0] else store.shape[2]
        if begin >= ka.shape[2]:
            refs = (la, lb, ta, tb)
            into = begin - ka.shape[2]
        for part, flip in enumerate(PAIR_FLIPS):
            for slot in range(4):
                spot = slot_place(place, flip, slot)
                copy = pltpu.make_async_copy(
                    store.at[spot, :, begin:end],
                    refs[part].at[slot, :, into : into + end - begin],
                    sems.at[chunk * 16 + part * 4 + slot],
                )
                copy.start()
                copies.append(copy)

    rows[...] = jnp.zeros(rows.shape, F32)
    for vector in range(12):
        for third in range(3):
            row = vector * 3 + third
            rows[row : row + 1, :] = small[vector : vector + 1, third * 256 : third * 256 + 256]
    store[:, :, 5 * width :] = jnp.broadcast_to(rows[...].astype(BF)[None], (16, 48, 256))
    low_t[...] = jnp.transpose(low[...])
    for side, mix in ((x, mix_own), (1 - x, mix_other)):
        product_ = dot(mix[...], branch_low[...], 0, 0).astype(BF)
        store[pl.ds(side * 8, 8), :, :width] = product_.reshape(8, width // 16, width)
    send(0)
    for index in range(inner_low.shape[0]):
        begin = (1 + index) * width
        product_ = dot(low_t[...], inner_low[index]).astype(BF)
        store[:, :, begin : begin + width] = product_.reshape(16, width // 16, width)
        send(1 + index)
    for copy in copies:
        copy.wait()


def blocks_out(place, parts, store, sems, flips, first):
    copies = []
    for part, (ref, offset) in enumerate(zip(parts, flips, strict=True)):
        for slot in range(ref.shape[0]):
            spot = slot_place(place, offset, slot)
            copies.append(
                pltpu.make_async_copy(
                    store.at[spot], ref.at[slot], sems.at[first + part * ref.shape[0] + slot]
                )
            )
    return copies


def retreat_kernel(
    place, lens, del_own, del_other, q_in, k_in, v_in, mg_own, mg_other, mix_own, mix_other,
    log_own, log_other, low, tags, dk, dv,
):
    x = place[3]
    ends = crop_ends_of(lens)
    half = del_own.shape[1]

    pair = pl.program_id(0)

    @pl.when(pair == 0)
    def _():
        for index, part in enumerate(tag_row(ends, x, del_own, del_other)):
            tall = jnp.transpose(jnp.broadcast_to(part.astype(F32), (8, half)))
            tags[index * half : (index + 1) * half, :] = tall[:, :1]

    dk[...] = jnp.zeros_like(dk)
    dv[...] = jnp.zeros_like(dv)
    block = half // 2
    lane_low = lax.broadcasted_iota(jnp.int32, (block, 128), 1) < 64
    heads = lax.div(lax.broadcasted_iota(jnp.int32, (8, 128), 1), 64)
    picks = (heads == lax.broadcasted_iota(jnp.int32, (8, 128), 0)).astype(F32)
    eighth = jnp.asarray(0.125, BF)

    def turn(index, start, wide):
        wide = wide * block
        key_low = lax.broadcasted_iota(jnp.int32, (wide, 128), 1) < 64
        begin = pl.multiple_of(index * block, block)
        spot = pl.multiple_of(lax.rem(index, 2) * block, block)
        places = begin + lax.broadcasted_iota(jnp.int32, (1, block), 1)
        key_places = start + lax.broadcasted_iota(jnp.int32, (wide, 1), 0)
        allowed = (tags[pl.ds(start, wide), :] == segment_of(ends, places).astype(F32)) | (
            key_places == places
        )
        bias = jnp.where(allowed, 0.0, -1e30)
        queries = q_in[pl.ds(begin, block), :] * eighth
        keys = k_in[pl.ds(start, wide), :]
        values = v_in[pl.ds(start, wide), :]
        near = lax.div(index, 2) == x
        rows = pl.ds(spot, block)
        grads = jnp.where(near, mg_own[rows, :], mg_other[rows, :])
        mixed = jnp.where(near, mix_own[rows, :], mix_other[rows, :])
        deltas = exact_dot(picks, grads.astype(F32) * mixed.astype(F32), 1, 1)
        q_total = jnp.zeros((block, 128), F32)
        k_total = jnp.zeros((wide, 128), F32)
        v_total = jnp.zeros((wide, 128), F32)
        for side in range(2):
            mine = lane_low if side == 0 else ~lane_low
            key_mine = key_low if side == 0 else ~key_low
            q_mine = jnp.where(mine, queries, 0)
            g_mine = jnp.where(mine, grads, 0)
            row = pl.ds(pair * 2 + side, 1)
            log = jnp.where(near, log_own[row, rows], log_other[row, rows])
            probs = jnp.exp(dot(keys, q_mine, 1, 1) + (bias - log))
            prob_grad = dot(values, g_mine, 1, 1) - deltas[side : side + 1, :]
            score_grad = (probs * prob_grad).astype(BF)
            v_total = v_total + dot(probs.astype(BF), g_mine)
            k_total = k_total + dot(score_grad, q_mine)
            q_total = q_total + dot(score_grad, jnp.where(key_mine, keys * eighth, 0), 0, 0)
        low[pl.ds(begin, block), :128] = q_total.astype(BF)
        dk[pl.ds(start, wide), :] += k_total
        dv[pl.ds(start, wide), :] += v_total

    for_windows(ends, block, jnp.int32(0), jnp.int32(4), turn)
    low[:, 128:256] = dk[...].astype(BF)
    low[:, 256:] = dv[...].astype(BF)


def project_sum_kernel(
    place, st_own, st_other, low, ka, kb, sa, sb, rows, store, rows_t, row_sems, sems
):
    x = place[3]
    row_copies = [
        pltpu.make_async_copy(st_own, rows.at[x], row_sems.at[0]),
        pltpu.make_async_copy(st_other, rows.at[1 - x], row_sems.at[1]),
    ]
    for copy in row_copies:
        copy.start()
    wide = low.shape[1] // 3
    lane_rows = lax.broadcasted_iota(jnp.int32, (24, 128), 0)
    extra = jnp.zeros((24, 128), F32)
    for index in range(3):
        for kind in range(2):
            begin = index * wide + kind * 256
            sums = jnp.sum(low[:, begin : begin + 128].astype(F32), axis=0, keepdims=True)
            extra = jnp.where(lane_rows == kind * 3 + index, sums, extra)
    extra = jnp.concatenate([extra, extra], axis=0).astype(BF)
    store[:, :, 3 * wide :] = jnp.broadcast_to(extra[None], (16, 48, 128))
    for copy in row_copies:
        copy.wait()
    rows_t[...] = jnp.transpose(rows[...].reshape(2 * st_own.shape[0], st_own.shape[1]))
    for index in range(3):
        columns = slice(index * wide, (index + 1) * wide)
        store[:, :, columns] = dot(rows_t[...], low[:, columns]).astype(BF).reshape(16, 48, wide)
    copies = blocks_out(place, (ka, kb, sa, sb), store, sems, PAIR_FLIPS, 0)
    for copy in copies:
        copy.start()
    for copy in copies:
        copy.wait()


def states_sum_kernel(
    place, low, residual, a0, a1, a2, a3, states_out, states_send, store, sems
):
    x = place[3]
    copies = blocks_in(place, (a0, a1, a2, a3), store, sems, PAIR_FLIPS)
    for copy in copies:
        copy.start()
    for copy in copies:
        copy.wait()
    half = residual.shape[0]
    weight = store[:, :48, :].reshape(768, low.shape[1])

    def share(side):
        begin = pl.multiple_of(side * half, half)
        return dot(low[pl.ds(begin, half), :], weight, 1, 1)

    states_send[...] = share(1 - x).astype(BF)
    states_out[...] = residual[...] + share(x)


def swap(value, axis):
    return lax.ppermute(value, axis, [(0, 1), (1, 0)])


def hop(value, planes, bits):
    return lax.ppermute(value, DP, [(i, i ^ bits) for i in range(planes)])


def add32(*terms):
    return sum((term.astype(F32) for term in terms[1:]), terms[0].astype(F32))


def add(*terms):
    return add32(*terms).astype(BF)


def here():
    dp, c, x = lax.axis_index(DP), lax.axis_index(FSDP), lax.axis_index(SEQ)
    return lax.div(dp, 2), lax.rem(dp, 2), c, x, (dp * 2 + c) * 2 + x


def call(kernel, outs, inputs, specs, scratch, name, grid=()):
    return pl.pallas_call(
        lambda *refs: kernel(here(), *refs),
        out_shape=[jax.ShapeDtypeStruct(shape, kind) for shape, kind, _ in outs],
        in_specs=[spec_of(key) for key in specs],
        out_specs=[spec_of(key) for _, _, key in outs],
        scratch_shapes=scratch,
        grid=grid,
        compiler_params=pltpu.CompilerParams(vmem_limit_bytes=60 * MIB),
        cost_estimate=pl.CostEstimate(flops=0, bytes_accessed=0, transcendentals=0),
        name=name,
    )(*inputs)


def spec_of(key):
    return pl.BlockSpec(memory_space=SPACES[key]) if isinstance(key, str) else key


SPACES = {"s": pltpu.SMEM, "v": pltpu.VMEM, "a": pl.ANY}


def after(value, *others):
    return lax.optimization_barrier((value,) + others)[0]


class Order:
    def __init__(self, last):
        self.last = last

    def take(self, *values):
        values = lax.optimization_barrier(values + (self.last,))[:-1]
        return values if len(values) > 1 else values[0]

    def step(self, value):
        self.last = value
        return value


def column(rows, wide=128):
    return pl.BlockSpec((rows, wide), lambda step: (0, step))


def halves_body(
    states, deleted, crop_lengths,
    query_weight, query_bias, key_weight, value_weight, value_bias, output_weight, output_bias,
    attn_gain, attn_shift, inner_weight, inner_bias, outer_weight, outer_bias, final_gain,
    final_shift, cotangent, pool_cotangent,
):
    planes = 8
    count, width = states.shape[1:]
    half = width // 2
    hidden = inner_weight.shape[1]
    part = query_weight.shape[0]
    long = outer_weight.shape[0]
    crops = crop_lengths.shape[1]
    tall = 3 * half
    flat = width + hidden // 2
    dma = pltpu.SemaphoreType.DMA
    dp, c, x = lax.axis_index(DP), lax.axis_index(FSDP), lax.axis_index(SEQ)
    device = (dp * 2 + c) * 2 + x
    lens = crop_lengths[0]
    own = states[0]

    vectors = [
        vector[None]
        for vector in (
            query_bias, value_bias, output_bias, attn_gain, attn_shift, outer_bias, final_gain,
            final_shift, inner_bias,
        )
    ]
    send, keep, small, p1, p2 = call(
        pack_kernel,
        [
            ((part, tall + width + hidden), BF, "v"),
            ((part, tall), BF, "v"),
            ((16, width), BF, "v"),
            ((part, width + hidden), BF, "v"),
            ((long, width), BF, "v"),
        ],
        (query_weight, key_weight, value_weight, output_weight, inner_weight, outer_weight, *vectors),
        "v" * 15,
        [],
        "pack",
    )

    def pair_up(mine, theirs):
        return jnp.where(
            x == 0,
            jnp.concatenate([mine, theirs], axis=0),
            jnp.concatenate([theirs, mine], axis=0),
        )

    def along_z(block):
        return tuple(hop(block, planes, bits) for bits in (2, 4, 6))

    order = Order(p2)
    sent_2 = along_z(p2)
    del_other, from_x, small_x = order.take(swap(deleted, SEQ), swap(send, SEQ), swap(small, SEQ))
    tail = jnp.pad(add(small, small_x), ((0, 0), (0, tall - width)))
    both_a = jnp.concatenate([pair_up(keep, from_x[:, :tall]), tail], axis=0)
    both_1 = pair_up(p1[:, :flat], from_x[:, tall : tall + flat])
    both_b = pair_up(p1[:, flat:], from_x[:, tall + flat :])
    order.step(both_a)
    sent_a = along_z(both_a)
    order.step(both_b)
    other = swap(order.take(own), SEQ)
    quad_2 = order.step(jnp.stack([p2, *order.take(*sent_2)]))
    octet = hop(quad_2, planes, 1)
    quad_a = order.step(jnp.stack([both_a, *order.take(*sent_a)]))
    quad_ay = hop(quad_a, planes, 1)
    sent_1 = along_z(order.take(both_1))
    octet = order.step(jnp.concatenate([quad_2, order.take(octet)], axis=0))
    octet_x = swap(octet, SEQ)
    quad_ay, other = order.take(quad_ay, other)
    order.step(quad_ay)
    quad_1 = order.step(jnp.stack([both_1, *order.take(*sent_1)]))
    parts_a = order.take(swap(quad_a, FSDP), swap(quad_ay, FSDP))
    parts_a = (quad_a, quad_ay) + parts_a
    order.step(parts_a[-1])
    quad_1y = hop(quad_1, planes, 1)
    sent_b = along_z(after(both_b, quad_1))

    marks = (lens, deleted, del_other)
    queries, keys, values, mix_send, log_other, small = call(
        attend_kernel,
        [((2 * count, half), BF, "v")] * 3
        + [((count, half), BF, "v"), ((8, count), F32, "v"), ((16, width), F32, "v")],
        marks + (order.take(own), other) + parts_a,
        "svvaaaaaa",
        [
            pltpu.VMEM((16, 64, tall), BF),
            pltpu.VMEM((2, count, width), BF),
            pltpu.VMEM((1, 2 * count), jnp.int32),
            dma((16,)),
            dma((2,)),
        ],
        "attend",
    )
    order.step(mix_send)
    mix_other = swap(mix_send, SEQ)
    quad_1y = order.step(order.take(quad_1y))
    quad_b = order.step(jnp.stack([both_b, *order.take(*sent_b)]))
    quad_by = hop(quad_b, planes, 1)
    mix_own, log_own = call(
        attend_own_kernel,
        [((count, half), BF, "v"), ((8, count), F32, "v")],
        marks + (order.take(queries), keys, values),
        "svvvvv",
        [pltpu.VMEM((1, 2 * count), jnp.int32)],
        "attend_own",
    )
    order.step(mix_own)
    octet_x, mix_other = order.take(octet_x, mix_other)
    order.step(octet_x)
    parts_2 = (octet, octet_x, swap(octet, FSDP), swap(octet_x, FSDP))
    parts_1 = (quad_1, quad_1y, swap(quad_1, FSDP), swap(quad_1y, FSDP))
    quad_by = order.take(quad_by)
    parts_1 += (quad_b, quad_by, swap(quad_b, FSDP), swap(quad_by, FSDP))
    four = ((hidden // width, count, width), BF, "a")
    tokens = ((count, width), BF, "v")
    (
        output, pooled, residual, mg_own, mg_send, small_grad,
        active, inner_low, low, outer_low, branch_low,
    ) = call(
        feed_kernel,
        [
            tokens,
            ((crops, width), F32, "v"),
            ((count, width), F32, "v"),
            ((count, half), BF, "v"),
            ((count, half), BF, "v"),
            ((16, width), F32, "v"),
            four, four, tokens, tokens, tokens,
        ],
        marks
        + (own, mix_own, mix_other, small, cotangent[0], pool_cotangent[0])
        + parts_1
        + parts_2,
        "svvvvvvvv" + "a" * 12,
        [
            pltpu.VMEM((16, 2 * part, width + hidden), BF),
            pltpu.VMEM((32, long, width), BF),
            pltpu.VMEM((hidden // width, count, width), F32),
            pltpu.VMEM((count, width), F32),
            pltpu.VMEM((count, 1), F32),
            pltpu.VMEM((count, width), F32),
            pltpu.VMEM((count, width), F32),
            pltpu.VMEM((hidden // width, count, width), BF),
            pltpu.VMEM((hidden // width, count, width), BF),
            dma((32,)),
            dma((32,)),
            dma((2 * hidden // width,)),
        ],
        "feed",
    )
    mg_other = swap(mg_send, SEQ)

    blocks_2 = ((8, long, width), BF, "a")
    keep_2a, keep_2b, send_2a, send_2b = call(
        outer_sum_kernel,
        [blocks_2] * 4,
        (active, outer_low),
        [pl.BlockSpec((1, count, width), lambda step: (step, 0, 0)), "v"],
        [pltpu.VMEM((32, long, width), BF), dma((32,))],
        "outer_sum",
        (hidden // width,),
    )
    order.step(send_2b)
    mg_other = order.step(order.take(mg_other))
    core_2b = swap(order.take(send_2b), FSDP)
    blocks_a = ((4, 2 * part, flat), BF, "a")
    blocks_b = ((4, 2 * part, width + hidden - flat + 256), BF, "a")
    keep_1a, keep_1b, send_1a, send_1b, keep_3a, keep_3b, send_3a, send_3b = call(
        inner_sum_kernel,
        [blocks_a] * 4 + [blocks_b] * 4,
        (order.take(low), inner_low, branch_low, mix_own, mix_other, small_grad),
        "vvvvvv",
        [
            pltpu.VMEM((16, 2 * part, width + hidden + 256), BF),
            pltpu.VMEM((width, count), BF),
            pltpu.VMEM((2 * part, 256), F32),
            dma((80,)),
        ],
        "inner_sum",
    )
    order.step(send_1b)
    t1_2 = order.step(add(keep_2b, order.take(core_2b)))
    sum_2x = swap(t1_2, SEQ)
    t1_1 = order.step(add(keep_1b, order.take(swap(send_1b, FSDP))))
    sum_1y = hop(t1_1, planes, 1)
    t1_3 = order.step(add(keep_3b, order.take(swap(send_3b, FSDP))))
    sum_3y = hop(t1_3, planes, 1)
    core_2, core_1, core_3 = (
        swap(value, FSDP) for value in order.take(send_2a, send_1a, send_3a)
    )

    def split_x(v):
        v = v.reshape((2, part) + v.shape[1:])
        return jnp.where(x == 0, v[0], v[1]), jnp.where(x == 0, v[1], v[0])

    def to_z(u):
        return tuple(hop(u[index], planes, 2 * index) for index in (1, 2, 3))

    specs = ["s", "v", "v"] + [column(2 * count)] * 3 + [column(count)] * 4 + ["v", "v"]
    (lows,) = call(
        retreat_kernel,
        [((2 * count, tall), BF, column(2 * count, 384))],
        marks
        + (order.take(queries), keys, values)
        + (mg_own, mg_other, mix_own, mix_send, log_own, log_other),
        specs,
        [
            pltpu.VMEM((2 * count, 1), F32),
            pltpu.VMEM((2 * count, 128), F32),
            pltpu.VMEM((2 * count, 128), F32),
        ],
        "retreat",
        (half // 128,),
    )
    order.step(lows)
    u_1 = add(keep_1a, *order.take(core_1, sum_1y))
    order.step(u_1)
    sum_1z = to_z(u_1)
    u_2 = order.step(add(keep_2a, *order.take(core_2, sum_2x)))
    sum_2y = hop(u_2[4:], planes, 1)
    wide = tall + 128
    keep_a, keep_b, send_a, send_b = call(
        project_sum_kernel,
        [((4, 2 * part, wide), BF, "a")] * 4,
        (order.take(own), other, lows),
        "aav",
        [
            pltpu.VMEM((2, count, width), BF),
            pltpu.VMEM((16, 2 * part, wide), BF),
            pltpu.VMEM((width, 2 * count), BF),
            dma((2,)),
            dma((16,)),
        ],
        "project_sum",
    )
    order.step(send_b)
    core_b, core_a = swap(send_b, FSDP), swap(send_a, FSDP)
    u_3 = add(keep_3a, *order.take(core_3, sum_3y))
    order.step(u_3)
    sum_3z = to_z(u_3)
    t1_a = order.step(add(keep_b, order.take(core_b)))
    sum_ay = hop(t1_a, planes, 1)
    v_1 = order.step(add(u_1[0], *order.take(*sum_1z)))
    v_2 = add(u_2[:4], order.take(sum_2y))
    order.step(v_2)
    sum_2z = to_z(v_2)
    v_3 = order.step(add(u_3[0], *order.take(*sum_3z)))
    states_part, states_send = call(
        states_sum_kernel,
        [((count, width), F32, "v"), tokens],
        (order.take(lows), residual) + parts_a,
        "vvaaaa",
        [pltpu.VMEM((16, 64, tall), BF), dma((16,))],
        "states_sum",
    )
    order.step(states_send)
    states_x = swap(states_send, SEQ)
    pooled_x = swap(pooled, SEQ)
    grad_outer_weight = order.step(add32(v_2[0], *order.take(*sum_2z)))
    u_a = add(keep_a, *order.take(core_a, sum_ay))
    order.step(u_a)
    sum_az = to_z(u_a)
    small = v_3[:, width + hidden - flat :]
    small = jnp.concatenate([small[:part], small[part:]], axis=1)
    mine_1, theirs_1 = split_x(
        jnp.concatenate([v_1, v_3[:, : width + hidden - flat]], axis=1)
    )
    sent_1x = swap(jnp.concatenate([theirs_1, small], axis=1), SEQ)
    v = order.step(add(u_a[0], *order.take(*sum_az)))
    mine_a, theirs_a = split_x(v)
    sent_ax = swap(theirs_a, SEQ)
    pooled = pooled + order.take(pooled_x)
    states_grad = order.step(add32(states_part, order.take(states_x)))
    sent_1x = order.take(sent_1x)
    total = mine_1.astype(F32) + sent_1x[:, : width + hidden].astype(F32)
    grad_output_weight, grad_inner_weight = total[:, :width], total[:, width:]
    small = small.astype(F32) + sent_1x[:, width + hidden :].astype(F32)
    small = jnp.concatenate([small[:, :256], small[:, 256:]], axis=0)
    smalls = small[:36].reshape(12, width)
    theirs = order.take(sent_ax)
    left = jnp.where(x == 0, mine_a, theirs).astype(F32)
    right = jnp.where(x == 0, theirs, mine_a).astype(F32)

    def gathered(index):
        columns = [
            side[:, (pair * 3 + index) * 128 : (pair * 3 + index + 1) * 128]
            for side in (left, right)
            for pair in range(half // 128)
        ]
        return jnp.concatenate(columns, axis=1)

    grad_query_weight, grad_key_weight, grad_value_weight = (gathered(i) for i in range(3))
    bias_grads = jnp.stack([left[:6, tall:], right[:6, tall:]]).reshape(2, 2, half)
    bias_grads = jnp.transpose(bias_grads, (1, 0, 2)).reshape(2, width)
    vectors = lax.dynamic_slice(smalls[:8], (0, device * part), (8, part))
    bias_grads = lax.dynamic_slice(bias_grads, (0, device * part), (2, part))
    grad_inner_bias = lax.dynamic_slice(
        smalls[8:12].reshape(hidden), (device * long,), (long,)
    )
    return (
        output[None],
        pooled[None],
        states_grad[None],
        grad_query_weight,
        bias_grads[0],
        grad_key_weight,
        grad_value_weight,
        bias_grads[1],
        grad_output_weight,
        vectors[2],
        vectors[3],
        vectors[4],
        grad_inner_weight,
        grad_inner_bias,
        grad_outer_weight,
        vectors[5],
        vectors[6],
        vectors[7],
    )


def solution(mesh):
    in_specs = (
        P(ROWS, SEQ, None),
        P(ROWS, SEQ),
        P(ROWS, None),
        BY_ROW,
        FLAT,
        BY_ROW,
        BY_ROW,
        FLAT,
        BY_ROW,
        FLAT,
        FLAT,
        FLAT,
        BY_ROW,
        FLAT,
        BY_ROW,
        FLAT,
        FLAT,
        FLAT,
        P(ROWS, SEQ, None),
        P(ROWS, None, None),
    )
    out_specs = (
        P(ROWS, SEQ, None),
        P(ROWS, None, None),
        P(ROWS, SEQ, None),
        BY_ROW,
        FLAT,
        BY_ROW,
        BY_ROW,
        FLAT,
        BY_ROW,
        FLAT,
        FLAT,
        FLAT,
        BY_ROW,
        FLAT,
        BY_ROW,
        FLAT,
        FLAT,
        FLAT,
    )
    shape = mesh.shape
    halves = (shape[DP], shape[FSDP], shape[SEQ]) == (8, 2, 2)
    chosen = halves_body if halves else body
    return jax.shard_map(chosen, mesh=mesh, in_specs=in_specs, out_specs=out_specs, check_vma=False)
```

```python
from functools import partial

import jax
import jax.numpy as jnp
from jax import lax
from jax.experimental import pallas as pl
from jax.experimental.pallas import tpu as pltpu
from jax.sharding import PartitionSpec as P

HEADS = 12
HEAD = 64


highest = lax.Precision.HIGHEST
DP, FSDP, SEQ = "dp", "fsdp", "seq"
EVERY = (DP, FSDP, SEQ)
BY_ROW, FLAT = P(EVERY, None), P(EVERY)
ROWS = (DP, FSDP)


def layer_norm(values, gain, shift):
    centered = values - jnp.mean(values, axis=-1, keepdims=True)
    spread = jnp.mean(centered * centered, axis=-1, keepdims=True)
    return centered * lax.rsqrt(spread + 1e-06) * gain + shift


def crop_layout(lengths, deleted, places):
    crop_ends = jnp.cumsum(lengths, axis=-1, dtype=jnp.int32)
    segment = jnp.sum(
        (places[..., :, None] >= crop_ends[..., None, :]).astype(jnp.int32),
        axis=-1,
        dtype=jnp.int32,
    )
    retained = (deleted == 0) & (segment < lengths.shape[-1])
    key_tag = jnp.where(retained, segment, -1)
    return (segment, retained, key_tag)


def product(left, right):
    return jnp.dot(left, right, preferred_element_type=jnp.float32)


def column_sum(values):
    return jnp.sum(values.astype(jnp.float32), axis=0)


def sweep(carry, pieces, inner):
    count = pieces[0].shape[1]
    width = 256

    def turn(index, totals):
        offset = index * width
        parts = tuple((lax.dynamic_slice_in_dim(piece, offset, width, 1) for piece in pieces))
        return inner(totals, parts, offset)

    return lax.fori_loop(0, count // width, turn, carry)


def scores_at(query_part, key_part):
    return (
        jnp.einsum("rqhd,rkhd->rhqk", query_part, key_part, preferred_element_type=jnp.float32)
        * 0.125
    )


def allowed_at(query_tag, query_place, tags, begin):
    key_place = begin + jnp.arange(tags.shape[1], dtype=jnp.int32)
    same = tags[:, None, :] == query_tag[:, :, None]
    itself = key_place[None, None, :] == query_place[None, :, None]
    return (same | itself)[:, None]


def probs_at(raw, allowed, log_part):
    return jnp.where(allowed, jnp.exp(raw - log_part[..., None]), 0.0)


def body(
    states,
    deleted,
    crop_lengths,
    query_weight,
    query_bias,
    key_weight,
    value_weight,
    value_bias,
    output_weight,
    output_bias,
    attn_gain,
    attn_shift,
    inner_weight,
    inner_bias,
    outer_weight,
    outer_bias,
    final_gain,
    final_shift,
    cotangent,
    pool_cotangent,
):
    rows, shard, width = states.shape
    lowered = [
        master.astype(jnp.bfloat16)
        for master in (
            query_weight,
            query_bias,
            key_weight,
            value_weight,
            value_bias,
            output_weight,
            output_bias,
            attn_gain,
            attn_shift,
            inner_weight,
            inner_bias,
            outer_weight,
            outer_bias,
            final_gain,
            final_shift,
        )
    ]
    (
        w_query,
        b_query,
        w_key,
        w_value,
        b_value,
        w_out,
        b_out,
        g_attn,
        s_attn,
        w_inner,
        b_inner,
        w_outer,
        b_outer,
        g_final,
        s_final,
    ) = (
        lax.all_gather(lowered[0], EVERY, axis=0, tiled=True),
        lax.all_gather(lowered[1], EVERY, axis=0, tiled=True),
        lax.all_gather(lowered[2], EVERY, axis=0, tiled=True),
        lax.all_gather(lowered[3], EVERY, axis=0, tiled=True),
        lax.all_gather(lowered[4], EVERY, axis=0, tiled=True),
        lax.all_gather(lowered[5], EVERY, axis=0, tiled=True),
        lax.all_gather(lowered[6], EVERY, axis=0, tiled=True),
        lax.all_gather(lowered[7], EVERY, axis=0, tiled=True),
        lax.all_gather(lowered[8], EVERY, axis=0, tiled=True),
        lax.all_gather(lowered[9], EVERY, axis=0, tiled=True),
        lax.all_gather(lowered[10], EVERY, axis=0, tiled=True),
        lax.all_gather(lowered[11], EVERY, axis=0, tiled=True),
        lax.all_gather(lowered[12], EVERY, axis=0, tiled=True),
        lax.all_gather(lowered[13], EVERY, axis=0, tiled=True),
        lax.all_gather(lowered[14], EVERY, axis=0, tiled=True),
    )
    own_start = lax.axis_index(SEQ) * shard
    places = own_start + jnp.arange(shard, dtype=jnp.int32)
    segment, retained, key_tag = crop_layout(crop_lengths, deleted, places)
    flat = states.reshape(rows * shard, width)
    split = (rows, shard, HEADS, HEAD)
    queries = (product(flat, w_query) + b_query).astype(jnp.bfloat16).reshape(split)
    keys = product(flat, w_key).astype(jnp.bfloat16).reshape(split)
    values = (product(flat, w_value) + b_value).astype(jnp.bfloat16).reshape(split)

    def scale_step(totals, parts, begin):
        top, total = totals
        key_part, tags = parts
        allowed = allowed_at(segment, places, tags, begin)
        masked = jnp.where(allowed, scores_at(queries, key_part), -1e30)
        new_top = jnp.maximum(top, jnp.max(masked, axis=-1))
        raised = jnp.where(allowed, jnp.exp(masked - new_top[..., None]), 0.0)
        return (new_top, total * jnp.exp(top - new_top) + jnp.sum(raised, axis=-1))

    stat_shape = (rows, HEADS, shard)
    scale_init = (jnp.full(stat_shape, -1e30, jnp.float32), jnp.zeros(stat_shape, jnp.float32))
    top, total = sweep(
        scale_init,
        (
            lax.all_gather(keys, SEQ, axis=1, tiled=True),
            lax.all_gather(key_tag, SEQ, axis=1, tiled=True),
        ),
        inner=scale_step,
    )
    log_total = top + jnp.log(total)

    def mix_step(totals, parts, begin):
        coarse, fine = totals
        key_part, value_part, tags = parts
        probs = probs_at(
            scores_at(queries, key_part), allowed_at(segment, places, tags, begin), log_total
        )
        probs_low = probs.astype(jnp.bfloat16)
        rest = (probs - probs_low.astype(jnp.float32)).astype(jnp.bfloat16)
        coarse = coarse + jnp.einsum(
            "rhqk,rkhd->rqhd", probs_low, value_part, preferred_element_type=jnp.float32
        )
        fine = fine + jnp.einsum(
            "rhqk,rkhd->rqhd", rest, value_part, preferred_element_type=jnp.float32
        )
        return (coarse, fine)

    empty = jnp.zeros(split, jnp.float32)
    coarse, fine = sweep(
        (empty, empty),
        (
            lax.all_gather(keys, SEQ, axis=1, tiled=True),
            lax.all_gather(values, SEQ, axis=1, tiled=True),
            lax.all_gather(key_tag, SEQ, axis=1, tiled=True),
        ),
        inner=mix_step,
    )
    attended = coarse.astype(jnp.bfloat16).reshape(rows * shard, width)
    branch = product(attended, w_out) + b_out
    residual = states.astype(jnp.float32).reshape(rows * shard, width) + branch
    normed, attn_back = jax.vjp(
        layer_norm, residual, g_attn.astype(jnp.float32), s_attn.astype(jnp.float32)
    )
    normed_low = normed.astype(jnp.bfloat16)
    inner = product(normed_low, w_inner) + b_inner
    active_full, gelu_back = jax.vjp(partial(jax.nn.gelu, approximate=False), inner)
    active = active_full.astype(jnp.bfloat16)
    outer = product(active, w_outer) + b_outer
    result, final_back = jax.vjp(
        layer_norm, normed + outer, g_final.astype(jnp.float32), s_final.astype(jnp.float32)
    )
    output = result.astype(jnp.bfloat16).reshape(rows, shard, width)
    crops = crop_lengths.shape[1]
    member = (
        (segment[..., None] == jnp.arange(crops, dtype=jnp.int32)) & retained[..., None]
    ).astype(jnp.float32)
    partial_sums = jnp.einsum(
        "rnc,rnd->rcd",
        member,
        result.reshape(rows, shard, width),
        precision=highest,
        preferred_element_type=jnp.float32,
    )
    sums, counts = lax.psum((partial_sums, jnp.sum(member, axis=1)), SEQ)
    divisor = jnp.maximum(counts, 1.0)[..., None]
    pooled = sums / divisor
    w_query, w_key, w_value, w_out, w_inner, w_outer = (
        lax.all_gather(lowered[0], EVERY, axis=0, tiled=True),
        lax.all_gather(lowered[2], EVERY, axis=0, tiled=True),
        lax.all_gather(lowered[3], EVERY, axis=0, tiled=True),
        lax.all_gather(lowered[5], EVERY, axis=0, tiled=True),
        lax.all_gather(lowered[9], EVERY, axis=0, tiled=True),
        lax.all_gather(lowered[11], EVERY, axis=0, tiled=True),
    )
    result_grad = cotangent.astype(jnp.float32) + jnp.einsum(
        "rnc,rcd->rnd",
        member,
        pool_cotangent / divisor,
        precision=highest,
        preferred_element_type=jnp.float32,
    )
    sum_grad, grad_final_gain, grad_final_shift = final_back(
        result_grad.reshape(rows * shard, width)
    )
    outer_grad = sum_grad.astype(jnp.bfloat16)
    grad_outer_bias = column_sum(outer_grad)
    grad_outer_weight = product(active.T, outer_grad)
    inner_grad = gelu_back(product(outer_grad, w_outer.T))[0].astype(jnp.bfloat16)
    grad_inner_bias = column_sum(inner_grad)
    grad_inner_weight = product(normed_low.T, inner_grad)
    normed_grad = sum_grad + product(inner_grad, w_inner.T)
    residual_grad, grad_attn_gain, grad_attn_shift = attn_back(normed_grad)
    branch_grad = residual_grad.astype(jnp.bfloat16)
    grad_output_bias = column_sum(branch_grad)
    grad_output_weight = product(attended.T, branch_grad)
    mixed_grad = product(branch_grad, w_out.T).astype(jnp.bfloat16).reshape(split)
    delta = jnp.sum(mixed_grad.astype(jnp.float32) * (coarse + fine), axis=-1)
    delta_local = jnp.transpose(delta, (0, 2, 1))
    all_log, all_delta = (
        lax.all_gather(jnp.transpose(log_total, (0, 2, 1)), SEQ, axis=1, tiled=True),
        lax.all_gather(delta, SEQ, axis=1, tiled=True),
    )

    def key_side(totals, parts, begin):
        key_grad, value_grad = totals
        query_part, grad_part, tags_part = parts
        count = tags_part.shape[1]
        log_part = jnp.transpose(lax.dynamic_slice_in_dim(all_log, begin, count, 1), (0, 2, 1))
        delta_part = jnp.transpose(lax.dynamic_slice_in_dim(all_delta, begin, count, 1), (0, 2, 1))
        query_place = begin + jnp.arange(count, dtype=jnp.int32)
        allowed = allowed_at(tags_part, query_place, key_tag, own_start)
        probs = probs_at(scores_at(query_part, keys), allowed, log_part)
        value_grad = value_grad + jnp.einsum(
            "rhqk,rqhd->rkhd",
            probs.astype(jnp.bfloat16),
            grad_part,
            preferred_element_type=jnp.float32,
        )
        prob_grad = jnp.einsum(
            "rqhd,rkhd->rhqk", grad_part, values, preferred_element_type=jnp.float32
        )
        score_grad = (probs * (prob_grad - delta_part[..., None]) * 0.125).astype(jnp.bfloat16)
        key_grad = key_grad + jnp.einsum(
            "rhqk,rqhd->rkhd", score_grad, query_part, preferred_element_type=jnp.float32
        )
        return (key_grad, value_grad)

    key_grad, value_grad = sweep(
        (empty, empty),
        (
            lax.all_gather(queries, SEQ, axis=1, tiled=True),
            lax.all_gather(mixed_grad, SEQ, axis=1, tiled=True),
            lax.all_gather(segment, SEQ, axis=1, tiled=True),
        ),
        inner=key_side,
    )

    def query_side(query_grad, parts, begin):
        key_part, value_part, tags = parts
        probs = probs_at(
            scores_at(queries, key_part), allowed_at(segment, places, tags, begin), log_total
        )
        prob_grad = jnp.einsum(
            "rqhd,rkhd->rhqk", mixed_grad, value_part, preferred_element_type=jnp.float32
        )
        score_grad = (probs * (prob_grad - delta_local[..., None]) * 0.125).astype(jnp.bfloat16)
        return query_grad + jnp.einsum(
            "rhqk,rkhd->rqhd", score_grad, key_part, preferred_element_type=jnp.float32
        )

    query_grad = sweep(
        empty,
        (
            lax.all_gather(keys, SEQ, axis=1, tiled=True),
            lax.all_gather(values, SEQ, axis=1, tiled=True),
            lax.all_gather(key_tag, SEQ, axis=1, tiled=True),
        ),
        inner=query_side,
    )
    query_low = query_grad.astype(jnp.bfloat16).reshape(rows * shard, width)
    key_low = key_grad.astype(jnp.bfloat16).reshape(rows * shard, width)
    value_low = value_grad.astype(jnp.bfloat16).reshape(rows * shard, width)
    grad_query_weight = product(flat.T, query_low)
    grad_query_bias = column_sum(query_low)
    grad_key_weight = product(flat.T, key_low)
    grad_value_weight = product(flat.T, value_low)
    grad_value_bias = column_sum(value_low)
    states_grad = (
        residual_grad
        + product(query_low, w_query.T)
        + product(key_low, w_key.T)
        + product(value_low, w_value.T)
    ).reshape(rows, shard, width)
    summed = (
        lax.psum_scatter(grad_query_weight, EVERY, scatter_dimension=0, tiled=True),
        lax.psum_scatter(grad_query_bias, EVERY, scatter_dimension=0, tiled=True),
        lax.psum_scatter(grad_key_weight, EVERY, scatter_dimension=0, tiled=True),
        lax.psum_scatter(grad_value_weight, EVERY, scatter_dimension=0, tiled=True),
        lax.psum_scatter(grad_value_bias, EVERY, scatter_dimension=0, tiled=True),
        lax.psum_scatter(
            grad_output_weight, EVERY, scatter_dimension=0, tiled=True
        ),
        lax.psum_scatter(grad_output_bias, EVERY, scatter_dimension=0, tiled=True),
        lax.psum_scatter(grad_attn_gain, EVERY, scatter_dimension=0, tiled=True),
        lax.psum_scatter(grad_attn_shift, EVERY, scatter_dimension=0, tiled=True),
        lax.psum_scatter(grad_inner_weight, EVERY, scatter_dimension=0, tiled=True),
        lax.psum_scatter(grad_inner_bias, EVERY, scatter_dimension=0, tiled=True),
        lax.psum_scatter(grad_outer_weight, EVERY, scatter_dimension=0, tiled=True),
        lax.psum_scatter(grad_outer_bias, EVERY, scatter_dimension=0, tiled=True),
        lax.psum_scatter(grad_final_gain, EVERY, scatter_dimension=0, tiled=True),
        lax.psum_scatter(grad_final_shift, EVERY, scatter_dimension=0, tiled=True),
    )
    return (output, pooled, states_grad) + tuple(summed)


BF = jnp.bfloat16
F32 = jnp.float32
MIB = 1 << 20


def dot(left, right, left_dim=1, right_dim=0):
    return lax.dot_general(
        left,
        right,
        (((left_dim,), (right_dim,)), ((), ())),
        preferred_element_type=F32,
    )


def exact_dot(left, right, left_dim=1, right_dim=0):
    return lax.dot_general(
        left,
        right,
        (((left_dim,), (right_dim,)), ((), ())),
        precision=highest,
        preferred_element_type=F32,
    )


def crop_ends_of(lens_ref):
    ends, total = [], jnp.int32(0)
    for slot in range(lens_ref.shape[0]):
        total = total + lens_ref[slot]
        ends.append(total)
    return ends


def segment_of(ends, places):
    segment = jnp.zeros(places.shape, jnp.int32)
    for end in ends:
        segment = segment + (places >= end).astype(jnp.int32)
    return segment


def for_windows(ends, block, first, last, turn):
    begin = ends[0] * 0
    for end in ends:
        begin = jnp.maximum(begin, jnp.where(end <= 2 * block, end, 0))
    single = (begin < block).astype(jnp.int32)

    def three(index, carry):
        start = jnp.where(index == 2, 1 - single, 0) * block
        turn(index, pl.multiple_of(start, block), 3)
        return carry

    def two(index, carry):
        start = jnp.where(index == 0, 0, 2) * block
        turn(index, pl.multiple_of(start, block), 2)
        return carry

    def one(index, carry):
        turn(index, pl.multiple_of(index * block, block), 1)
        return carry

    low = jnp.maximum(first, 1 - single)
    lax.fori_loop(low, jnp.minimum(last, 3), three, 0)
    lax.fori_loop(first, jnp.where((first == 0) & (single == 0), 1, first), two, 0)
    final = jnp.where(last == 4, 1, 0)
    lax.fori_loop(3, 3 + final * (1 - single), two, 0)
    lax.fori_loop(3, 3 + final * single, one, 0)


def pack_kernel(
    place, wq, wk, wv, wo, w1, w2, v0, v1, v2, v3, v4, v5, v6, v7, v96,
    send, keep, small, p1, p2,
):
    x = place[3]
    device = place[4]
    half = wq.shape[1] // 2
    for pair in range(half // 128):
        for index, ref in enumerate((wq, wk, wv)):
            left = ref[:, pair * 128 : pair * 128 + 128].astype(BF)
            right = ref[:, half + pair * 128 : half + pair * 128 + 128].astype(BF)
            begin = (pair * 3 + index) * 128
            keep[:, begin : begin + 128] = jnp.where(x == 0, left, right)
            send[:, begin : begin + 128] = jnp.where(x == 0, right, left)
    width = wo.shape[1]
    tall = keep.shape[1]
    for ref, begin in ((send, tall), (p1, 0)):
        ref[:, begin : begin + width] = wo[...].astype(BF)
        ref[:, begin + width :] = w1[...].astype(BF)
    p2[...] = w2[...].astype(BF)
    part = v0.shape[1]
    row = lax.broadcasted_iota(jnp.int32, (8, part), 0)
    stacked = jnp.zeros((8, part), F32)
    for index, ref in enumerate((v0, v1, v2, v3, v4, v5, v6, v7)):
        stacked = jnp.where(row == index, ref[...], stacked)
    row = lax.broadcasted_iota(jnp.int32, (part, width), 0)
    lane = lax.broadcasted_iota(jnp.int32, (part, width), 1)
    spread = (row + device * part == lane).astype(BF)
    first = dot(stacked.astype(BF), spread)
    part = v96.shape[1]
    row = lax.broadcasted_iota(jnp.int32, (part, width), 0)
    lane = lax.broadcasted_iota(jnp.int32, (part, width), 1)
    rows = []
    for index in range(8):
        if index < v96.shape[1] * 32 // width:
            spread = (row + device * part == lane + index * width).astype(BF)
            rows.append(dot(jnp.broadcast_to(v96[...], (8, part)).astype(BF), spread))
    tall = lax.broadcasted_iota(jnp.int32, (8, width), 0)
    second = jnp.zeros((8, width), F32)
    for index, value in enumerate(rows):
        second = jnp.where(tall == index, value[:1], second)
    small[...] = jnp.concatenate([first, second], axis=0).astype(BF)


def blocks_in(place, parts, store, sems, flips, first=0):
    copies = []
    for part, (ref, offset) in enumerate(zip(parts, flips, strict=True)):
        for slot in range(ref.shape[0]):
            spot = slot_place(place, offset, slot)
            copies.append(
                pltpu.make_async_copy(
                    ref.at[slot], store.at[spot], sems.at[first + part * ref.shape[0] + slot]
                )
            )
    return copies


def xor(value, bits):
    if bits & 1:
        value = value + 1 - 2 * lax.rem(value, 2)
    if bits & 2:
        value = lax.rem(value + 2, 4)
    return value


def slot_place(place, flip, slot):
    flip_y, flip_c, flip_x = flip
    z = xor(place[0], slot % 4)
    y = xor(place[1], flip_y ^ (slot // 4))
    c = xor(place[2], flip_c)
    spot = (z * 2 + y) * 2 + c
    if flip_x is None:
        return spot
    return spot * 2 + xor(place[3], flip_x)


PAIR_FLIPS = ((0, 0, None), (1, 0, None), (0, 1, None), (1, 1, None))
FULL_FLIPS = ((0, 0, 0), (0, 0, 1), (0, 1, 0), (0, 1, 1))


def tag_row(ends, x, own, other):
    half = own.shape[1]
    parts = []
    for index in range(2):
        deleted = jnp.where(x == index, own[...], other[...])
        places = index * half + lax.broadcasted_iota(jnp.int32, (1, half), 1)
        segment = segment_of(ends, places)
        parts.append(jnp.where((deleted == 0) & (segment < len(ends)), segment, -1))
    return parts


def attend_block(ends, tags, q_ref, k_ref, v_ref, index, block, start, wide):
    wide = wide * block
    lane_low = lax.broadcasted_iota(jnp.int32, (block, 128), 1) < 64
    key_low = lax.broadcasted_iota(jnp.int32, (wide, 128), 1) < 64
    begin = pl.multiple_of(index * block, block)
    places = begin + lax.broadcasted_iota(jnp.int32, (block, 1), 0)
    key_places = start + lax.broadcasted_iota(jnp.int32, (1, wide), 1)
    allowed = (tags[0:1, pl.ds(start, wide)] == segment_of(ends, places)) | (key_places == places)
    bias = jnp.where(allowed, 0.0, -1e30)
    outs = []
    lanes = lax.broadcasted_iota(jnp.int32, (block, 128), 1)
    logs = jnp.zeros((block, 128), F32)
    for pair in range(q_ref.shape[1] // 128):
        columns = slice(pair * 128, pair * 128 + 128)
        queries = q_ref[pl.ds(begin, block), columns] * jnp.asarray(0.125, BF)
        keys = k_ref[pl.ds(start, wide), columns]
        values = v_ref[pl.ds(start, wide), columns]
        total = jnp.zeros((block, 128), F32)
        for side in range(2):
            mine = lane_low if side == 0 else ~lane_low
            key_mine = key_low if side == 0 else ~key_low
            scores = dot(jnp.where(mine, queries, 0), keys, 1, 1) + bias
            top = jnp.max(scores, axis=1, keepdims=True)
            raised = jnp.exp(scores - top)
            amount = jnp.sum(raised, axis=1, keepdims=True)
            probs = (raised * (1.0 / amount)).astype(BF)
            total = total + dot(probs, jnp.where(key_mine, values, 0))
            logs = jnp.where(lanes == pair * 2 + side, top + jnp.log(amount), logs)
        outs.append(total.astype(BF))
    return jnp.concatenate(outs, axis=1), jnp.transpose(logs)[:8]


def attend_half(ends, tags, q_ref, k_ref, v_ref, side, out, logs):
    block = out.shape[0] // 2

    def turn(index, start, wide):
        spot = pl.multiple_of((index - side * 2) * block, block)
        mixed, rows = attend_block(ends, tags, q_ref, k_ref, v_ref, index, block, start, wide)
        out[pl.ds(spot, block), :] = mixed
        logs[:, pl.ds(spot, block)] = rows

    for_windows(ends, block, side * 2, side * 2 + 2, turn)


def fill_tags(ends, x, del_own, del_other, tags):
    half = del_own.shape[1]
    for index, part in enumerate(tag_row(ends, x, del_own, del_other)):
        tags[0:1, index * half : (index + 1) * half] = part


def attend_kernel(
    place, lens, del_own, del_other, st_own, st_other, a0, a1, a2, a3,
    q_out, k_out, v_out, mixed, logs, small_out,
    store, rows, tags, sems, row_sems,
):
    x = place[3]
    copies = blocks_in(place, (a0, a1, a2, a3), store, sems, PAIR_FLIPS)
    for copy in copies:
        copy.start()
    own_copy = pltpu.make_async_copy(st_own, rows.at[x], row_sems.at[0])
    other_copy = pltpu.make_async_copy(st_other, rows.at[1 - x], row_sems.at[1])
    own_copy.start()
    other_copy.start()
    ends = crop_ends_of(lens)
    half = del_own.shape[1]
    fill_tags(ends, x, del_own, del_other, tags)
    for copy in copies:
        copy.wait()
    own_copy.wait()
    other_copy.wait()

    depth = store.shape[2] // 3
    small_out[...] = jnp.sum(store[:, 48:, :768].astype(F32), axis=0)
    split = pl.multiple_of(x * depth, depth)
    bias_q = small_out[0:1, pl.ds(split, depth)]
    bias_v = small_out[1:2, pl.ds(split, depth)]
    weight = store[:, :48, :].reshape(768, 3 * depth)

    def project(index, carry):
        begin = pl.multiple_of(index * half, half)
        product_ = dot(rows[index], weight)
        for pair in range(depth // 128):
            columns = slice(pair * 128, pair * 128 + 128)
            at = pair * 384
            q_out[pl.ds(begin, half), columns] = (
                product_[:, at : at + 128] + bias_q[:, columns]
            ).astype(BF)
            k_out[pl.ds(begin, half), columns] = product_[:, at + 128 : at + 256].astype(BF)
            v_out[pl.ds(begin, half), columns] = (
                product_[:, at + 256 : at + 384] + bias_v[:, columns]
            ).astype(BF)
        return carry

    lax.fori_loop(0, 2, project, 0)
    attend_half(ends, tags, q_out, k_out, v_out, 1 - x, mixed, logs)


def attend_own_kernel(place, lens, del_own, del_other, q_in, k_in, v_in, mixed, logs, tags):
    x = place[3]
    ends = crop_ends_of(lens)
    fill_tags(ends, x, del_own, del_other, tags)
    attend_half(ends, tags, q_in, k_in, v_in, x, mixed, logs)


def norm_parts(values):
    centered = values - jnp.mean(values, axis=-1, keepdims=True)
    spread = jnp.mean(centered * centered, axis=-1, keepdims=True)
    scale = lax.rsqrt(spread + 1e-06)
    return centered * scale, scale


def norm_back(grad, gain, unit, scale):
    lifted = grad * gain
    return scale * (
        lifted
        - jnp.mean(lifted, axis=-1, keepdims=True)
        - unit * jnp.mean(lifted * unit, axis=-1, keepdims=True)
    )


def gelu_parts(inner):
    phi = 0.5 * (1.0 + lax.erf(inner * 0.7071067811865476))
    density = jnp.exp(inner * inner * -0.5) * 0.3989422804014327
    return inner * phi, phi + inner * density


def feed_kernel(
    place, lens, del_own, del_other, states, mix_own, mix_other, small, cot, pool_cot,
    p0, p1, p2, p3, r0, r1, r2, r3, f0, f1, f2, f3,
    output, pooled, residual_out, mg_own, mg_other, small_out, active, inner_low, low, outer_low, branch_low,
    w1, w2, slope, unit_a, scale_a, outer, grad, acts, inners, sems1, sems2, sems_o,
):
    x = place[3]
    width = states.shape[1]
    count = states.shape[0]
    hidden = 4 * width
    part = width
    flat = p0.shape[2]
    in1 = blocks_in(place, (p0, p1, p2, p3), w1.at[:, :, :flat], sems1, PAIR_FLIPS)
    in1 += blocks_in(place, (r0, r1, r2, r3), w1.at[:, :, flat:], sems1, PAIR_FLIPS, 16)
    in2 = blocks_in(place, (f0, f1, f2, f3), w2, sems2, FULL_FLIPS)
    for copy in in1 + in2:
        copy.start()
    ends = crop_ends_of(lens)
    tags = tag_row(ends, x, del_own, del_other)
    slots = lax.broadcasted_iota(jnp.int32, (len(ends), count), 0)
    members = [(tag == slots).astype(F32) for tag in tags]
    counts = sum(jnp.sum(member, axis=1, keepdims=True) for member in members)
    divisor = jnp.maximum(counts, 1.0)
    member = jnp.where(x == 0, members[0], members[1])
    for copy in in1:
        copy.wait()

    def out_weight(side):
        return w1[pl.ds(side * 8, 8), :, :width].reshape(width // 2, width)

    branch = dot(mix_own[...], out_weight(x)) + dot(mix_other[...], out_weight(1 - x))
    branch = branch + small[2:3, :]
    unit, scale = norm_parts(states[...].astype(F32) + branch)
    unit_a[...] = unit
    scale_a[...] = scale
    value = unit * small[3:4, :] + small[4:5, :]
    low[...] = value.astype(BF)
    outer[...] = value + small[5:6, :]
    for copy in in2:
        copy.wait()

    def leave(here, there, index, sem):
        return pltpu.make_async_copy(here.at[index], there.at[index], sems_o.at[sem])

    def ahead(index, carry):
        begin = pl.multiple_of(index * part, part)
        weight = w1[:, :, pl.ds(width + begin, part)].reshape(width, part)
        inner = dot(low[...], weight) + small[pl.ds(8 + index, 1), :]
        act, bend = gelu_parts(inner)
        act = act.astype(BF)
        acts[index] = act
        leave(acts, active, index, index).start()
        slope[index] = bend
        outer[...] += dot(act, w2[pl.ds(index * 8, 8)].reshape(part, width))
        return carry

    lax.fori_loop(0, hidden // part, ahead, 0)

    unit, scale = norm_parts(outer[...])
    result = unit * small[6:7, :] + small[7:8, :]
    output[...] = result.astype(BF)
    pooled[...] = exact_dot(member, result) / divisor
    grad_in = cot[...].astype(F32) + exact_dot(member, pool_cot[...] / divisor, 0, 0)
    small_out[0:2, :] = jnp.zeros((2, width), F32)
    small_out[12:16, :] = jnp.zeros((4, width), F32)
    small_out[6:7, :] = jnp.sum(grad_in * unit, axis=0, keepdims=True)
    small_out[7:8, :] = jnp.sum(grad_in, axis=0, keepdims=True)
    total = norm_back(grad_in, small[6:7, :], unit, scale)
    grad[...] = total
    outer_low[...] = total.astype(BF)
    small_out[5:6, :] = jnp.sum(outer_low[...].astype(F32), axis=0, keepdims=True)

    def back(index, carry):
        begin = pl.multiple_of(index * part, part)
        weight = w2[pl.ds(index * 8, 8)].reshape(part, width)
        inner = (dot(outer_low[...], weight, 1, 1) * slope[index]).astype(BF)
        inners[index] = inner
        leave(inners, inner_low, index, hidden // part + index).start()
        small_out[pl.ds(8 + index, 1), :] = jnp.sum(inner.astype(F32), axis=0, keepdims=True)
        weight = w1[:, :, pl.ds(width + begin, part)].reshape(width, part)
        grad[...] += dot(inner, weight, 1, 1)
        return carry

    lax.fori_loop(0, hidden // part, back, 0)

    total = grad[...]
    unit = unit_a[...]
    small_out[3:4, :] = jnp.sum(total * unit, axis=0, keepdims=True)
    small_out[4:5, :] = jnp.sum(total, axis=0, keepdims=True)
    residual = norm_back(total, small[3:4, :], unit, scale_a[...])
    residual_out[...] = residual
    branch_low[...] = residual.astype(BF)
    small_out[2:3, :] = jnp.sum(branch_low[...].astype(F32), axis=0, keepdims=True)
    mg_own[...] = dot(branch_low[...], out_weight(x), 1, 1).astype(BF)
    mg_other[...] = dot(branch_low[...], out_weight(1 - x), 1, 1).astype(BF)
    for index in range(hidden // part):
        leave(acts, active, index, index).wait()
        leave(inners, inner_low, index, hidden // part + index).wait()


def outer_sum_kernel(place, active, outer_low, ka, kb, sa, sb, store, sems):
    step = pl.program_id(0)
    width = outer_low.shape[1]
    product_ = dot(active[0], outer_low[...], 0, 0).astype(BF)
    store[pl.ds(step * 8, 8)] = product_.reshape(8, width // 8, width)
    slot = lax.bitwise_xor(step, place[0])
    refs = (ka, kb, sa, sb)

    def copy(part, flip_y, spot, at, sem):
        return pltpu.make_async_copy(store.at[spot], refs[part].at[flip_y * 4 + at], sems.at[sem])

    for part in range(4):
        for flip_y in range(2):
            y = xor(place[1], flip_y)
            c = xor(place[2], part // 2)
            x = xor(place[3], part % 2)
            spot = ((step * 2 + y) * 2 + c) * 2 + x
            copy(part, flip_y, spot, slot, step * 8 + part * 2 + flip_y).start()

    @pl.when(step == 3)
    def _():
        for index in range(32):
            copy(0, 0, index, 0, index).wait()


def inner_sum_kernel(
    place, low, inner_low, branch_low, mix_own, mix_other, small,
    ka, kb, sa, sb, la, lb, ta, tb, store, low_t, rows, sems,
):
    x = place[3]
    width = low.shape[1]
    copies = []

    def send(chunk):
        begin = chunk * width
        refs = (ka, kb, sa, sb)
        into = begin
        end = begin + width if chunk < inner_low.shape[0] else store.shape[2]
        if begin >= ka.shape[2]:
            refs = (la, lb, ta, tb)
            into = begin - ka.shape[2]
        for part, flip in enumerate(PAIR_FLIPS):
            for slot in range(4):
                spot = slot_place(place, flip, slot)
                copy = pltpu.make_async_copy(
                    store.at[spot, :, begin:end],
                    refs[part].at[slot, :, into : into + end - begin],
                    sems.at[chunk * 16 + part * 4 + slot],
                )
                copy.start()
                copies.append(copy)

    rows[...] = jnp.zeros(rows.shape, F32)
    for vector in range(12):
        for third in range(3):
            row = vector * 3 + third
            rows[row : row + 1, :] = small[vector : vector + 1, third * 256 : third * 256 + 256]
    store[:, :, 5 * width :] = jnp.broadcast_to(rows[...].astype(BF)[None], (16, 48, 256))
    low_t[...] = jnp.transpose(low[...])
    for side, mix in ((x, mix_own), (1 - x, mix_other)):
        product_ = dot(mix[...], branch_low[...], 0, 0).astype(BF)
        store[pl.ds(side * 8, 8), :, :width] = product_.reshape(8, width // 16, width)
    send(0)
    for index in range(inner_low.shape[0]):
        begin = (1 + index) * width
        product_ = dot(low_t[...], inner_low[index]).astype(BF)
        store[:, :, begin : begin + width] = product_.reshape(16, width // 16, width)
        send(1 + index)
    for copy in copies:
        copy.wait()


def blocks_out(place, parts, store, sems, flips, first):
    copies = []
    for part, (ref, offset) in enumerate(zip(parts, flips, strict=True)):
        for slot in range(ref.shape[0]):
            spot = slot_place(place, offset, slot)
            copies.append(
                pltpu.make_async_copy(
                    store.at[spot], ref.at[slot], sems.at[first + part * ref.shape[0] + slot]
                )
            )
    return copies


def retreat_kernel(
    place, lens, del_own, del_other, q_in, k_in, v_in, mg_own, mg_other, mix_own, mix_other,
    log_own, log_other, low, tags, dk, dv,
):
    x = place[3]
    ends = crop_ends_of(lens)
    half = del_own.shape[1]

    pair = pl.program_id(0)

    @pl.when(pair == 0)
    def _():
        for index, part in enumerate(tag_row(ends, x, del_own, del_other)):
            tall = jnp.transpose(jnp.broadcast_to(part.astype(F32), (8, half)))
            tags[index * half : (index + 1) * half, :] = tall[:, :1]

    dk[...] = jnp.zeros_like(dk)
    dv[...] = jnp.zeros_like(dv)
    block = half // 2
    lane_low = lax.broadcasted_iota(jnp.int32, (block, 128), 1) < 64
    heads = lax.div(lax.broadcasted_iota(jnp.int32, (8, 128), 1), 64)
    picks = (heads == lax.broadcasted_iota(jnp.int32, (8, 128), 0)).astype(F32)
    eighth = jnp.asarray(0.125, BF)

    def turn(index, start, wide):
        wide = wide * block
        key_low = lax.broadcasted_iota(jnp.int32, (wide, 128), 1) < 64
        begin = pl.multiple_of(index * block, block)
        spot = pl.multiple_of(lax.rem(index, 2) * block, block)
        places = begin + lax.broadcasted_iota(jnp.int32, (1, block), 1)
        key_places = start + lax.broadcasted_iota(jnp.int32, (wide, 1), 0)
        allowed = (tags[pl.ds(start, wide), :] == segment_of(ends, places).astype(F32)) | (
            key_places == places
        )
        bias = jnp.where(allowed, 0.0, -1e30)
        queries = q_in[pl.ds(begin, block), :] * eighth
        keys = k_in[pl.ds(start, wide), :]
        values = v_in[pl.ds(start, wide), :]
        near = lax.div(index, 2) == x
        rows = pl.ds(spot, block)
        grads = jnp.where(near, mg_own[rows, :], mg_other[rows, :])
        mixed = jnp.where(near, mix_own[rows, :], mix_other[rows, :])
        deltas = exact_dot(picks, grads.astype(F32) * mixed.astype(F32), 1, 1)
        q_total = jnp.zeros((block, 128), F32)
        k_total = jnp.zeros((wide, 128), F32)
        v_total = jnp.zeros((wide, 128), F32)
        for side in range(2):
            mine = lane_low if side == 0 else ~lane_low
            key_mine = key_low if side == 0 else ~key_low
            q_mine = jnp.where(mine, queries, 0)
            g_mine = jnp.where(mine, grads, 0)
            row = pl.ds(pair * 2 + side, 1)
            log = jnp.where(near, log_own[row, rows], log_other[row, rows])
            probs = jnp.exp(dot(keys, q_mine, 1, 1) + (bias - log))
            prob_grad = dot(values, g_mine, 1, 1) - deltas[side : side + 1, :]
            score_grad = (probs * prob_grad).astype(BF)
            v_total = v_total + dot(probs.astype(BF), g_mine)
            k_total = k_total + dot(score_grad, q_mine)
            q_total = q_total + dot(score_grad, jnp.where(key_mine, keys, 0), 0, 0)
        low[pl.ds(begin, block), :128] = (q_total * 0.125).astype(BF)
        dk[pl.ds(start, wide), :] += k_total
        dv[pl.ds(start, wide), :] += v_total

    for_windows(ends, block, jnp.int32(0), jnp.int32(4), turn)
    low[:, 128:256] = dk[...].astype(BF)
    low[:, 256:] = dv[...].astype(BF)


def project_sum_kernel(
    place, st_own, st_other, low, ka, kb, sa, sb, rows, store, rows_t, row_sems, sems
):
    x = place[3]
    row_copies = [
        pltpu.make_async_copy(st_own, rows.at[x], row_sems.at[0]),
        pltpu.make_async_copy(st_other, rows.at[1 - x], row_sems.at[1]),
    ]
    for copy in row_copies:
        copy.start()
    wide = low.shape[1] // 3
    lane_rows = lax.broadcasted_iota(jnp.int32, (24, 128), 0)
    extra = jnp.zeros((24, 128), F32)
    for index in range(3):
        for kind in range(2):
            begin = index * wide + kind * 256
            sums = jnp.sum(low[:, begin : begin + 128].astype(F32), axis=0, keepdims=True)
            extra = jnp.where(lane_rows == kind * 3 + index, sums, extra)
    extra = jnp.concatenate([extra, extra], axis=0).astype(BF)
    store[:, :, 3 * wide :] = jnp.broadcast_to(extra[None], (16, 48, 128))
    for copy in row_copies:
        copy.wait()
    rows_t[...] = jnp.transpose(rows[...].reshape(2 * st_own.shape[0], st_own.shape[1]))
    for index in range(3):
        columns = slice(index * wide, (index + 1) * wide)
        store[:, :, columns] = dot(rows_t[...], low[:, columns]).astype(BF).reshape(16, 48, wide)
    copies = blocks_out(place, (ka, kb, sa, sb), store, sems, PAIR_FLIPS, 0)
    for copy in copies:
        copy.start()
    for copy in copies:
        copy.wait()


def states_sum_kernel(
    place, low, residual, a0, a1, a2, a3, states_out, states_send, store, sems
):
    x = place[3]
    copies = blocks_in(place, (a0, a1, a2, a3), store, sems, PAIR_FLIPS)
    for copy in copies:
        copy.start()
    for copy in copies:
        copy.wait()
    half = residual.shape[0]
    weight = store[:, :48, :].reshape(768, low.shape[1])

    def share(side):
        begin = pl.multiple_of(side * half, half)
        return dot(low[pl.ds(begin, half), :], weight, 1, 1)

    states_send[...] = share(1 - x).astype(BF)
    states_out[...] = residual[...] + share(x)


def swap(value, axis):
    return lax.ppermute(value, axis, [(0, 1), (1, 0)])


def hop(value, planes, bits):
    return lax.ppermute(value, DP, [(i, i ^ bits) for i in range(planes)])


def add32(*terms):
    return sum((term.astype(F32) for term in terms[1:]), terms[0].astype(F32))


def add(*terms):
    return add32(*terms).astype(BF)


def here():
    dp, c, x = lax.axis_index(DP), lax.axis_index(FSDP), lax.axis_index(SEQ)
    return lax.div(dp, 2), lax.rem(dp, 2), c, x, (dp * 2 + c) * 2 + x


def call(kernel, outs, inputs, specs, scratch, name, grid=()):
    return pl.pallas_call(
        lambda *refs: kernel(here(), *refs),
        out_shape=[jax.ShapeDtypeStruct(shape, kind) for shape, kind, _ in outs],
        in_specs=[spec_of(key) for key in specs],
        out_specs=[spec_of(key) for _, _, key in outs],
        scratch_shapes=scratch,
        grid=grid,
        compiler_params=pltpu.CompilerParams(vmem_limit_bytes=60 * MIB),
        cost_estimate=pl.CostEstimate(flops=0, bytes_accessed=0, transcendentals=0),
        name=name,
    )(*inputs)


def spec_of(key):
    return pl.BlockSpec(memory_space=SPACES[key]) if isinstance(key, str) else key


SPACES = {"s": pltpu.SMEM, "v": pltpu.VMEM, "a": pl.ANY}


def after(value, *others):
    return lax.optimization_barrier((value,) + others)[0]


class Order:
    def __init__(self, last):
        self.last = last

    def take(self, *values):
        values = lax.optimization_barrier(values + (self.last,))[:-1]
        return values if len(values) > 1 else values[0]

    def step(self, value):
        self.last = value
        return value


def column(rows, wide=128):
    return pl.BlockSpec((rows, wide), lambda step: (0, step))


def halves_body(
    states, deleted, crop_lengths,
    query_weight, query_bias, key_weight, value_weight, value_bias, output_weight, output_bias,
    attn_gain, attn_shift, inner_weight, inner_bias, outer_weight, outer_bias, final_gain,
    final_shift, cotangent, pool_cotangent,
):
    planes = 8
    count, width = states.shape[1:]
    half = width // 2
    hidden = inner_weight.shape[1]
    part = query_weight.shape[0]
    long = outer_weight.shape[0]
    crops = crop_lengths.shape[1]
    tall = 3 * half
    flat = width + hidden // 2
    dma = pltpu.SemaphoreType.DMA
    dp, c, x = lax.axis_index(DP), lax.axis_index(FSDP), lax.axis_index(SEQ)
    device = (dp * 2 + c) * 2 + x
    lens = crop_lengths[0]
    own = states[0]

    vectors = [
        vector[None]
        for vector in (
            query_bias, value_bias, output_bias, attn_gain, attn_shift, outer_bias, final_gain,
            final_shift, inner_bias,
        )
    ]
    send, keep, small, p1, p2 = call(
        pack_kernel,
        [
            ((part, tall + width + hidden), BF, "v"),
            ((part, tall), BF, "v"),
            ((16, width), BF, "v"),
            ((part, width + hidden), BF, "v"),
            ((long, width), BF, "v"),
        ],
        (query_weight, key_weight, value_weight, output_weight, inner_weight, outer_weight, *vectors),
        "v" * 15,
        [],
        "pack",
    )

    def pair_up(mine, theirs):
        return jnp.where(
            x == 0,
            jnp.concatenate([mine, theirs], axis=0),
            jnp.concatenate([theirs, mine], axis=0),
        )

    def along_z(block):
        return tuple(hop(block, planes, bits) for bits in (2, 4, 6))

    order = Order(p2)
    sent_2 = along_z(p2)
    del_other, from_x, small_x = order.take(swap(deleted, SEQ), swap(send, SEQ), swap(small, SEQ))
    tail = jnp.pad(add(small, small_x), ((0, 0), (0, tall - width)))
    both_a = jnp.concatenate([pair_up(keep, from_x[:, :tall]), tail], axis=0)
    both_1 = pair_up(p1[:, :flat], from_x[:, tall : tall + flat])
    both_b = pair_up(p1[:, flat:], from_x[:, tall + flat :])
    order.step(both_a)
    sent_a = along_z(both_a)
    order.step(both_b)
    other = swap(order.take(own), SEQ)
    quad_2 = order.step(jnp.stack([p2, *order.take(*sent_2)]))
    octet = hop(quad_2, planes, 1)
    quad_a = order.step(jnp.stack([both_a, *order.take(*sent_a)]))
    quad_ay = hop(quad_a, planes, 1)
    sent_1 = along_z(order.take(both_1))
    octet = order.step(jnp.concatenate([quad_2, order.take(octet)], axis=0))
    octet_x = swap(octet, SEQ)
    quad_ay, other = order.take(quad_ay, other)
    order.step(quad_ay)
    quad_1 = order.step(jnp.stack([both_1, *order.take(*sent_1)]))
    parts_a = order.take(swap(quad_a, FSDP), swap(quad_ay, FSDP))
    parts_a = (quad_a, quad_ay) + parts_a
    order.step(parts_a[-1])
    quad_1y = hop(quad_1, planes, 1)
    sent_b = along_z(after(both_b, quad_1))

    marks = (lens, deleted, del_other)
    queries, keys, values, mix_send, log_other, small = call(
        attend_kernel,
        [((2 * count, half), BF, "v")] * 3
        + [((count, half), BF, "v"), ((8, count), F32, "v"), ((16, width), F32, "v")],
        marks + (order.take(own), other) + parts_a,
        "svvaaaaaa",
        [
            pltpu.VMEM((16, 64, tall), BF),
            pltpu.VMEM((2, count, width), BF),
            pltpu.VMEM((1, 2 * count), jnp.int32),
            dma((16,)),
            dma((2,)),
        ],
        "attend",
    )
    order.step(mix_send)
    mix_other = swap(mix_send, SEQ)
    quad_1y = order.step(order.take(quad_1y))
    quad_b = order.step(jnp.stack([both_b, *order.take(*sent_b)]))
    quad_by = hop(quad_b, planes, 1)
    mix_own, log_own = call(
        attend_own_kernel,
        [((count, half), BF, "v"), ((8, count), F32, "v")],
        marks + (order.take(queries), keys, values),
        "svvvvv",
        [pltpu.VMEM((1, 2 * count), jnp.int32)],
        "attend_own",
    )
    order.step(mix_own)
    octet_x, mix_other = order.take(octet_x, mix_other)
    order.step(octet_x)
    parts_2 = (octet, octet_x, swap(octet, FSDP), swap(octet_x, FSDP))
    parts_1 = (quad_1, quad_1y, swap(quad_1, FSDP), swap(quad_1y, FSDP))
    quad_by = order.take(quad_by)
    parts_1 += (quad_b, quad_by, swap(quad_b, FSDP), swap(quad_by, FSDP))
    four = ((hidden // width, count, width), BF, "a")
    tokens = ((count, width), BF, "v")
    (
        output, pooled, residual, mg_own, mg_send, small_grad,
        active, inner_low, low, outer_low, branch_low,
    ) = call(
        feed_kernel,
        [
            tokens,
            ((crops, width), F32, "v"),
            ((count, width), F32, "v"),
            ((count, half), BF, "v"),
            ((count, half), BF, "v"),
            ((16, width), F32, "v"),
            four, four, tokens, tokens, tokens,
        ],
        marks
        + (own, mix_own, mix_other, small, cotangent[0], pool_cotangent[0])
        + parts_1
        + parts_2,
        "svvvvvvvv" + "a" * 12,
        [
            pltpu.VMEM((16, 2 * part, width + hidden), BF),
            pltpu.VMEM((32, long, width), BF),
            pltpu.VMEM((hidden // width, count, width), F32),
            pltpu.VMEM((count, width), F32),
            pltpu.VMEM((count, 1), F32),
            pltpu.VMEM((count, width), F32),
            pltpu.VMEM((count, width), F32),
            pltpu.VMEM((hidden // width, count, width), BF),
            pltpu.VMEM((hidden // width, count, width), BF),
            dma((32,)),
            dma((32,)),
            dma((2 * hidden // width,)),
        ],
        "feed",
    )
    mg_other = swap(mg_send, SEQ)

    blocks_2 = ((8, long, width), BF, "a")
    keep_2a, keep_2b, send_2a, send_2b = call(
        outer_sum_kernel,
        [blocks_2] * 4,
        (active, outer_low),
        [pl.BlockSpec((1, count, width), lambda step: (step, 0, 0)), "v"],
        [pltpu.VMEM((32, long, width), BF), dma((32,))],
        "outer_sum",
        (hidden // width,),
    )
    order.step(send_2b)
    mg_other = order.step(order.take(mg_other))
    core_2b = swap(order.take(send_2b), FSDP)
    blocks_a = ((4, 2 * part, flat), BF, "a")
    blocks_b = ((4, 2 * part, width + hidden - flat + 256), BF, "a")
    keep_1a, keep_1b, send_1a, send_1b, keep_3a, keep_3b, send_3a, send_3b = call(
        inner_sum_kernel,
        [blocks_a] * 4 + [blocks_b] * 4,
        (order.take(low), inner_low, branch_low, mix_own, mix_other, small_grad),
        "vvvvvv",
        [
            pltpu.VMEM((16, 2 * part, width + hidden + 256), BF),
            pltpu.VMEM((width, count), BF),
            pltpu.VMEM((2 * part, 256), F32),
            dma((80,)),
        ],
        "inner_sum",
    )
    order.step(send_1b)
    t1_2 = order.step(add(keep_2b, order.take(core_2b)))
    sum_2x = swap(t1_2, SEQ)
    t1_1 = order.step(add(keep_1b, order.take(swap(send_1b, FSDP))))
    sum_1y = hop(t1_1, planes, 1)
    t1_3 = order.step(add(keep_3b, order.take(swap(send_3b, FSDP))))
    sum_3y = hop(t1_3, planes, 1)
    core_2, core_1, core_3 = (
        swap(value, FSDP) for value in order.take(send_2a, send_1a, send_3a)
    )

    def split_x(v):
        v = v.reshape((2, part) + v.shape[1:])
        return jnp.where(x == 0, v[0], v[1]), jnp.where(x == 0, v[1], v[0])

    def to_z(u):
        return tuple(hop(u[index], planes, 2 * index) for index in (1, 2, 3))

    specs = ["s", "v", "v"] + [column(2 * count)] * 3 + [column(count)] * 4 + ["v", "v"]
    (lows,) = call(
        retreat_kernel,
        [((2 * count, tall), BF, column(2 * count, 384))],
        marks
        + (order.take(queries), keys, values)
        + (mg_own, mg_other, mix_own, mix_send, log_own, log_other),
        specs,
        [
            pltpu.VMEM((2 * count, 1), F32),
            pltpu.VMEM((2 * count, 128), F32),
            pltpu.VMEM((2 * count, 128), F32),
        ],
        "retreat",
        (half // 128,),
    )
    order.step(lows)
    u_1 = add(keep_1a, *order.take(core_1, sum_1y))
    order.step(u_1)
    sum_1z = to_z(u_1)
    u_2 = order.step(add(keep_2a, *order.take(core_2, sum_2x)))
    sum_2y = hop(u_2[4:], planes, 1)
    wide = tall + 128
    keep_a, keep_b, send_a, send_b = call(
        project_sum_kernel,
        [((4, 2 * part, wide), BF, "a")] * 4,
        (order.take(own), other, lows),
        "aav",
        [
            pltpu.VMEM((2, count, width), BF),
            pltpu.VMEM((16, 2 * part, wide), BF),
            pltpu.VMEM((width, 2 * count), BF),
            dma((2,)),
            dma((16,)),
        ],
        "project_sum",
    )
    order.step(send_b)
    core_b, core_a = swap(send_b, FSDP), swap(send_a, FSDP)
    u_3 = add(keep_3a, *order.take(core_3, sum_3y))
    order.step(u_3)
    sum_3z = to_z(u_3)
    t1_a = order.step(add(keep_b, order.take(core_b)))
    sum_ay = hop(t1_a, planes, 1)
    v_1 = order.step(add(u_1[0], *order.take(*sum_1z)))
    v_2 = add(u_2[:4], order.take(sum_2y))
    order.step(v_2)
    sum_2z = to_z(v_2)
    v_3 = order.step(add(u_3[0], *order.take(*sum_3z)))
    states_part, states_send = call(
        states_sum_kernel,
        [((count, width), F32, "v"), tokens],
        (order.take(lows), residual) + parts_a,
        "vvaaaa",
        [pltpu.VMEM((16, 64, tall), BF), dma((16,))],
        "states_sum",
    )
    order.step(states_send)
    states_x = swap(states_send, SEQ)
    pooled_x = swap(pooled, SEQ)
    grad_outer_weight = order.step(add32(v_2[0], *order.take(*sum_2z)))
    u_a = add(keep_a, *order.take(core_a, sum_ay))
    order.step(u_a)
    sum_az = to_z(u_a)
    small = v_3[:, width + hidden - flat :]
    small = jnp.concatenate([small[:part], small[part:]], axis=1)
    mine_1, theirs_1 = split_x(
        jnp.concatenate([v_1, v_3[:, : width + hidden - flat]], axis=1)
    )
    sent_1x = swap(jnp.concatenate([theirs_1, small], axis=1), SEQ)
    v = order.step(add(u_a[0], *order.take(*sum_az)))
    mine_a, theirs_a = split_x(v)
    sent_ax = swap(theirs_a, SEQ)
    pooled = pooled + order.take(pooled_x)
    states_grad = order.step(add32(states_part, order.take(states_x)))
    sent_1x = order.take(sent_1x)
    total = mine_1.astype(F32) + sent_1x[:, : width + hidden].astype(F32)
    grad_output_weight, grad_inner_weight = total[:, :width], total[:, width:]
    small = small.astype(F32) + sent_1x[:, width + hidden :].astype(F32)
    small = jnp.concatenate([small[:, :256], small[:, 256:]], axis=0)
    smalls = small[:36].reshape(12, width)
    theirs = order.take(sent_ax)
    left = jnp.where(x == 0, mine_a, theirs).astype(F32)
    right = jnp.where(x == 0, theirs, mine_a).astype(F32)

    def gathered(index):
        columns = [
            side[:, (pair * 3 + index) * 128 : (pair * 3 + index + 1) * 128]
            for side in (left, right)
            for pair in range(half // 128)
        ]
        return jnp.concatenate(columns, axis=1)

    grad_query_weight, grad_key_weight, grad_value_weight = (gathered(i) for i in range(3))
    bias_grads = jnp.stack([left[:6, tall:], right[:6, tall:]]).reshape(2, 2, half)
    bias_grads = jnp.transpose(bias_grads, (1, 0, 2)).reshape(2, width)
    vectors = lax.dynamic_slice(smalls[:8], (0, device * part), (8, part))
    bias_grads = lax.dynamic_slice(bias_grads, (0, device * part), (2, part))
    grad_inner_bias = lax.dynamic_slice(
        smalls[8:12].reshape(hidden), (device * long,), (long,)
    )
    return (
        output[None],
        pooled[None],
        states_grad[None],
        grad_query_weight,
        bias_grads[0],
        grad_key_weight,
        grad_value_weight,
        bias_grads[1],
        grad_output_weight,
        vectors[2],
        vectors[3],
        vectors[4],
        grad_inner_weight,
        grad_inner_bias,
        grad_outer_weight,
        vectors[5],
        vectors[6],
        vectors[7],
    )


def solution(mesh):
    in_specs = (
        P(ROWS, SEQ, None),
        P(ROWS, SEQ),
        P(ROWS, None),
        BY_ROW,
        FLAT,
        BY_ROW,
        BY_ROW,
        FLAT,
        BY_ROW,
        FLAT,
        FLAT,
        FLAT,
        BY_ROW,
        FLAT,
        BY_ROW,
        FLAT,
        FLAT,
        FLAT,
        P(ROWS, SEQ, None),
        P(ROWS, None, None),
    )
    out_specs = (
        P(ROWS, SEQ, None),
        P(ROWS, None, None),
        P(ROWS, SEQ, None),
        BY_ROW,
        FLAT,
        BY_ROW,
        BY_ROW,
        FLAT,
        BY_ROW,
        FLAT,
        FLAT,
        FLAT,
        BY_ROW,
        FLAT,
        BY_ROW,
        FLAT,
        FLAT,
        FLAT,
    )
    shape = mesh.shape
    halves = (shape[DP], shape[FSDP], shape[SEQ]) == (8, 2, 2)
    chosen = halves_body if halves else body
    return jax.shard_map(chosen, mesh=mesh, in_specs=in_specs, out_specs=out_specs, check_vma=False)
```
